32 devices in a mesh: dp: 4 (over y, x), shard: 8 (over z, core).
Axes of the slice: x: 2, y: 2, z: 4, core: 2. Of those that a mesh axis runs over, the one named last changes fastest.
Arguments:
- frames: bfloat16 [128, 64, 1536], P(('dp', 'shard')), may hold values from -6 to 6
- cotangent: bfloat16 [128, 64, 1536], P(('dp', 'shard')), may hold values from -6 to 6
- lengths: int32 [128], P(('dp', 'shard')), may hold values from 1 to 64, 6144 in all
- send_order: int32 [128], P(('dp', 'shard')), may hold values from 0 to 3, as said below
- norm_gain: bfloat16 [1536], P('shard'), may hold values from 0.099609375 to 1.8984375
- conv_bias: bfloat16 [1536], P('shard'), may hold values from -3 to 3
- kernel: bfloat16 [1536, 31], P('shard'), may hold values from -1 to 1
- expand_weight: bfloat16 [1536, 3072], P('shard'), may hold values from -0.15625 to 0.15625
- project_weight: bfloat16 [1536, 1536], P('shard'), may hold values from -0.15625 to 0.15625
Outputs:
- encoded: bfloat16 [128, 64, 1536], P(('dp', 'shard'))
- frame_grad: bfloat16 [128, 64, 1536], P(('dp', 'shard'))
- gain_grad: float32 [1536], P('shard')
- bias_grad: float32 [1536], P('shard')
- kernel_grad: float32 [1536, 31], P('shard')
- expand_grad: float32 [1536, 3072], P('shard')
- project_grad: float32 [1536, 1536], P('shard')
The draws below stay inside these ranges and needn't reach their ends.
Inputs may be any that keep to these rules, and one draw needn't show every extreme that they name: `send_order`: each aligned block of 4 entries, the utterances of one device, is a permutation of 0 to 3. `lengths`: at least one utterance has exactly 64 live frames.
All inputs are finite; a program needn't handle non-finite values. No bound on the sum of `lengths` on one device may be relied on, other than what follows from the above.
Results may differ from the reference program's by a relative error of at most 0.03.
Values may be sent and summed in bfloat16 or wider, within the bound.
No kernel may reach another device: no remote copies, remote signals or barrier semaphores. Data moves between devices by JAX's collectives and lax.ppermute only.
A program may use at most 128 MiB of HBM per device.

```python
import math
import jax
import jax.numpy as jnp
import numpy as np
from jax import lax

D = 1536
KW = 31
L = 64
UPEER = 1
U_DEV = 4
UTT = 128
N_DP = 4
N_SHARD = 8


def draw_send_order(key, part):
    split_keys = jax.random.split(key, UTT // U_DEV)
    blocks = jax.vmap(lambda single: jax.random.permutation(single, U_DEV))(split_keys)
    return blocks.reshape(UTT).astype(jnp.int32)


def raised(entries, rng, source, target, blocks, factor):
    def block_of(axis_at):
        return (jnp.arange(entries.shape[axis_at]) // (entries.shape[axis_at] // blocks)).reshape((-1,) + (1,) * (entries.ndim - 1 - axis_at))

    first = jax.random.permutation(rng, blocks)[block_of(target)]
    other_side = (block_of(target) + blocks // 2) % blocks
    return jnp.where((block_of(source) == first) | (block_of(source) == other_side), factor * entries, entries)


def level_of(key, shape, cuts, smallest, top_value):
    factor_of, own = 1.0, jax.random.fold_in(key, 6)
    for axis_at, blocks in cuts:
        heights = jnp.exp(jax.random.uniform(jax.random.fold_in(own, axis_at), (blocks,), jnp.float32, smallest / len(cuts), top_value / len(cuts)))
        factor_of = factor_of * jnp.repeat(heights, shape[axis_at] // blocks).reshape([-1 if axis == axis_at else 1 for axis in range(len(shape))])
    return factor_of


def split_up(amount, total, limit, lean):
    weights = [(1 << 20) // math.isqrt(rank ** lean) + 1 for rank in range(2, amount + 1)]
    rest, counts = total - limit - (amount - 1), [1] * (amount - 1)
    while rest > 0:
        free = [i for i in range(amount - 1) if counts[i] < limit]
        pool, budget = sum([weights[i] for i in free]), rest
        for i in free:
            more = min(limit - counts[i], max(1, budget * weights[i] // pool), rest)
            counts[i] = counts[i] + more
            rest = rest - more
    return np.array([limit] + counts)


def ragged_sizes(key, number_of, total, limit, lean):
    if number_of == 2:
        one = jax.random.randint(key, (), max(1, total - limit), min(limit, total - 1) + 1)
        return jnp.stack([one, total - one])
    tallies = jnp.asarray(split_up(number_of, total, limit, lean), jnp.int32)
    pairs = (number_of - 1) // 2
    donor, receiver = tallies[1:1 + 2 * pairs:2], tallies[2:2 + 2 * pairs:2]
    margin = jnp.minimum(donor - 1, limit - receiver)
    moved = jax.random.randint(jax.random.fold_in(key, 1), (pairs,), 0, 1 << 20) % (margin + 1)
    tallies = tallies.at[1:1 + 2 * pairs:2].set(donor - moved).at[2:2 + 2 * pairs:2].set(receiver + moved)
    return tallies[jax.random.permutation(jax.random.fold_in(key, 2), number_of)]


def bell_draw(stream_key, dims, spread, bound, cuts=(), kind=jnp.bfloat16):
    level = level_of(stream_key, dims, cuts, -0.22, 0.18) if cuts else 1.0
    drawn = jax.random.normal(stream_key, dims, jnp.float32) * spread * level
    return jnp.minimum(jnp.maximum(drawn, -bound), bound).astype(kind)


def noise_with(stream_key, extent, scale, limit, cuts, heavy, kind=jnp.bfloat16):
    entries = scale * jax.random.normal(stream_key, extent, jnp.float32)
    if cuts:
        entries = entries * level_of(stream_key, extent, cuts, -0.22, 0.18)
    return jnp.clip(raised(entries, jax.random.fold_in(stream_key, 3), *heavy), -limit, limit).astype(kind)


def setup_inputs(seed: int = 0) -> dict:
    streams_of = jax.random.split(jax.random.key(seed), 10)
    frames = noise_with(streams_of[0], (UTT, L, D), 1.0, 6.0, ((0, 32),), (0, 2, 32, 2.75))
    cotangent = noise_with(streams_of[1], (UTT, L, D), 1.0, 6.0, ((0, 32),), (0, 2, 32, 2.75))
    lengths = ragged_sizes(streams_of[2], UTT, UTT * L * 3 // 4, L, 1).astype(jnp.int32)
    send_order = draw_send_order(jax.random.fold_in(streams_of[9], 71), 0)
    norm_gain = jnp.clip(1.0 + 0.18 * jax.random.normal(streams_of[4], (D,), jnp.float32), 0.099609375, 1.8984375).astype(jnp.bfloat16)
    conv_bias = bell_draw(streams_of[5], (D,), 0.5, 3.0, ((0, 8),))
    kernel = bell_draw(streams_of[6], (D, KW), KW ** -0.5, 1.0, ((0, 8),))
    expand_weight = bell_draw(streams_of[7], (D, 2 * D), D ** -0.5, 0.15625, ((0, 8),))
    project_weight = bell_draw(streams_of[8], (D, D), D ** -0.5, 0.15625, ((0, 8),))
    return {"frames": frames, "cotangent": cotangent, "lengths": lengths, "send_order": send_order, "norm_gain": norm_gain, "conv_bias": conv_bias, "kernel": kernel, "expand_weight": expand_weight, "project_weight": project_weight}


EPS = 1e-05

def depthwise(signal, taps_table):
    taps = taps_table.shape[1]
    half = (taps - 1) // 2
    length = signal.shape[1]
    padded = jnp.pad(signal, ((0, 0), (half, half), (0, 0)))
    result = jnp.zeros_like(signal)
    for offset in range(taps):
        result = result + padded[:, offset:offset + length, :] * taps_table[:, offset]
    return result

def kernel_terms(signal, upstream, taps):
    half = (taps - 1) // 2
    length = signal.shape[1]
    padded = jnp.pad(signal, ((0, 0), (half, half), (0, 0)))
    columns = []
    for offset in range(taps):
        columns.append(lax.optimization_barrier(jnp.sum(padded[:, offset:offset + length, :] * upstream, axis=(0, 1))))
    return jnp.stack(columns, axis=1)

def block_local(frames, cotangent, live, norm_gain, conv_bias, kernel, expand_weight, project_weight):
    count, length, width = frames.shape
    total_rows = count * length
    inputs = frames.reshape(total_rows, width).astype(jnp.float32)
    live_rows = live.reshape(total_rows, 1)
    centre = lax.optimization_barrier(jnp.mean(inputs, axis=1, keepdims=True))
    centred = inputs - centre
    variance = lax.optimization_barrier(jnp.mean(centred * centred, axis=1, keepdims=True))
    inverse = lax.rsqrt(variance + EPS)
    standard = centred * inverse
    complete_gain = norm_gain.astype(jnp.float32)
    normed = (standard * complete_gain).astype(jnp.bfloat16)
    expanded = jnp.dot(normed, expand_weight, preferred_element_type=jnp.float32)
    value_portion = expanded[:, :width]
    gate_sig = jax.nn.sigmoid(expanded[:, width:])
    glu_out = (value_portion * gate_sig * live_rows).astype(jnp.bfloat16)
    taps_full = kernel.astype(jnp.float32)
    glu_cube = glu_out.astype(jnp.float32).reshape(count, length, width)
    conv_out = depthwise(glu_cube, taps_full).reshape(total_rows, width) + conv_bias.astype(jnp.float32)
    conv_sig = jax.nn.sigmoid(conv_out)
    swished = (conv_out * conv_sig).astype(jnp.bfloat16)
    projected = jnp.dot(swished, project_weight, preferred_element_type=jnp.float32)
    encoded = (inputs + projected * live_rows).astype(jnp.bfloat16)
    upstream = cotangent.reshape(total_rows, width).astype(jnp.float32)
    masked = (upstream * live_rows).astype(jnp.bfloat16)
    project_part = jnp.dot(swished.T, masked, preferred_element_type=jnp.float32)
    grad_swish = jnp.dot(masked, project_weight.T, preferred_element_type=jnp.float32)
    grad_conv = grad_swish * conv_sig * (1.0 + conv_out * (1.0 - conv_sig))
    bias_portion = lax.optimization_barrier(jnp.sum(grad_conv, axis=0))
    gradient_volume = grad_conv.reshape(count, length, width)
    kernel_part = kernel_terms(glu_cube, gradient_volume, kernel.shape[1])
    grad_glu = depthwise(gradient_volume, taps_full[:, ::-1]).reshape(total_rows, width) * live_rows
    grad_expanded = jnp.concatenate([grad_glu * gate_sig, grad_glu * value_portion * gate_sig * (1.0 - gate_sig)], axis=1).astype(jnp.bfloat16)
    expand_part = jnp.dot(normed.T, grad_expanded, preferred_element_type=jnp.float32)
    grad_normed = jnp.dot(grad_expanded, expand_weight.T, preferred_element_type=jnp.float32)
    gain_part = lax.optimization_barrier(jnp.sum(grad_normed * standard, axis=0))
    grad_standard = grad_normed * complete_gain
    grad_inputs = inverse * (grad_standard - lax.optimization_barrier(jnp.mean(grad_standard, axis=1, keepdims=True)) - standard * lax.optimization_barrier(jnp.mean(grad_standard * standard, axis=1, keepdims=True)))
    frame_grad = (upstream + grad_inputs).astype(jnp.bfloat16)
    return (encoded.reshape(count, length, width), frame_grad.reshape(count, length, width), (gain_part, bias_portion, kernel_part, expand_part, project_part))

def reference(frames, cotangent, lengths, send_order, norm_gain, conv_bias, kernel, expand_weight, project_weight):
    balanced = jnp.arange(UTT, dtype=jnp.int32)
    device = balanced // U_DEV
    within = balanced % U_DEV
    target_dp = device // N_SHARD
    shard_pos = device % N_SHARD
    source_dp = within // UPEER
    slot_pos = within % UPEER
    source_device = source_dp * N_SHARD + shard_pos
    source = source_device * U_DEV + jnp.take(send_order, source_device * U_DEV + target_dp * UPEER + slot_pos)
    frames_bal = jnp.take(frames, source, axis=0)
    cot_bal = jnp.take(cotangent, source, axis=0)
    length_bal = jnp.take(lengths, source)
    positions = lax.broadcasted_iota(jnp.int32, (UTT, L), 1)
    live = (positions < length_bal[:, None]).astype(jnp.float32)
    devices_all = N_DP * N_SHARD
    zeros_init = (jnp.zeros((D,), jnp.float32), jnp.zeros((D,), jnp.float32), jnp.zeros((D, KW), jnp.float32), jnp.zeros((D, 2 * D), jnp.float32), jnp.zeros((D, D), jnp.float32))

    def device_step(running, pieces):
        enc_part, gradient_portion, parts = block_local(pieces[0], pieces[1], pieces[2], norm_gain, conv_bias, kernel, expand_weight, project_weight)
        rounded = lax.optimization_barrier(tuple((part.astype(jnp.bfloat16) for part in parts)))
        updated_params = tuple((total + piece.astype(jnp.float32) for total, piece in zip(running, rounded)))
        return (updated_params, (enc_part, gradient_portion))
    totals, outputs = lax.scan(device_step, zeros_init, (frames_bal.reshape(devices_all, U_DEV, L, D), cot_bal.reshape(devices_all, U_DEV, L, D), live.reshape(devices_all, U_DEV, L)))
    encoded = outputs[0].reshape(UTT, L, D)
    frame_grad = jnp.zeros((UTT, L, D), jnp.bfloat16).at[source].set(outputs[1].reshape(UTT, L, D))
    return (encoded, frame_grad, totals[0], totals[1], totals[2], totals[3], totals[4])
```

```python
import jax
import jax.numpy as jnp
from jax import lax
from jax.sharding import PartitionSpec as P

EPS = 1e-05
F32 = jnp.float32
BF16 = jnp.bfloat16


def depthwise(signal, taps_table):
    taps = taps_table.shape[0]
    half = (taps - 1) // 2
    length = signal.shape[1]
    padded = jnp.pad(signal, ((0, 0), (half, half), (0, 0)))
    result = jnp.zeros_like(signal)
    for offset in range(taps):
        result = result + padded[:, offset : offset + length, :] * taps_table[offset]
    return result


def kernel_terms(signal, upstream, taps):
    half = (taps - 1) // 2
    length = signal.shape[1]
    padded = jnp.pad(signal, ((0, 0), (half, half), (0, 0)))
    rows = []
    for offset in range(taps):
        rows.append(jnp.sum(padded[:, offset : offset + length, :] * upstream, axis=(0, 1)))
    return jnp.stack(rows, axis=0)


def chunk_compute(x, g, live, gain, taps, bias, expand_slice, project_slice):
    count, length, width = x.shape
    rows = count * length
    channels = taps.shape[1]
    inputs = x.reshape(rows, width).astype(F32)
    live_rows = live.reshape(rows, 1)
    centred = inputs - jnp.mean(inputs, axis=1, keepdims=True)
    variance = jnp.mean(centred * centred, axis=1, keepdims=True)
    standard = centred * lax.rsqrt(variance + EPS)
    normed = (standard * gain).astype(BF16)
    expanded = jnp.dot(normed, expand_slice, preferred_element_type=F32)
    value = expanded[:, :channels]
    gate = jax.nn.sigmoid(expanded[:, channels:])
    glu = (value * gate * live_rows).astype(BF16).astype(F32).reshape(count, length, channels)
    conv = depthwise(glu, taps).reshape(rows, channels) + bias
    conv_sig = jax.nn.sigmoid(conv)
    swished = (conv * conv_sig).astype(BF16)
    masked = (g.reshape(rows, width).astype(F32) * live_rows).astype(BF16)
    grad_swish = lax.dot_general(
        masked, project_slice, (((1,), (1,)), ((), ())), preferred_element_type=F32
    )
    grad_conv = grad_swish * conv_sig * (1.0 + conv * (1.0 - conv_sig))
    bias_part = jnp.sum(grad_conv, axis=0)
    volume = grad_conv.reshape(count, length, channels)
    kernel_part = kernel_terms(glu, volume, taps.shape[0])
    grad_glu = depthwise(volume, taps[::-1]).reshape(rows, channels) * live_rows
    grad_expanded = jnp.concatenate(
        [grad_glu * gate, grad_glu * value * gate * (1.0 - gate)], axis=1
    ).astype(BF16)
    grad_normed = lax.dot_general(
        grad_expanded, expand_slice, (((1,), (1,)), ((), ())), preferred_element_type=F32
    )
    gain_part = jnp.sum(grad_normed * standard, axis=0)
    return normed, masked, swished, grad_expanded, grad_normed.astype(BF16), (
        gain_part,
        bias_part,
        kernel_part,
    )


def swap(x, axis, size, k):
    return lax.ppermute(x, axis, [(p, p ^ k) for p in range(size)])


def gather_dp(x, n_dp):
    if n_dp == 4:
        half = x.shape[0] // 2
        along_x = swap(x, "dp", 4, 1)
        along_y = swap(x, "dp", 4, 2)
        far = jnp.concatenate(
            [swap(along_x[:half], "dp", 4, 2), swap(along_y[half:], "dp", 4, 1)], axis=0
        )
        return [x, along_x, along_y, far]
    return [x] + [swap(x, "dp", n_dp, k) for k in range(1, n_dp)]


def gather_shard(x, n_shard):
    if n_shard == 8:
        me = lax.axis_index("shard")
        chip, core = me // 2, me % 2
        blocks = [x] + [
            lax.ppermute(x, "shard", [(p, (p + 2 * k) % 8) for p in range(8)]) for k in (1, 2, 3)
        ]
        mine = jnp.stack(blocks)
        mine = jnp.take(mine, (chip - jnp.arange(4)) % 4, axis=0)
        other = swap(mine, "shard", 8, 1)
        pair = jnp.where(core == 0, jnp.stack([mine, other], 1), jnp.stack([other, mine], 1))
        return pair.reshape((8,) + x.shape)
    return lax.all_gather(x, "shard", axis=0)


def reduce_shard(x, n_shard):
    x = x.astype(BF16)
    if n_shard == 8:
        me = lax.axis_index("shard")
        chip, core = me // 2, me % 2
        cube = x.reshape((4, 2) + x.shape[1:])
        keep = jnp.take(cube, core, axis=1)
        give = jnp.take(cube, 1 - core, axis=1)
        both = (keep.astype(F32) + swap(give, "shard", 8, 1).astype(F32)).astype(BF16)
        total = jnp.take(both, chip, axis=0).astype(F32)
        for k in (1, 2, 3):
            piece = jnp.take(both, (chip + k) % 4, axis=0)
            total = total + lax.ppermute(
                piece, "shard", [(p, (p + 2 * k) % 8) for p in range(8)]
            ).astype(F32)
        return total
    return lax.psum_scatter(x, "shard", scatter_dimension=0, tiled=False).astype(F32)


def body(
    frames,
    cotangent,
    lengths,
    send_order,
    norm_gain,
    conv_bias,
    kernel,
    expand_weight,
    project_weight,
):
    n_dp, n_shard = lax.axis_size("dp"), lax.axis_size("shard")
    count, length, width = frames.shape
    per_peer = count // n_dp
    owned, taps = kernel.shape
    part = owned // n_dp
    channels = n_shard * part
    me = lax.axis_index("dp")

    x_own = jnp.take(frames, send_order, axis=0)
    g_own = jnp.take(cotangent, send_order, axis=0)
    len_own = jnp.take(lengths, send_order, axis=0)

    expand_cols = lax.dynamic_index_in_dim(
        expand_weight.reshape(owned, 2, n_shard, n_dp, part), me, axis=3, keepdims=False
    ).reshape(owned, 2 * channels)
    project_rows = lax.dynamic_slice_in_dim(project_weight, me * part, part, axis=0)
    small = jnp.concatenate(
        [
            lax.dynamic_slice_in_dim(kernel, me * part, part, axis=0).reshape(-1),
            lax.dynamic_slice_in_dim(conv_bias, me * part, part, axis=0),
            norm_gain,
        ]
    )
    wide = 2 * channels
    small_rows = 16
    small = jnp.pad(small, (0, small_rows * wide - small.shape[0])).reshape(small_rows, wide)
    n_halves = width // wide
    pack = jnp.concatenate(
        [expand_cols] + [project_rows[:, h * wide : (h + 1) * wide] for h in range(n_halves)] + [small], axis=0
    )
    packs = gather_shard(pack, n_shard)
    expand_slice = packs[:, :owned].reshape(width, wide)
    project_slice = jnp.concatenate(
        [
            packs[:, owned + h * part : owned + (h + 1) * part].reshape(channels, wide)
            for h in range(n_halves)
        ],
        axis=1,
    )
    small_all = packs[:, owned + n_halves * part :].reshape(n_shard, -1).astype(F32)
    taps_table = small_all[:, : part * taps].reshape(channels, taps).T
    bias = small_all[:, part * taps : part * (taps + 1)].reshape(channels)
    gain = small_all[:, part * (taps + 1) : part * (taps + 1) + owned].reshape(width)
    project_full = gather_shard(project_weight, n_shard).reshape(n_shard, n_dp, part, width)

    x_all = gather_dp(x_own, n_dp)
    g_all = gather_dp(g_own, n_dp)
    len_all = [len_own] + [swap(len_own, "dp", n_dp, k) for k in range(1, n_dp)]

    normeds, maskeds, swisheds, grad_expandeds, returned = [], [], [], [], []
    sums = None
    positions = lax.broadcasted_iota(jnp.int32, (count, length), 1)
    for k in range(n_dp):
        live = (positions < len_all[k][:, None]).astype(F32)
        normed, masked, swished, grad_expanded, grad_normed, parts = chunk_compute(
            x_all[k], g_all[k], live, gain, taps_table, bias, expand_slice, project_slice
        )
        normeds.append(normed)
        maskeds.append(masked)
        swisheds.append(swished.reshape(n_dp, per_peer, length, channels))
        grad_expandeds.append(grad_expanded)
        returned.append(grad_normed if k == 0 else swap(grad_normed, "dp", n_dp, k))
        sums = parts if sums is None else tuple(a + b for a, b in zip(sums, parts))

    stack = jnp.stack(swisheds)
    total = None
    for m in range(n_dp):
        piece = lax.dynamic_index_in_dim(stack, me ^ m, axis=1, keepdims=False)
        if m:
            piece = swap(piece, "dp", n_dp, m)
        piece = jnp.stack([piece[k ^ m] for k in range(n_dp)])
        rows = lax.dynamic_index_in_dim(project_full, me ^ m, axis=1, keepdims=False)
        term = jnp.dot(
            piece.reshape(count * length, channels),
            rows.reshape(channels, width),
            preferred_element_type=F32,
        )
        total = term if total is None else total + term
    mine = jnp.stack(
        [
            lax.dynamic_slice_in_dim(x_all[k], me * per_peer, per_peer, axis=0)
            for k in range(n_dp)
        ]
    )
    len_mine = jnp.stack(
        [
            lax.dynamic_slice_in_dim(len_all[k], me * per_peer, per_peer, axis=0)
            for k in range(n_dp)
        ]
    )
    live_mine = (positions < len_mine.reshape(count, 1)).astype(F32)
    encoded = (
        mine.reshape(count, length, width).astype(F32)
        + total.reshape(count, length, width) * live_mine[:, :, None]
    ).astype(BF16)
    encoded = jnp.take(
        encoded.reshape(n_dp, per_peer, length, width), me ^ jnp.arange(n_dp), axis=0
    ).reshape(count, length, width)

    grad_normed = sum(piece.astype(F32) for piece in returned)
    inputs = x_own.reshape(count * length, width).astype(F32)
    centred = inputs - jnp.mean(inputs, axis=1, keepdims=True)
    variance = jnp.mean(centred * centred, axis=1, keepdims=True)
    inverse = lax.rsqrt(variance + EPS)
    standard = centred * inverse
    grad_standard = grad_normed * gain
    grad_inputs = inverse * (
        grad_standard
        - jnp.mean(grad_standard, axis=1, keepdims=True)
        - standard * jnp.mean(grad_standard * standard, axis=1, keepdims=True)
    )
    frame_sorted = (g_own.reshape(count * length, width).astype(F32) + grad_inputs).astype(BF16)
    back = jnp.argmax(
        send_order[None, :] == jnp.arange(count, dtype=jnp.int32)[:, None], axis=1
    )
    frame_grad = jnp.take(frame_sorted.reshape(count, length, width), back, axis=0)

    expand_part = sum(
        lax.dot_general(a, b, (((0,), (0,)), ((), ())), preferred_element_type=F32)
        for a, b in zip(normeds, grad_expandeds)
    )
    project_part = sum(
        lax.dot_general(
            a.reshape(-1, channels), b, (((0,), (0,)), ((), ())), preferred_element_type=F32
        )
        for a, b in zip(swisheds, maskeds)
    )
    gain_part, bias_part, kernel_part = sums
    small_part = jnp.concatenate(
        [
            kernel_part.T.reshape(n_shard, part * taps),
            bias_part.reshape(n_shard, part),
            gain_part.reshape(n_shard, owned),
        ],
        axis=1,
    )
    small_part = jnp.pad(small_part, ((0, 0), (0, small_rows * wide - small_part.shape[1])))
    project_part = project_part.reshape(n_shard, part, width)
    grad_pack = jnp.concatenate(
        [expand_part.reshape(n_shard, owned, wide)]
        + [project_part[:, :, h * wide : (h + 1) * wide] for h in range(n_halves)]
        + [small_part.reshape(n_shard, small_rows, wide)],
        axis=1,
    )
    reduced = reduce_shard(grad_pack, n_shard).astype(BF16)
    gathered = jnp.stack(gather_dp(reduced, n_dp))
    gathered = jnp.take(gathered, me ^ jnp.arange(n_dp), axis=0).astype(F32)
    expand_grad = (
        gathered[:, :owned]
        .reshape(n_dp, owned, 2, n_shard, part)
        .transpose(1, 2, 3, 0, 4)
        .reshape(owned, 2 * width)
    )
    project_grad = jnp.concatenate(
        [
            gathered[:, owned + h * part : owned + (h + 1) * part].reshape(owned, wide)
            for h in range(n_halves)
        ],
        axis=1,
    )
    small_grad = gathered[:, owned + n_halves * part :].reshape(n_dp, -1)
    kernel_grad = small_grad[:, : part * taps].reshape(owned, taps)
    bias_grad = small_grad[:, part * taps : part * (taps + 1)].reshape(owned)
    gain_grad = jnp.sum(small_grad[:, part * (taps + 1) : part * (taps + 1) + owned], axis=0)
    return encoded, frame_grad, gain_grad, bias_grad, kernel_grad, expand_grad, project_grad


def solution(mesh):
    return jax.shard_map(
        body,
        mesh=mesh,
        in_specs=(
            P(("dp", "shard"), None, None),
            P(("dp", "shard"), None, None),
            P(("dp", "shard")),
            P(("dp", "shard")),
            P("shard"),
            P("shard"),
            P("shard", None),
            P("shard", None),
            P("shard", None),
        ),
        out_specs=(
            P(("dp", "shard"), None, None),
            P(("dp", "shard"), None, None),
            P("shard"),
            P("shard"),
            P("shard", None),
            P("shard", None),
            P("shard", None),
        ),
        check_vma=False,
    )
```

```python
import functools

import jax
import jax.numpy as jnp
from jax import lax
from jax.experimental import pallas as pl
from jax.experimental.pallas import tpu as pltpu
from jax.sharding import PartitionSpec as P

EPS = 1e-05
F32 = jnp.float32
BF16 = jnp.bfloat16
LANES = 128
MARGIN = 16
VMEM_BYTES = 56 * 1024 * 1024
NT = (((1,), (1,)), ((), ()))
TN = (((0,), (0,)), ((), ()))


def chunk_kernel(dims, meta, x_ref, g_ref, gain_ref, taps_ref, *refs):
    count, length, owned, part, taps, n_blocks = dims
    blocks = refs[:n_blocks]
    normed_ref, sw_ref, ge_ref, gn_ref, small_ref, gain_part_ref = refs[n_blocks : n_blocks + 6]
    we, wp, ab, standard, pad, gpad, slope, sems = refs[n_blocks + 6 :]
    rows, width = x_ref.shape
    wide = we.shape[1]
    channels = wide // 2
    tiles = channels // LANES

    def copies(b):
        owner = meta[b]
        out = [
            pltpu.make_async_copy(
                blocks[b].at[pl.ds(0, owned)],
                we.at[pl.ds(pl.multiple_of(owner * owned, owned), owned)],
                sems.at[b, 0],
            )
        ]
        for h in range(width // wide):
            out.append(
                pltpu.make_async_copy(
                    blocks[b].at[pl.ds(owned + h * part, part)],
                    wp.at[
                        pl.ds(pl.multiple_of(owner * part, part), part),
                        pl.ds(h * wide, wide),
                    ],
                    sems.at[b, 1 + h],
                )
            )
        return out

    for b in range(n_blocks):
        @pl.when(meta[b] >= 0)
        def _():
            for copy in copies(b):
                copy.start()

    step = 32
    gain = gain_ref[...]

    @pl.loop(0, rows // step)
    def _(index):
        at = pl.ds(pl.multiple_of(index * step, step), step)
        x = x_ref[at, :].astype(F32)
        centred = x - jnp.mean(x, axis=1, keepdims=True)
        variance = jnp.mean(centred * centred, axis=1, keepdims=True)
        unit = centred * lax.rsqrt(variance + EPS)
        standard[at, :] = unit
        normed_ref[at, :] = (unit * gain).astype(BF16)

    zeros = jnp.zeros((MARGIN, LANES), F32)
    for u in range(count):
        for tile in range(tiles):
            for ref in (pad, gpad):
                ref[u, tile, :MARGIN, :] = zeros
                ref[u, tile, MARGIN + length :, :] = zeros
    small_ref[...] = jnp.zeros_like(small_ref)

    for b in range(n_blocks):
        @pl.when(meta[b] >= 0)
        def _():
            for copy in copies(b):
                copy.wait()

    expanded = jnp.dot(normed_ref[...], we[...], preferred_element_type=F32)
    for tile in range(2 * tiles):
        ab[tile] = expanded[:, tile * LANES : (tile + 1) * LANES]

    first = (taps - 1) // 2
    positions = lax.broadcasted_iota(jnp.int32, (length, LANES), 0)

    @pl.loop(0, count)
    def _(u):
        at = pl.ds(pl.multiple_of(u * length, length), length)
        live = positions < meta[n_blocks + u]
        for tile in range(tiles):
            lanes = pl.ds(tile * LANES, LANES)
            gate = jax.nn.sigmoid(ab[tiles + tile, at, :])
            glu = jnp.where(live, ab[tile, at, :] * gate, 0.0).astype(BF16).astype(F32)
            pad[u, tile, MARGIN : MARGIN + length, :] = glu
            ab[tiles + tile, at, :] = gate
            conv = jnp.broadcast_to(taps_ref[taps : taps + 1, lanes], (length, LANES))
            for t in range(taps):
                conv += taps_ref[t : t + 1, lanes] * pad[u, tile, pl.ds(MARGIN - first + t, length), :]
            sig = jax.nn.sigmoid(conv)
            sw_ref[at, lanes] = jnp.where(live, conv * sig, 0.0).astype(BF16)
            slope[u, tile] = jnp.where(live, sig * (1.0 + conv * (1.0 - sig)), 0.0)

    grad_swish = lax.dot_general(g_ref[...], wp[...], NT, preferred_element_type=F32)
    for u in range(count):
        for tile in range(tiles):
            gpad[u, tile, MARGIN : MARGIN + length, :] = (
                grad_swish[u * length : (u + 1) * length, tile * LANES : (tile + 1) * LANES]
                * slope[u, tile]
            )

    def fold(value):
        return jnp.sum(value.reshape(length // 8, 8, LANES), axis=0)

    @pl.loop(0, count)
    def _(u):
        at = pl.ds(pl.multiple_of(u * length, length), length)
        live = positions < meta[n_blocks + u]
        for tile in range(tiles):
            lanes = pl.ds(tile * LANES, LANES)
            grad_conv = gpad[u, tile, MARGIN : MARGIN + length, :]
            grad_glu = jnp.zeros((length, LANES), F32)
            for t in range(taps):
                small_ref[tile, t] += fold(
                    pad[u, tile, pl.ds(MARGIN - first + t, length), :] * grad_conv
                )
                grad_glu += (
                    taps_ref[t : t + 1, lanes] * gpad[u, tile, pl.ds(MARGIN + first - t, length), :]
                )
            small_ref[tile, taps] += fold(grad_conv)
            grad_glu = jnp.where(live, grad_glu, 0.0)
            gate = ab[tiles + tile, at, :]
            through = grad_glu * gate
            ge_ref[at, lanes] = through.astype(BF16)
            ge_ref[at, pl.ds(channels + tile * LANES, LANES)] = (
                through * ab[tile, at, :] * (1.0 - gate)
            ).astype(BF16)

    span = 512
    for start in range(0, width, span):
        cols = slice(start, start + span)
        grad_normed = lax.dot_general(ge_ref[...], we[cols, :], NT, preferred_element_type=F32)
        gn_ref[:, cols] = grad_normed.astype(BF16)
        gain_part_ref[:, cols] = jnp.sum(
            (grad_normed * standard[:, cols]).reshape(rows // 8, 8, span), axis=0
        )


def chunk_call(x, g, gain, taps_table, blocks, owners, lengths, owned, part, taps):
    count, length, width = x.shape
    rows = count * length
    wide = blocks[0].shape[1]
    channels = wide // 2
    tiles = channels // LANES
    n_blocks = len(blocks)
    meta = jnp.concatenate([owners, lengths]).astype(jnp.int32)
    vmem = pl.BlockSpec(memory_space=pltpu.VMEM)
    anywhere = pl.BlockSpec(memory_space=pl.ANY)
    flops = 2 * rows * width * wide * 3
    return pl.pallas_call(
        functools.partial(chunk_kernel, (count, length, owned, part, taps, n_blocks)),
        out_shape=(
            jax.ShapeDtypeStruct((rows, width), BF16),
            jax.ShapeDtypeStruct((rows, channels), BF16),
            jax.ShapeDtypeStruct((rows, wide), BF16),
            jax.ShapeDtypeStruct((rows, width), BF16),
            jax.ShapeDtypeStruct((tiles, taps + 1, 8, LANES), F32),
            jax.ShapeDtypeStruct((8, width), F32),
        ),
        in_specs=[pl.BlockSpec(memory_space=pltpu.SMEM)] + [vmem] * 4 + [anywhere] * n_blocks,
        out_specs=(vmem,) * 6,
        scratch_shapes=[
            pltpu.VMEM((width, wide), BF16),
            pltpu.VMEM((channels, width), BF16),
            pltpu.VMEM((2 * tiles, rows, LANES), F32),
            pltpu.VMEM((rows, width), F32),
            pltpu.VMEM((count, tiles, length + 2 * MARGIN, LANES), F32),
            pltpu.VMEM((count, tiles, length + 2 * MARGIN, LANES), F32),
            pltpu.VMEM((count, tiles, length, LANES), F32),
            pltpu.SemaphoreType.DMA((n_blocks, 1 + width // wide)),
        ],
        compiler_params=pltpu.CompilerParams(vmem_limit_bytes=VMEM_BYTES),
        cost_estimate=pl.CostEstimate(
            flops=flops, bytes_accessed=6 * rows * width * 2, transcendentals=rows * wide
        ),
        name="chunk",
    )(meta, x.reshape(rows, width), g.reshape(rows, width), gain, taps_table, *blocks)


def vmem_params():
    return pltpu.CompilerParams(vmem_limit_bytes=VMEM_BYTES)


def in_vmem():
    return pl.BlockSpec(memory_space=pltpu.VMEM)


def in_smem():
    return pl.BlockSpec(memory_space=pltpu.SMEM)


def owned_column(channel, index, owned, part):
    return (channel // part) * owned + index * part + channel % part


def pack_kernel(meta, expand_ref, project_ref, pack_ref):
    owned, width = project_ref.shape
    wide = pack_ref.shape[1]
    channels = wide // 2
    part = owned * channels // width
    index = meta[0]
    row = lax.broadcasted_iota(jnp.int32, (width, channels), 0)
    col = lax.broadcasted_iota(jnp.int32, (width, channels), 1)
    pick = (row == owned_column(col, index, owned, part)).astype(F32).astype(BF16)
    for h in range(2):
        pack_ref[:owned, h * channels : (h + 1) * channels] = jnp.dot(
            expand_ref[:, h * width : (h + 1) * width], pick, preferred_element_type=F32
        ).astype(BF16)
    rows = project_ref[pl.ds(pl.multiple_of(index * part, part), part), :]
    for h in range(width // wide):
        pack_ref[owned + h * part : owned + (h + 1) * part, :] = rows[:, h * wide : (h + 1) * wide]


def pack_call(index, expand_weight, project_weight, part, wide):
    owned, width = project_weight.shape
    return pl.pallas_call(
        pack_kernel,
        out_shape=jax.ShapeDtypeStruct((owned + width // wide * part, wide), BF16),
        in_specs=[in_smem(), in_vmem(), in_vmem()],
        out_specs=in_vmem(),
        compiler_params=vmem_params(),
        cost_estimate=pl.CostEstimate(
            flops=2 * owned * width * wide, bytes_accessed=8 * owned * width, transcendentals=0
        ),
        name="pack",
    )(index.reshape(1), expand_weight, project_weight)


def grads_kernel(dims, meta, *refs):
    n, chips, owned, part, taps = dims
    normed, ge, sw, g, small, gain = [refs[i * n : (i + 1) * n] for i in range(6)]
    keep, give = refs[6 * n :]
    core = meta[0]
    wide = ge[0].shape[1]
    width = normed[0].shape[1]
    channels = wide // 2
    tiles = channels // LANES

    def emit(chip, which, rows, cols, value):
        @pl.when(core == which)
        def _():
            keep[chip, rows, cols] = value

        @pl.when(core != which)
        def _():
            give[chip, rows, cols] = value

    def total(left, right):
        out = None
        for a, b in zip(left, right):
            term = lax.dot_general(a, b[...], TN, preferred_element_type=F32)
            out = term if out is None else out + term
        return out

    every = slice(None)
    for chip in range(chips):
        cols = slice(2 * chip * owned, 2 * (chip + 1) * owned)
        block = total([a[:, cols] for a in normed], ge).astype(BF16)
        for which in range(2):
            emit(chip, which, slice(0, owned), every, block[which * owned : (which + 1) * owned])
    block = total([a[...] for a in sw], g).astype(BF16)
    sums = sum(a[...] for a in small)
    sums = jnp.sum(sums, axis=2)
    sums = jnp.concatenate([sums[tile] for tile in range(tiles)], axis=1)
    gains = jnp.sum(sum(a[...] for a in gain), axis=0, keepdims=True)
    base = owned + width // wide * part
    for chip in range(chips):
        for which in range(2):
            owner = 2 * chip + which
            rows = block[owner * part : (owner + 1) * part]
            for h in range(width // wide):
                emit(
                    chip,
                    which,
                    slice(owned + h * part, owned + (h + 1) * part),
                    every,
                    rows[:, h * wide : (h + 1) * wide],
                )
            mine = sums[:, owner * part : (owner + 1) * part]
            pad = jnp.zeros((16, LANES - part), F32)
            own_gain = gains[:, owner * owned : (owner + 1) * owned]
            line = jnp.concatenate(
                [mine[:16], pad, mine[16:], pad, jnp.broadcast_to(own_gain, (16, owned))], axis=1
            )
            line = jnp.concatenate(
                [line, jnp.zeros((16, wide - line.shape[1]), F32)], axis=1
            ).astype(BF16)
            emit(chip, which, slice(base, base + 16), every, line)


def grads_call(core, normed, ge, sw, g, small, gain, owned, part, taps):
    n = len(normed)
    rows, width = normed[0].shape
    wide = ge[0].shape[1]
    chips = width // owned // 2
    height = owned + width // wide * part + 16
    shape = jax.ShapeDtypeStruct((chips, height, wide), BF16)
    return pl.pallas_call(
        functools.partial(grads_kernel, (n, chips, owned, part, taps)),
        out_shape=(shape, shape),
        in_specs=[in_smem()] + [in_vmem()] * (6 * n),
        out_specs=(in_vmem(), in_vmem()),
        compiler_params=vmem_params(),
        cost_estimate=pl.CostEstimate(
            flops=3 * n * rows * width * wide,
            bytes_accessed=n * rows * width * 8,
            transcendentals=0,
        ),
        name="weight_grads",
    )(core.reshape(1), *normed, *ge, *sw, *g, *small, *gain)


def route_kernel(n, meta, *refs):
    me = meta[0]
    for m in range(n):
        for k in range(n):
            chosen = meta[1 + k * n + (me ^ m)]
            refs[n + m][k] = refs[k][chosen]


def route_call(meta, swished, length):
    n = len(swished)
    channels = swished[0].shape[1]
    shape = jax.ShapeDtypeStruct((n, length, channels), BF16)
    return pl.pallas_call(
        functools.partial(route_kernel, n),
        out_shape=(shape,) * n,
        in_specs=[in_smem()] + [in_vmem()] * n,
        out_specs=(in_vmem(),) * n,
        compiler_params=vmem_params(),
        cost_estimate=pl.CostEstimate(
            flops=0, bytes_accessed=4 * n * n * length * channels, transcendentals=0
        ),
        name="route",
    )(meta, *[a.reshape(n, length, channels) for a in swished])


def encode_kernel(dims, meta, *refs):
    n, n_blocks, length, owned, part = dims
    pieces = refs[:n]
    frames = refs[n : 2 * n]
    blocks = refs[2 * n : 2 * n + n_blocks]
    out_ref = refs[2 * n + n_blocks]
    cat, weight, residual, frame_sems, sems = refs[2 * n + n_blocks + 1 :]
    channels = pieces[0].shape[2]
    me = meta[0]
    first = 1 + n * n

    def weight_copies(b):
        owner = meta[first + b]
        return [
            pltpu.make_async_copy(
                blocks[b].at[pl.ds(i * part, part)],
                weight.at[pl.ds(pl.multiple_of(i * channels + owner * part, part), part)],
                sems.at[b, i],
            )
            for i in range(n)
        ]

    frame_copies = [
        pltpu.make_async_copy(
            frames[k].at[meta[1 + k * n + me]], residual.at[me ^ k], frame_sems.at[k]
        )
        for k in range(n)
    ]
    for copy in frame_copies:
        copy.start()
    for b in range(n_blocks):
        @pl.when(meta[first + b] >= 0)
        def _():
            for copy in weight_copies(b):
                copy.start()

    for m in range(n):
        lanes = pl.ds(pl.multiple_of((me ^ m) * channels, channels), channels)
        for k in range(n):
            rows = pl.ds(pl.multiple_of((me ^ m ^ k) * length, length), length)
            cat[rows, lanes] = pieces[m][k]
    for copy in frame_copies:
        copy.wait()
    for b in range(n_blocks):
        @pl.when(meta[first + b] >= 0)
        def _():
            for copy in weight_copies(b):
                copy.wait()

    for r in range(n):
        term = jnp.dot(
            cat[r * length : (r + 1) * length, :], weight[...], preferred_element_type=F32
        )
        out_ref[r] = (residual[r].astype(F32) + term).astype(BF16)


def encode_call(me, orders, pieces, frames, blocks, owners, owned, part):
    n, length, channels = pieces[0].shape
    width = blocks[0].shape[1]
    n_blocks = len(blocks)
    meta = jnp.concatenate([me.reshape(1), orders, owners])
    anywhere = pl.BlockSpec(memory_space=pl.ANY)
    return pl.pallas_call(
        functools.partial(encode_kernel, (n, n_blocks, length, owned, part)),
        out_shape=jax.ShapeDtypeStruct((n, length, width), BF16),
        in_specs=[in_smem()] + [in_vmem()] * n + [anywhere] * (n + n_blocks),
        out_specs=in_vmem(),
        scratch_shapes=[
            pltpu.VMEM((n * length, width), BF16),
            pltpu.VMEM((width, width), BF16),
            pltpu.VMEM((n, length, width), BF16),
            pltpu.SemaphoreType.DMA((n,)),
            pltpu.SemaphoreType.DMA((n_blocks, n)),
        ],
        compiler_params=vmem_params(),
        cost_estimate=pl.CostEstimate(
            flops=2 * n * length * width * width, bytes_accessed=4 * width * width, transcendentals=0
        ),
        name="encode",
    )(meta, *pieces, *frames, *blocks)


def frame_grad_kernel(n, x_ref, g_ref, gain_ref, *refs):
    out_ref = refs[n]
    x = x_ref[...].astype(F32)
    centred = x - jnp.mean(x, axis=1, keepdims=True)
    inverse = lax.rsqrt(jnp.mean(centred * centred, axis=1, keepdims=True) + EPS)
    standard = centred * inverse
    grad = sum(ref[...].astype(F32) for ref in refs[:n]) * gain_ref[...]
    grad_in = inverse * (
        grad
        - jnp.mean(grad, axis=1, keepdims=True)
        - standard * jnp.mean(grad * standard, axis=1, keepdims=True)
    )
    out_ref[...] = (g_ref[...].astype(F32) + grad_in).astype(BF16)


def frame_grad_call(x, g, gain, returned):
    count, length, width = x.shape
    rows = count * length
    step = 64
    block = pl.BlockSpec((step, width), lambda s: (s, 0))
    out = pl.pallas_call(
        functools.partial(frame_grad_kernel, len(returned)),
        out_shape=jax.ShapeDtypeStruct((rows, width), BF16),
        grid=(rows // step,),
        in_specs=[block, block, pl.BlockSpec((1, width), lambda s: (0, 0))]
        + [block] * len(returned),
        out_specs=block,
        compiler_params=vmem_params(),
        cost_estimate=pl.CostEstimate(
            flops=20 * rows * width, bytes_accessed=14 * rows * width, transcendentals=rows
        ),
        name="frame_grad",
    )(x.reshape(rows, width), g.reshape(rows, width), gain, *returned)
    return out.reshape(count, length, width)


def unpack_kernel(dims, meta, *refs):
    n, owned, part = dims
    blocks = refs[:n]
    expand_ref, project_ref, cat = refs[n:]
    wide = blocks[0].shape[1]
    channels = wide // 2
    width = project_ref.shape[1]
    me = meta[0]
    row = lax.broadcasted_iota(jnp.int32, (width, width), 0)
    col = lax.broadcasted_iota(jnp.int32, (width, width), 1)
    place = owned_column(row % channels, row // channels, owned, part)
    spread = (place == col).astype(F32).astype(BF16)
    for k in range(n):
        index = me ^ k
        lanes = pl.ds(pl.multiple_of(index * channels, channels), channels)
        for h in range(2):
            cat[h, :, lanes] = blocks[k][:owned, h * channels : (h + 1) * channels]
        rows = pl.ds(pl.multiple_of(index * part, part), part)
        for h in range(width // wide):
            project_ref[rows, h * wide : (h + 1) * wide] = blocks[k][
                owned + h * part : owned + (h + 1) * part, :
            ].astype(F32)
    for h in range(2):
        expand_ref[:, h * width : (h + 1) * width] = jnp.dot(
            cat[h], spread, preferred_element_type=F32
        )


def unpack_call(me, blocks, owned, part, width):
    return pl.pallas_call(
        functools.partial(unpack_kernel, (len(blocks), owned, part)),
        out_shape=(
            jax.ShapeDtypeStruct((owned, 2 * width), F32),
            jax.ShapeDtypeStruct((owned, width), F32),
        ),
        in_specs=[in_smem()] + [in_vmem()] * len(blocks),
        out_specs=(in_vmem(), in_vmem()),
        scratch_shapes=[pltpu.VMEM((2, owned, width), BF16)],
        compiler_params=vmem_params(),
        cost_estimate=pl.CostEstimate(
            flops=4 * owned * width * width, bytes_accessed=18 * owned * width, transcendentals=0
        ),
        name="unpack",
    )(me.reshape(1), *blocks)


def along_z(x, pairs):
    return lax.ppermute(x, "shard", [(2 * a + c, 2 * b + c) for a, b in pairs for c in range(2)])


RIGHT = [(0, 1), (1, 2), (2, 3)]
LEFT = [(3, 2), (2, 1), (1, 0)]


def gather_line(x, chip, core):
    right = along_z(x, RIGHT)
    left = along_z(x, LEFT)
    right2 = along_z(right, [(1, 2), (2, 3)])
    left2 = along_z(left, [(2, 1), (1, 0)])
    second = jnp.where(chip >= 2, right2, left2)
    third = along_z(second, [(1, 0), (2, 3)])
    blocks = [x, right, left, second, third]
    chips = [
        chip,
        jnp.where(chip >= 1, chip - 1, -1),
        jnp.where(chip <= 2, chip + 1, -1),
        jnp.where(chip >= 2, chip - 2, chip + 2),
        jnp.where(chip == 0, 3, jnp.where(chip == 3, 0, -1)),
    ]
    others = [swap(block, "shard", 8, 1) for block in blocks]
    owners = [jnp.where(c >= 0, 2 * c + core, -1) for c in chips]
    owners += [jnp.where(c >= 0, 2 * c + 1 - core, -1) for c in chips]
    return blocks + others, jnp.stack(owners).astype(jnp.int32)


def reduce_line(keep, give, chip):
    got = swap(give, "shard", 8, 1)

    def block(at):
        return lax.dynamic_index_in_dim(keep, at, 0, False).astype(
            F32
        ) + lax.dynamic_index_in_dim(got, at, 0, False).astype(F32)

    def send(at, carried, pairs):
        value = block(at)
        if carried is not None:
            value = value + carried.astype(F32)
        return along_z(value.astype(BF16), pairs)

    far = send(jnp.where(chip <= 1, 3, 0), None, [(0, 1), (3, 2)])
    right = send(jnp.minimum(chip + 2, 3), far, [(0, 1), (1, 2)])
    left = send(jnp.maximum(chip - 2, 0), far, [(3, 2), (2, 1)])
    right = send(jnp.minimum(chip + 1, 3), right, RIGHT)
    left = send(jnp.maximum(chip - 1, 0), left, LEFT)
    return (block(chip) + right.astype(F32) + left.astype(F32)).astype(BF16)


def fast_body(
    frames,
    cotangent,
    lengths,
    send_order,
    norm_gain,
    conv_bias,
    kernel,
    expand_weight,
    project_weight,
):
    n_dp, n_shard = lax.axis_size("dp"), lax.axis_size("shard")
    count, length, width = frames.shape
    owned, taps = kernel.shape
    part = owned // n_dp
    channels = n_shard * part
    wide = 2 * channels
    me = lax.axis_index("dp").astype(jnp.int32)
    shard = lax.axis_index("shard").astype(jnp.int32)
    chip, core = shard // 2, shard % 2

    x_all = gather_dp(frames, n_dp)
    g_all = gather_dp(cotangent, n_dp)
    small_ints = jnp.concatenate([lengths, send_order])
    ints = [small_ints] + [swap(small_ints, "dp", n_dp, k) for k in range(1, n_dp)]
    orders = jnp.concatenate([a[count:] for a in ints])

    small = jnp.concatenate(
        [
            lax.dynamic_slice_in_dim(kernel, me * part, part, axis=0).T,
            lax.dynamic_slice_in_dim(conv_bias, me * part, part, axis=0)[None],
            norm_gain.reshape(n_dp, part),
        ],
        axis=0,
    )
    small_all = gather_shard(small, n_shard)
    taps_table = (
        small_all[:, : taps + 1].transpose(1, 0, 2).reshape(taps + 1, channels).astype(F32)
    )
    gain = small_all[:, taps + 1 :].reshape(1, width).astype(F32)

    pack = pack_call(me, expand_weight, project_weight, part, wide)
    packs, owners = gather_line(pack, chip, core)
    project_blocks, _ = gather_line(project_weight, chip, core)

    normed, swished, ge, returned, small_parts, gain_parts = [], [], [], [], [], []
    for k in range(n_dp):
        out = chunk_call(
            x_all[k], g_all[k], gain, taps_table, packs, owners, ints[k][:count], owned, part, taps
        )
        normed.append(out[0])
        swished.append(out[1])
        ge.append(out[2])
        returned.append(out[3] if k == 0 else swap(out[3], "dp", n_dp, k))
        small_parts.append(out[4])
        gain_parts.append(out[5])

    keep, give = grads_call(
        core,
        normed,
        ge,
        swished,
        [a.reshape(count * length, width) for a in g_all],
        small_parts,
        gain_parts,
        owned,
        part,
        taps,
    )
    reduced = reduce_line(keep, give, chip)

    pieces = route_call(jnp.concatenate([me.reshape(1), orders]), swished, length)
    pieces = [pieces[0]] + [swap(pieces[m], "dp", n_dp, m) for m in range(1, n_dp)]
    encoded = encode_call(me, orders, pieces, x_all, project_blocks, owners, owned, part)

    frame_grad = frame_grad_call(frames, cotangent, gain, returned)

    gathered = gather_dp(reduced, n_dp)
    expand_grad, project_grad = unpack_call(me, gathered, owned, part, width)
    base = owned + width // wide * part
    tails = jnp.stack([a[base:] for a in gathered])
    tails = jnp.take(tails, me ^ jnp.arange(n_dp), axis=0).astype(F32)
    table = jnp.concatenate([tails[:, :, :part], tails[:, :, LANES : LANES + part]], axis=1)
    table = table.transpose(0, 2, 1).reshape(owned, taps + 1)
    gain_grad = jnp.sum(tails[:, 0, 2 * LANES : 2 * LANES + owned], axis=0)
    return (
        encoded,
        frame_grad,
        gain_grad,
        table[:, taps],
        table[:, :taps],
        expand_grad,
        project_grad,
    )


def depthwise(signal, taps_table):
    taps = taps_table.shape[0]
    half = (taps - 1) // 2
    length = signal.shape[1]
    padded = jnp.pad(signal, ((0, 0), (half, half), (0, 0)))
    result = jnp.zeros_like(signal)
    for offset in range(taps):
        result = result + padded[:, offset : offset + length, :] * taps_table[offset]
    return result


def kernel_terms(signal, upstream, taps):
    half = (taps - 1) // 2
    length = signal.shape[1]
    padded = jnp.pad(signal, ((0, 0), (half, half), (0, 0)))
    rows = []
    for offset in range(taps):
        rows.append(jnp.sum(padded[:, offset : offset + length, :] * upstream, axis=(0, 1)))
    return jnp.stack(rows, axis=0)


def chunk_compute(x, g, live, gain, taps, bias, expand_slice, project_slice):
    count, length, width = x.shape
    rows = count * length
    channels = taps.shape[1]
    inputs = x.reshape(rows, width).astype(F32)
    live_rows = live.reshape(rows, 1)
    centred = inputs - jnp.mean(inputs, axis=1, keepdims=True)
    variance = jnp.mean(centred * centred, axis=1, keepdims=True)
    standard = centred * lax.rsqrt(variance + EPS)
    normed = (standard * gain).astype(BF16)
    expanded = jnp.dot(normed, expand_slice, preferred_element_type=F32)
    value = expanded[:, :channels]
    gate = jax.nn.sigmoid(expanded[:, channels:])
    glu = (value * gate * live_rows).astype(BF16).astype(F32).reshape(count, length, channels)
    conv = depthwise(glu, taps).reshape(rows, channels) + bias
    conv_sig = jax.nn.sigmoid(conv)
    swished = (conv * conv_sig).astype(BF16)
    masked = (g.reshape(rows, width).astype(F32) * live_rows).astype(BF16)
    grad_swish = lax.dot_general(
        masked, project_slice, (((1,), (1,)), ((), ())), preferred_element_type=F32
    )
    grad_conv = grad_swish * conv_sig * (1.0 + conv * (1.0 - conv_sig))
    bias_part = jnp.sum(grad_conv, axis=0)
    volume = grad_conv.reshape(count, length, channels)
    kernel_part = kernel_terms(glu, volume, taps.shape[0])
    grad_glu = depthwise(volume, taps[::-1]).reshape(rows, channels) * live_rows
    grad_expanded = jnp.concatenate(
        [grad_glu * gate, grad_glu * value * gate * (1.0 - gate)], axis=1
    ).astype(BF16)
    grad_normed = lax.dot_general(
        grad_expanded, expand_slice, (((1,), (1,)), ((), ())), preferred_element_type=F32
    )
    gain_part = jnp.sum(grad_normed * standard, axis=0)
    return normed, masked, swished, grad_expanded, grad_normed.astype(BF16), (
        gain_part,
        bias_part,
        kernel_part,
    )


def swap(x, axis, size, k):
    return lax.ppermute(x, axis, [(p, p ^ k) for p in range(size)])


def gather_dp(x, n_dp):
    if n_dp == 4:
        half = x.shape[0] // 2
        along_x = swap(x, "dp", 4, 1)
        along_y = swap(x, "dp", 4, 2)
        far = jnp.concatenate(
            [swap(along_x[:half], "dp", 4, 2), swap(along_y[half:], "dp", 4, 1)], axis=0
        )
        return [x, along_x, along_y, far]
    return [x] + [swap(x, "dp", n_dp, k) for k in range(1, n_dp)]


def gather_shard(x, n_shard):
    if n_shard == 8:
        me = lax.axis_index("shard")
        chip, core = me // 2, me % 2
        blocks = [x] + [
            lax.ppermute(x, "shard", [(p, (p + 2 * k) % 8) for p in range(8)]) for k in (1, 2, 3)
        ]
        mine = jnp.stack(blocks)
        mine = jnp.take(mine, (chip - jnp.arange(4)) % 4, axis=0)
        other = swap(mine, "shard", 8, 1)
        pair = jnp.where(core == 0, jnp.stack([mine, other], 1), jnp.stack([other, mine], 1))
        return pair.reshape((8,) + x.shape)
    return lax.all_gather(x, "shard", axis=0)


def reduce_shard(x, n_shard):
    x = x.astype(BF16)
    if n_shard == 8:
        me = lax.axis_index("shard")
        chip, core = me // 2, me % 2
        cube = x.reshape((4, 2) + x.shape[1:])
        keep = jnp.take(cube, core, axis=1)
        give = jnp.take(cube, 1 - core, axis=1)
        both = (keep.astype(F32) + swap(give, "shard", 8, 1).astype(F32)).astype(BF16)
        total = jnp.take(both, chip, axis=0).astype(F32)
        for k in (1, 2, 3):
            piece = jnp.take(both, (chip + k) % 4, axis=0)
            total = total + lax.ppermute(
                piece, "shard", [(p, (p + 2 * k) % 8) for p in range(8)]
            ).astype(F32)
        return total
    return lax.psum_scatter(x, "shard", scatter_dimension=0, tiled=False).astype(F32)


def generic_body(
    frames,
    cotangent,
    lengths,
    send_order,
    norm_gain,
    conv_bias,
    kernel,
    expand_weight,
    project_weight,
):
    n_dp, n_shard = lax.axis_size("dp"), lax.axis_size("shard")
    count, length, width = frames.shape
    per_peer = count // n_dp
    owned, taps = kernel.shape
    part = owned // n_dp
    channels = n_shard * part
    me = lax.axis_index("dp")

    x_own = jnp.take(frames, send_order, axis=0)
    g_own = jnp.take(cotangent, send_order, axis=0)
    len_own = jnp.take(lengths, send_order, axis=0)

    expand_cols = lax.dynamic_index_in_dim(
        expand_weight.reshape(owned, 2, n_shard, n_dp, part), me, axis=3, keepdims=False
    ).reshape(owned, 2 * channels)
    project_rows = lax.dynamic_slice_in_dim(project_weight, me * part, part, axis=0)
    small = jnp.concatenate(
        [
            lax.dynamic_slice_in_dim(kernel, me * part, part, axis=0).reshape(-1),
            lax.dynamic_slice_in_dim(conv_bias, me * part, part, axis=0),
            norm_gain,
        ]
    )
    wide = 2 * channels
    small_rows = 16
    small = jnp.pad(small, (0, small_rows * wide - small.shape[0])).reshape(small_rows, wide)
    n_halves = width // wide
    pack = jnp.concatenate(
        [expand_cols] + [project_rows[:, h * wide : (h + 1) * wide] for h in range(n_halves)] + [small], axis=0
    )
    packs = gather_shard(pack, n_shard)
    expand_slice = packs[:, :owned].reshape(width, wide)
    project_slice = jnp.concatenate(
        [
            packs[:, owned + h * part : owned + (h + 1) * part].reshape(channels, wide)
            for h in range(n_halves)
        ],
        axis=1,
    )
    small_all = packs[:, owned + n_halves * part :].reshape(n_shard, -1).astype(F32)
    taps_table = small_all[:, : part * taps].reshape(channels, taps).T
    bias = small_all[:, part * taps : part * (taps + 1)].reshape(channels)
    gain = small_all[:, part * (taps + 1) : part * (taps + 1) + owned].reshape(width)
    project_full = gather_shard(project_weight, n_shard).reshape(n_shard, n_dp, part, width)

    x_all = gather_dp(x_own, n_dp)
    g_all = gather_dp(g_own, n_dp)
    len_all = [len_own] + [swap(len_own, "dp", n_dp, k) for k in range(1, n_dp)]

    normeds, maskeds, swisheds, grad_expandeds, returned = [], [], [], [], []
    sums = None
    positions = lax.broadcasted_iota(jnp.int32, (count, length), 1)
    for k in range(n_dp):
        live = (positions < len_all[k][:, None]).astype(F32)
        normed, masked, swished, grad_expanded, grad_normed, parts = chunk_compute(
            x_all[k], g_all[k], live, gain, taps_table, bias, expand_slice, project_slice
        )
        normeds.append(normed)
        maskeds.append(masked)
        swisheds.append(swished.reshape(n_dp, per_peer, length, channels))
        grad_expandeds.append(grad_expanded)
        returned.append(grad_normed if k == 0 else swap(grad_normed, "dp", n_dp, k))
        sums = parts if sums is None else tuple(a + b for a, b in zip(sums, parts))

    stack = jnp.stack(swisheds)
    total = None
    for m in range(n_dp):
        piece = lax.dynamic_index_in_dim(stack, me ^ m, axis=1, keepdims=False)
        if m:
            piece = swap(piece, "dp", n_dp, m)
        piece = jnp.stack([piece[k ^ m] for k in range(n_dp)])
        rows = lax.dynamic_index_in_dim(project_full, me ^ m, axis=1, keepdims=False)
        term = jnp.dot(
            piece.reshape(count * length, channels),
            rows.reshape(channels, width),
            preferred_element_type=F32,
        )
        total = term if total is None else total + term
    mine = jnp.stack(
        [
            lax.dynamic_slice_in_dim(x_all[k], me * per_peer, per_peer, axis=0)
            for k in range(n_dp)
        ]
    )
    len_mine = jnp.stack(
        [
            lax.dynamic_slice_in_dim(len_all[k], me * per_peer, per_peer, axis=0)
            for k in range(n_dp)
        ]
    )
    live_mine = (positions < len_mine.reshape(count, 1)).astype(F32)
    encoded = (
        mine.reshape(count, length, width).astype(F32)
        + total.reshape(count, length, width) * live_mine[:, :, None]
    ).astype(BF16)
    encoded = jnp.take(
        encoded.reshape(n_dp, per_peer, length, width), me ^ jnp.arange(n_dp), axis=0
    ).reshape(count, length, width)

    grad_normed = sum(piece.astype(F32) for piece in returned)
    inputs = x_own.reshape(count * length, width).astype(F32)
    centred = inputs - jnp.mean(inputs, axis=1, keepdims=True)
    variance = jnp.mean(centred * centred, axis=1, keepdims=True)
    inverse = lax.rsqrt(variance + EPS)
    standard = centred * inverse
    grad_standard = grad_normed * gain
    grad_inputs = inverse * (
        grad_standard
        - jnp.mean(grad_standard, axis=1, keepdims=True)
        - standard * jnp.mean(grad_standard * standard, axis=1, keepdims=True)
    )
    frame_sorted = (g_own.reshape(count * length, width).astype(F32) + grad_inputs).astype(BF16)
    back = jnp.argmax(
        send_order[None, :] == jnp.arange(count, dtype=jnp.int32)[:, None], axis=1
    )
    frame_grad = jnp.take(frame_sorted.reshape(count, length, width), back, axis=0)

    expand_part = sum(
        lax.dot_general(a, b, (((0,), (0,)), ((), ())), preferred_element_type=F32)
        for a, b in zip(normeds, grad_expandeds)
    )
    project_part = sum(
        lax.dot_general(
            a.reshape(-1, channels), b, (((0,), (0,)), ((), ())), preferred_element_type=F32
        )
        for a, b in zip(swisheds, maskeds)
    )
    gain_part, bias_part, kernel_part = sums
    small_part = jnp.concatenate(
        [
            kernel_part.T.reshape(n_shard, part * taps),
            bias_part.reshape(n_shard, part),
            gain_part.reshape(n_shard, owned),
        ],
        axis=1,
    )
    small_part = jnp.pad(small_part, ((0, 0), (0, small_rows * wide - small_part.shape[1])))
    project_part = project_part.reshape(n_shard, part, width)
    grad_pack = jnp.concatenate(
        [expand_part.reshape(n_shard, owned, wide)]
        + [project_part[:, :, h * wide : (h + 1) * wide] for h in range(n_halves)]
        + [small_part.reshape(n_shard, small_rows, wide)],
        axis=1,
    )
    reduced = reduce_shard(grad_pack, n_shard).astype(BF16)
    gathered = jnp.stack(gather_dp(reduced, n_dp))
    gathered = jnp.take(gathered, me ^ jnp.arange(n_dp), axis=0).astype(F32)
    expand_grad = (
        gathered[:, :owned]
        .reshape(n_dp, owned, 2, n_shard, part)
        .transpose(1, 2, 3, 0, 4)
        .reshape(owned, 2 * width)
    )
    project_grad = jnp.concatenate(
        [
            gathered[:, owned + h * part : owned + (h + 1) * part].reshape(owned, wide)
            for h in range(n_halves)
        ],
        axis=1,
    )
    small_grad = gathered[:, owned + n_halves * part :].reshape(n_dp, -1)
    kernel_grad = small_grad[:, : part * taps].reshape(owned, taps)
    bias_grad = small_grad[:, part * taps : part * (taps + 1)].reshape(owned)
    gain_grad = jnp.sum(small_grad[:, part * (taps + 1) : part * (taps + 1) + owned], axis=0)
    return encoded, frame_grad, gain_grad, bias_grad, kernel_grad, expand_grad, project_grad


def body(*arrays):
    fast = lax.axis_size("dp") == 4 and lax.axis_size("shard") == 8
    return (fast_body if fast else generic_body)(*arrays)


def solution(mesh):
    return jax.shard_map(
        body,
        mesh=mesh,
        in_specs=(
            P(("dp", "shard"), None, None),
            P(("dp", "shard"), None, None),
            P(("dp", "shard")),
            P(("dp", "shard")),
            P("shard"),
            P("shard"),
            P("shard", None),
            P("shard", None),
            P("shard", None),
        ),
        out_specs=(
            P(("dp", "shard"), None, None),
            P(("dp", "shard"), None, None),
            P("shard"),
            P("shard"),
            P("shard", None),
            P("shard", None),
            P("shard", None),
        ),
        check_vma=False,
    )
```

```python
import functools

import jax
import jax.numpy as jnp
from jax import lax
from jax.experimental import pallas as pl
from jax.experimental.pallas import tpu as pltpu
from jax.sharding import PartitionSpec as P

EPS = 1e-05
F32 = jnp.float32
BF16 = jnp.bfloat16
LANES = 128
MARGIN = 16
NT = (((1,), (1,)), ((), ()))
TN = (((0,), (0,)), ((), ()))
LIGHT = pl.CostEstimate(flops=1, bytes_accessed=1, transcendentals=0)


def chunk_kernel(dims, meta, normed_ref, g_ref, taps_ref, we, wp, *refs):
    count, length, taps, source = dims
    before, refs = refs[: count if source else 0], refs[count if source else 0 :]
    sw_ref, ge_ref, gn_ref, small_ref = refs[:4]
    pieces, (ab, pad, gpad, slope) = refs[4 : 4 + count], refs[4 + count :]
    width, wide = we.shape
    channels = wide // 2
    tiles = channels // LANES

    zeros = jnp.zeros((MARGIN, LANES), F32)
    for u in range(count):
        for tile in range(tiles):
            for ref in (pad, gpad):
                ref[u, tile, :MARGIN, :] = zeros
                ref[u, tile, MARGIN + length :, :] = zeros
    small_ref[...] = jnp.zeros_like(small_ref)

    expanded = jnp.dot(normed_ref[...], we[...], preferred_element_type=F32)
    for tile in range(2 * tiles):
        ab[tile] = expanded[:, tile * LANES : (tile + 1) * LANES]

    first = (taps - 1) // 2
    positions = lax.broadcasted_iota(jnp.int32, (length, LANES), 0)

    @pl.loop(0, count)
    def _(u):
        at = pl.ds(pl.multiple_of(u * length, length), length)
        live = positions < meta[u]
        for tile in range(tiles):
            lanes = pl.ds(tile * LANES, LANES)
            gate = jax.nn.sigmoid(ab[tiles + tile, at, :])
            glu = jnp.where(live, ab[tile, at, :] * gate, 0.0).astype(BF16).astype(F32)
            pad[u, tile, MARGIN : MARGIN + length, :] = glu
            ab[tiles + tile, at, :] = gate
            conv = jnp.broadcast_to(taps_ref[taps : taps + 1, lanes], (length, LANES))
            for t in range(taps):
                conv += taps_ref[t : t + 1, lanes] * pad[u, tile, pl.ds(MARGIN - first + t, length), :]
            sig = jax.nn.sigmoid(conv)
            sw_ref[at, lanes] = jnp.where(live, conv * sig, 0.0).astype(BF16)
            slope[u, tile] = jnp.where(live, sig * (1.0 + conv * (1.0 - sig)), 0.0)

    for m in range(count):
        if source:
            pieces[m][:source] = before[m][...]
        chosen = meta[2 * count + (meta[count] ^ m)]
        pieces[m][source] = sw_ref[pl.ds(pl.multiple_of(chosen * length, length), length), :]

    grad_swish = lax.dot_general(g_ref[...], wp[...], NT, preferred_element_type=F32)
    for u in range(count):
        for tile in range(tiles):
            gpad[u, tile, MARGIN : MARGIN + length, :] = (
                grad_swish[u * length : (u + 1) * length, tile * LANES : (tile + 1) * LANES]
                * slope[u, tile]
            )

    def fold(value):
        return jnp.sum(value.reshape(length // 8, 8, LANES), axis=0)

    @pl.loop(0, count)
    def _(u):
        at = pl.ds(pl.multiple_of(u * length, length), length)
        live = positions < meta[u]
        for tile in range(tiles):
            lanes = pl.ds(tile * LANES, LANES)
            grad_conv = gpad[u, tile, MARGIN : MARGIN + length, :]
            grad_glu = jnp.zeros((length, LANES), F32)
            for t in range(taps):
                small_ref[tile, t] += fold(
                    pad[u, tile, pl.ds(MARGIN - first + t, length), :] * grad_conv
                )
                grad_glu += (
                    taps_ref[t : t + 1, lanes] * gpad[u, tile, pl.ds(MARGIN + first - t, length), :]
                )
            small_ref[tile, taps] += fold(grad_conv)
            grad_glu = jnp.where(live, grad_glu, 0.0)
            gate = ab[tiles + tile, at, :]
            through = grad_glu * gate
            ge_ref[at, lanes] = through.astype(BF16)
            ge_ref[at, pl.ds(channels + tile * LANES, LANES)] = (
                through * ab[tile, at, :] * (1.0 - gate)
            ).astype(BF16)

    span = 512
    for start in range(0, width, span):
        cols = slice(start, start + span)
        gn_ref[:, cols] = lax.dot_general(
            ge_ref[...], we[cols, :], NT, preferred_element_type=F32
        ).astype(BF16)


def chunk_call(meta, normed, g, taps_table, we, wp, before, dims):
    count, length, taps = dims
    source = before[0].shape[0] if before else 0
    rows, width = normed.shape
    wide = we.shape[1]
    channels = wide // 2
    tiles = channels // LANES
    last = g.shape[0] // rows - 1
    padded = pltpu.VMEM((count, tiles, length + 2 * MARGIN, LANES), F32)
    return pl.pallas_call(
        functools.partial(chunk_kernel, (count, length, taps, source)),
        out_shape=(
            jax.ShapeDtypeStruct((rows, channels), BF16),
            jax.ShapeDtypeStruct((rows, wide), BF16),
            jax.ShapeDtypeStruct((rows, width), BF16),
            jax.ShapeDtypeStruct((tiles, taps + 1, 8, LANES), F32),
        )
        + (jax.ShapeDtypeStruct((source + 1, length, channels), BF16),) * count,
        grid=(1,),
        in_specs=[in_smem(), in_vmem(), pl.BlockSpec((rows, width), lambda s: (last, 0))]
        + [in_vmem()] * (3 + len(before)),
        out_specs=(in_vmem(),) * (4 + count),
        scratch_shapes=[
            pltpu.VMEM((2 * tiles, rows, LANES), F32),
            padded,
            padded,
            pltpu.VMEM((count, tiles, length, LANES), F32),
        ],
        compiler_params=vmem_params(16),
        cost_estimate=LIGHT,
        name="chunk",
    )(meta, normed, g, taps_table, we, wp, *before)


def norm_kernel(x_ref, gain_ref, out_ref):
    x = x_ref[...].astype(F32)
    centred = x - jnp.mean(x, axis=1, keepdims=True)
    variance = jnp.mean(centred * centred, axis=1, keepdims=True)
    out_ref[...] = (centred * lax.rsqrt(variance + EPS) * gain_ref[...]).astype(BF16)


def norm_call(x, gain, rows):
    width = x.shape[1]
    step = 128
    block = pl.BlockSpec((step, width), lambda s: (s, 0))
    return pl.pallas_call(
        norm_kernel,
        out_shape=jax.ShapeDtypeStruct((rows, width), BF16),
        grid=(rows // step,),
        in_specs=[block, pl.BlockSpec((1, width), lambda s: (0, 0))],
        out_specs=block,
        compiler_params=vmem_params(8),
        cost_estimate=LIGHT,
        name="norm",
    )(x, gain)


def assemble_kernel(dims, meta, *refs):
    owned, part, taps, n_blocks = dims
    blocks = refs[:n_blocks]
    we, wp, taps_ref, gain_ref, small, sems = refs[n_blocks:]
    width, wide = we.shape
    halves = width // wide

    def copies(b):
        owner = meta[b]
        yield pltpu.make_async_copy(
            blocks[b].at[pl.ds(owned + halves * part, 16)], small.at[owner], sems.at[b, 0]
        )
        yield pltpu.make_async_copy(
            blocks[b].at[pl.ds(0, owned)],
            we.at[pl.ds(pl.multiple_of(owner * owned, owned), owned)],
            sems.at[b, 1],
        )
        for h in range(halves):
            yield pltpu.make_async_copy(
                blocks[b].at[pl.ds(owned + h * part, part)],
                wp.at[pl.ds(pl.multiple_of(owner * part, part), part), pl.ds(h * wide, wide)],
                sems.at[b, 2 + h],
            )

    for b in range(n_blocks):
        @pl.when(meta[b] >= 0)
        def _():
            for copy in copies(b):
                copy.start()
    for b in range(n_blocks):
        @pl.when(meta[b] >= 0)
        def _():
            for copy in copies(b):
                copy.wait()

    rows = [small[j].astype(F32) for j in range(small.shape[0])]
    taps_ref[:16] = jnp.concatenate([r[:, :part] for r in rows], axis=1)
    taps_ref[16:] = jnp.concatenate([r[:, LANES : LANES + part] for r in rows], axis=1)
    gain_ref[...] = jnp.concatenate([r[:1, 2 * LANES : 2 * LANES + owned] for r in rows], axis=1)


def assemble_call(blocks, owners, owned, part, width, taps):
    wide = blocks[0].shape[1]
    n_blocks = len(blocks)
    anywhere = pl.BlockSpec(memory_space=pl.ANY)
    return pl.pallas_call(
        functools.partial(assemble_kernel, (owned, part, taps, n_blocks)),
        out_shape=(
            jax.ShapeDtypeStruct((width, wide), BF16),
            jax.ShapeDtypeStruct((wide // 2, width), BF16),
            jax.ShapeDtypeStruct((taps + 1, wide // 2), F32),
            jax.ShapeDtypeStruct((1, width), F32),
        ),
        in_specs=[in_smem()] + [anywhere] * n_blocks,
        out_specs=(in_vmem(),) * 4,
        scratch_shapes=[
            pltpu.VMEM((width // owned, 16, wide), BF16),
            pltpu.SemaphoreType.DMA((n_blocks, 2 + width // wide)),
        ],
        compiler_params=vmem_params(8),
        cost_estimate=LIGHT,
        name="assemble",
    )(owners, *blocks)


def vmem_params(mib):
    return pltpu.CompilerParams(vmem_limit_bytes=mib * 1024 * 1024)


def in_vmem():
    return pl.BlockSpec(memory_space=pltpu.VMEM)


def in_smem():
    return pl.BlockSpec(memory_space=pltpu.SMEM)


def owned_column(channel, index, owned, part):
    return (channel // part) * owned + index * part + channel % part


def pack_kernel(
    meta, expand_ref, project_ref, kernel_ref, bias_ref, gain_ref, x_ref, g_ref, pack_ref, both_ref, sems
):
    rows = x_ref.shape[0]
    copies = [
        pltpu.make_async_copy(ref, both_ref.at[pl.ds(i * rows, rows)], sems.at[i])
        for i, ref in enumerate((x_ref, g_ref))
    ]
    for copy in copies:
        copy.start()
    owned, width = project_ref.shape
    taps = kernel_ref.shape[1]
    wide = pack_ref.shape[1]
    channels = wide // 2
    part = owned * channels // width
    index = meta[0]
    row = lax.broadcasted_iota(jnp.int32, (width, channels), 0)
    col = lax.broadcasted_iota(jnp.int32, (1, channels), 1)
    pick = jnp.where(row == owned_column(col, index, owned, part), 1.0, 0.0).astype(BF16)
    for h in range(2):
        pack_ref[:owned, h * channels : (h + 1) * channels] = jnp.dot(
            expand_ref[:, h * width : (h + 1) * width], pick, preferred_element_type=F32
        ).astype(BF16)
    block = project_ref[pl.ds(pl.multiple_of(index * part, part), part), :]
    for h in range(width // wide):
        pack_ref[owned + h * part : owned + (h + 1) * part, :] = block[:, h * wide : (h + 1) * wide]
    mine = lax.broadcasted_iota(jnp.int32, (owned, LANES), 1) + index * part
    mine = jnp.where(lax.broadcasted_iota(jnp.int32, (owned, LANES), 0) == mine, 1.0, 0.0)
    mine = mine.astype(BF16)
    table = jnp.concatenate(
        [
            lax.dot_general(kernel_ref[...], mine, TN, preferred_element_type=F32),
            jnp.dot(bias_ref[...], mine, preferred_element_type=F32),
        ],
        axis=0,
    )
    base = owned + width // wide * part
    pack_ref[base:, :LANES] = table[:16].astype(BF16)
    pack_ref[base:, LANES : 2 * LANES] = table[16:].astype(BF16)
    gain = jnp.broadcast_to(gain_ref[...].astype(F32), (16, owned))
    rest = jnp.zeros((16, wide - 2 * LANES - owned), F32)
    pack_ref[base:, 2 * LANES :] = jnp.concatenate([gain, rest], axis=1).astype(BF16)
    for copy in copies:
        copy.wait()


def pack_call(index, expand_weight, project_weight, kernel, bias, gain, x, g, part, wide):
    owned, width = project_weight.shape
    rows = x.shape[0]
    anywhere = pl.BlockSpec(memory_space=pl.ANY)
    return pl.pallas_call(
        pack_kernel,
        out_shape=(
            jax.ShapeDtypeStruct((owned + width // wide * part + 16, wide), BF16),
            jax.ShapeDtypeStruct((2 * rows, width), BF16),
        ),
        in_specs=[in_smem()] + [in_vmem()] * 5 + [anywhere] * 2,
        out_specs=(in_vmem(), anywhere),
        scratch_shapes=[pltpu.SemaphoreType.DMA((2,))],
        compiler_params=vmem_params(16),
        cost_estimate=LIGHT,
        name="pack",
    )(index.reshape(1), expand_weight, project_weight, kernel, bias[None], gain[None], x, g)


def grads_kernel(dims, meta, *refs):
    n, chips, owned, part, taps = dims
    normed, ge, sw, g, small = [refs[i * n : (i + 1) * n] for i in range(5)]
    keep, give, cotangent, sems = refs[5 * n :]
    core = meta[0]
    rows = ge[0].shape[0]
    copies = [
        pltpu.make_async_copy(
            g[k].at[pl.ds(g[k].shape[0] - rows, rows)],
            cotangent.at[pl.ds(k * rows, rows)],
            sems.at[k],
        )
        for k in range(n)
    ]
    for copy in copies:
        copy.start()
    wide = ge[0].shape[1]
    width = normed[0].shape[1]
    channels = wide // 2
    tiles = channels // LANES

    def emit(chip, which, rows, cols, value):
        @pl.when(core == which)
        def _():
            keep[chip, rows, cols] = value

        @pl.when(core != which)
        def _():
            give[chip, rows, cols] = value

    every = slice(None)
    upstream = jnp.concatenate([a[...] for a in ge], axis=0)
    for chip in range(chips):
        cols = slice(2 * chip * owned, 2 * (chip + 1) * owned)
        inputs = jnp.concatenate([a[:, cols] for a in normed], axis=0)
        block = lax.dot_general(inputs, upstream, TN, preferred_element_type=F32).astype(BF16)
        for which in range(2):
            emit(chip, which, slice(0, owned), every, block[which * owned : (which + 1) * owned])
    for copy in copies:
        copy.wait()
    block = lax.dot_general(
        jnp.concatenate([a[...] for a in sw], axis=0),
        cotangent[...],
        TN,
        preferred_element_type=F32,
    ).astype(BF16)
    sums = sum(a[...] for a in small)
    sums = jnp.sum(sums, axis=2)
    sums = jnp.concatenate([sums[tile] for tile in range(tiles)], axis=1)
    base = owned + width // wide * part
    for chip in range(chips):
        for which in range(2):
            owner = 2 * chip + which
            rows = block[owner * part : (owner + 1) * part]
            for h in range(width // wide):
                emit(
                    chip,
                    which,
                    slice(owned + h * part, owned + (h + 1) * part),
                    every,
                    rows[:, h * wide : (h + 1) * wide],
                )
            mine = sums[:, owner * part : (owner + 1) * part]
            pad = jnp.zeros((16, LANES - part), F32)
            line = jnp.concatenate(
                [mine[:16], pad, mine[16:], pad], axis=1
            )
            line = jnp.concatenate(
                [line, jnp.zeros((16, wide - line.shape[1]), F32)], axis=1
            ).astype(BF16)
            emit(chip, which, slice(base, base + 16), every, line)


def grads_call(core, normed, ge, sw, g, small, owned, part, taps):
    n = len(normed)
    rows, width = normed[0].shape
    wide = ge[0].shape[1]
    chips = width // owned // 2
    height = owned + width // wide * part + 16
    shape = jax.ShapeDtypeStruct((chips, height, wide), BF16)
    return pl.pallas_call(
        functools.partial(grads_kernel, (n, chips, owned, part, taps)),
        out_shape=(shape, shape),
        in_specs=[in_smem()]
        + [in_vmem()] * (3 * n)
        + [pl.BlockSpec(memory_space=pl.ANY)] * n
        + [in_vmem()] * n,
        out_specs=(in_vmem(), in_vmem()),
        scratch_shapes=[pltpu.VMEM((n * rows, width), BF16), pltpu.SemaphoreType.DMA((n,))],
        compiler_params=vmem_params(32),
        cost_estimate=LIGHT,
        name="weight_grads",
    )(core.reshape(1), *normed, *ge, *sw, *g, *small)


def encode_kernel(dims, meta, *refs):
    n, n_blocks, length, owned, part = dims
    pieces = refs[:n]
    frames = refs[n : 2 * n]
    blocks = refs[2 * n : 2 * n + n_blocks]
    out_ref = refs[2 * n + n_blocks]
    cat, weight, residual, frame_sems, piece_sems, sems = refs[2 * n + n_blocks + 1 :]
    channels = pieces[0].shape[2]
    me = meta[0]
    first = 1 + n * n

    def weight_copies(b):
        owner = meta[first + b]
        return [
            pltpu.make_async_copy(
                blocks[b].at[pl.ds(i * part, part)],
                weight.at[pl.ds(pl.multiple_of(i * channels + owner * part, part), part)],
                sems.at[b, i],
            )
            for i in range(n)
        ]

    def rows(utterance):
        return pl.ds(pl.multiple_of(utterance * length, length), length)

    frame_copies = [
        pltpu.make_async_copy(
            frames[k].at[rows(meta[1 + k * n + me])], residual.at[rows(me ^ k)], frame_sems.at[k]
        )
        for k in range(n)
    ]
    for m in range(n):
        lanes = pl.ds(pl.multiple_of((me ^ m) * channels, channels), channels)
        for k in range(n):
            frame_copies.append(
                pltpu.make_async_copy(
                    pieces[m].at[k], cat.at[rows(me ^ m ^ k), lanes], piece_sems.at[m, k]
                )
            )
    for copy in frame_copies:
        copy.start()
    for b in range(n_blocks):
        @pl.when(meta[first + b] >= 0)
        def _():
            for copy in weight_copies(b):
                copy.start()

    for copy in frame_copies:
        copy.wait()
    for b in range(n_blocks):
        @pl.when(meta[first + b] >= 0)
        def _():
            for copy in weight_copies(b):
                copy.wait()

    span = 512
    for start in range(0, cat.shape[1], span):
        cols = slice(start, start + span)
        term = jnp.dot(cat[...], weight[:, cols], preferred_element_type=F32)
        out_ref[:, cols] = (residual[:, cols].astype(F32) + term).astype(BF16)


def encode_call(me, orders, pieces, frames, blocks, owners, owned, part, length):
    n = len(pieces)
    channels = pieces[0].shape[2]
    width = blocks[0].shape[1]
    n_blocks = len(blocks)
    meta = jnp.concatenate([me.reshape(1), orders, owners])
    anywhere = pl.BlockSpec(memory_space=pl.ANY)
    return pl.pallas_call(
        functools.partial(encode_kernel, (n, n_blocks, length, owned, part)),
        out_shape=jax.ShapeDtypeStruct((n * length, width), BF16),
        in_specs=[in_smem()] + [anywhere] * (2 * n + n_blocks),
        out_specs=in_vmem(),
        scratch_shapes=[
            pltpu.VMEM((n * length, width), BF16),
            pltpu.VMEM((width, width), BF16),
            pltpu.VMEM((n * length, width), BF16),
            pltpu.SemaphoreType.DMA((n,)),
            pltpu.SemaphoreType.DMA((n, n)),
            pltpu.SemaphoreType.DMA((n_blocks, n)),
        ],
        compiler_params=vmem_params(48),
        cost_estimate=LIGHT,
        name="encode",
    )(meta, *pieces, *frames, *blocks)


def frame_grad_kernel(n, x_ref, g_ref, gain_ref, *refs):
    out_ref = refs[n]
    x = x_ref[...].astype(F32)
    centred = x - jnp.mean(x, axis=1, keepdims=True)
    inverse = lax.rsqrt(jnp.mean(centred * centred, axis=1, keepdims=True) + EPS)
    standard = centred * inverse
    grad = sum(ref[...].astype(F32) for ref in refs[:n]) * gain_ref[...]
    grad_in = inverse * (
        grad
        - jnp.mean(grad, axis=1, keepdims=True)
        - standard * jnp.mean(grad * standard, axis=1, keepdims=True)
    )
    out_ref[...] = (g_ref[...].astype(F32) + grad_in).astype(BF16)


def frame_grad_call(x, g, gain, returned):
    count, length, width = x.shape
    rows = count * length
    step = 64
    block = pl.BlockSpec((step, width), lambda s: (s, 0))
    out = pl.pallas_call(
        functools.partial(frame_grad_kernel, len(returned)),
        out_shape=jax.ShapeDtypeStruct((rows, width), BF16),
        grid=(rows // step,),
        in_specs=[block, block, pl.BlockSpec((1, width), lambda s: (0, 0))]
        + [block] * len(returned),
        out_specs=block,
        compiler_params=vmem_params(48),
        cost_estimate=LIGHT,
        name="frame_grad",
    )(x.reshape(rows, width), g.reshape(rows, width), gain, *returned)
    return out.reshape(count, length, width)


def unpack_kernel(dims, meta, *refs):
    n, owned, part = dims
    lows, highs = refs[:n], refs[n : 2 * n]
    weight_ref, gain_ref, expand_ref, project_ref, gain_out, cat = refs[2 * n :]
    wide = lows[0].shape[1]
    cut = lows[0].shape[0]
    channels = wide // 2
    width = project_ref.shape[1]
    me = meta[0]
    for k in range(n):
        index = me ^ k
        lanes = pl.ds(pl.multiple_of(index * channels, channels), channels)
        for h in range(2):
            cols = slice(h * channels, (h + 1) * channels)
            cat[h, :cut, lanes] = lows[k][:, cols]
            cat[h, cut:, lanes] = highs[k][: owned - cut, cols]
        rows = pl.ds(pl.multiple_of(index * part, part), part)
        for h in range(width // wide):
            start = owned - cut + h * part
            project_ref[rows, h * wide : (h + 1) * wide] = highs[k][
                start : start + part, :
            ].astype(F32)
    along = jnp.zeros((owned, 1), F32)
    span = 512
    for start in range(0, width, span):
        row = lax.broadcasted_iota(jnp.int32, (width, span), 0)
        col = lax.broadcasted_iota(jnp.int32, (1, span), 1) + start
        place = col % owned // part * channels + col // owned * part + col % part
        spread = jnp.where(row == place, 1.0, 0.0).astype(BF16)
        for h in range(2):
            cols = slice(h * width + start, h * width + start + span)
            grad = jnp.dot(cat[h], spread, preferred_element_type=F32)
            expand_ref[:, cols] = grad
            along += jnp.sum(grad * weight_ref[:, cols].astype(F32), axis=1, keepdims=True)
    gain_out[...] = along / gain_ref[...]


def unpack_call(me, lows, highs, weight, gain, owned, part, width):
    return pl.pallas_call(
        functools.partial(unpack_kernel, (len(lows), owned, part)),
        out_shape=(
            jax.ShapeDtypeStruct((owned, 2 * width), F32),
            jax.ShapeDtypeStruct((owned, width), F32),
            jax.ShapeDtypeStruct((owned, 1), F32),
        ),
        in_specs=[in_smem()] + [in_vmem()] * (2 * len(lows) + 2),
        out_specs=(in_vmem(),) * 3,
        scratch_shapes=[pltpu.VMEM((2, owned, width), BF16)],
        compiler_params=vmem_params(24),
        cost_estimate=LIGHT,
        name="unpack",
    )(me.reshape(1), *lows, *highs, weight, gain)


def along_z(x, pairs):
    return lax.ppermute(x, "shard", [(2 * a + c, 2 * b + c) for a, b in pairs for c in range(2)])


RIGHT = [(0, 1), (1, 2), (2, 3)]
LEFT = [(3, 2), (2, 1), (1, 0)]


def tie(value, *after):
    return lax.optimization_barrier((value,) + after)[0]


def line_hops(x, chip, before_second=(), before_third=()):
    right = along_z(x, RIGHT)
    left = along_z(x, LEFT)
    held = lax.optimization_barrier((right, left) + tuple(before_second))
    right2 = along_z(held[0], [(1, 2), (2, 3)])
    left2 = along_z(held[1], [(2, 1), (1, 0)])
    held = lax.optimization_barrier((right2, left2) + tuple(before_third))
    right3 = along_z(held[0], [(2, 3)])
    left3 = along_z(held[1], [(1, 0)])
    return x, right, left, right2, left2, right3, left3


def line_owners(chip, core):
    chips = [chip]
    for distance in (1, 2, 3):
        chips.append(jnp.where(chip >= distance, chip - distance, -1))
        chips.append(jnp.where(chip + distance <= 3, chip + distance, -1))
    owners = [jnp.where(c >= 0, 2 * c + core, -1) for c in chips]
    owners += [jnp.where(c >= 0, 2 * c + 1 - core, -1) for c in chips]
    return jnp.stack(owners).astype(jnp.int32)


def across_cores(blocks):
    return list(blocks) + [swap(block, "shard", 8, 1) for block in blocks]


def hop_kernel(counts, meta, *refs):
    n = len(counts)
    outs = refs[-n:]
    keep, got, carried = refs[:n], refs[n : 2 * n], list(refs[2 * n : -n])
    for i in range(n):
        total = keep[i][...].astype(F32) + got[i][...].astype(F32)
        for _ in range(counts[i]):
            total = total + carried.pop(0)[...].astype(F32)
        outs[i][...] = total.astype(BF16)


def hop_call(keep, got, chips, carried):
    n = len(chips)
    rows, wide = keep.shape[1:]
    step = rows // 2
    pick = [
        pl.BlockSpec((None, step, wide), lambda s, meta, i=i: (meta[i], s, 0)) for i in range(n)
    ]
    plain = pl.BlockSpec((step, wide), lambda s, meta: (s, 0))
    flat = [array for arrays in carried for array in arrays]
    return pl.pallas_call(
        functools.partial(hop_kernel, [len(arrays) for arrays in carried]),
        out_shape=(jax.ShapeDtypeStruct((rows, wide), BF16),) * n,
        grid_spec=pltpu.PrefetchScalarGridSpec(
            num_scalar_prefetch=1,
            grid=(rows // step,),
            in_specs=pick + pick + [plain] * len(flat),
            out_specs=(plain,) * n,
        ),
        compiler_params=vmem_params(12),
        cost_estimate=LIGHT,
        name="hop",
    )(jnp.stack(chips).astype(jnp.int32), *[keep] * n, *[got] * n, *flat)


def fast_body(
    frames,
    cotangent,
    lengths,
    send_order,
    norm_gain,
    conv_bias,
    kernel,
    expand_weight,
    project_weight,
):
    n_dp, n_shard = lax.axis_size("dp"), lax.axis_size("shard")
    count, length, width = frames.shape
    owned, taps = kernel.shape
    part = owned // n_dp
    channels = n_shard * part
    wide = 2 * channels
    me = lax.axis_index("dp").astype(jnp.int32)
    shard = lax.axis_index("shard").astype(jnp.int32)
    chip, core = shard // 2, shard % 2

    rows = count * length
    dims = (count, length, taps)
    ints = jnp.concatenate([lengths, lengths, send_order])
    ints = lax.all_to_all(jnp.broadcast_to(ints, (n_dp, 3 * count)), "dp", 0, 0, tiled=True)
    x_own = frames.reshape(rows, width)
    g_own = cotangent.reshape(rows, width)
    pack, both = pack_call(
        me, expand_weight, project_weight, kernel, conv_bias, norm_gain, x_own, g_own, part, wide
    )
    pack, both, ints = lax.optimization_barrier((pack, both, ints))
    ints = jnp.take(ints, me ^ jnp.arange(n_dp), axis=0)
    ints = jnp.where(jnp.arange(3 * count) // count == 1, me, ints)
    orders = ints[:, 2 * count :].reshape(-1)
    hops = line_hops(pack, chip)
    both_x = swap(both, "dp", 4, 1)
    both_y = swap(both, "dp", 4, 2)
    far_x = swap(both_x[:rows], "dp", 4, 2)
    far_g = swap(both_y[rows:], "dp", 4, 1)
    x_all = [x_own, both_x, both_y, far_x]
    g_all = [g_own, both_x, both_y, far_g]
    owners = line_owners(chip, core)
    blocks = across_cores(hops)
    we, wp, taps_table, gain = assemble_call(blocks, owners, owned, part, width, taps)
    normed = [norm_call(x, gain, rows) for x in x_all]

    project_hops = line_hops(tie(project_weight, hops[5], hops[6]), chip)

    swished, ge, returned, small_parts, pieces = [], [], [], [], []
    for k in range(n_dp):
        if k == 2:
            normed[k] = tie(normed[k], project_hops[1], project_hops[2])
        out = chunk_call(ints[k], normed[k], g_all[k], taps_table, we, wp, pieces, dims)
        swished.append(out[0])
        ge.append(out[1])
        returned.append(out[2])
        small_parts.append(out[3])
        pieces = list(out[4:])
        if k in (1, 2):
            returned[k] = swap(returned[k], "dp", n_dp, k)

    keep, give = grads_call(
        core,
        [tie(normed[0], returned[1], project_hops[3], project_hops[4])] + normed[1:],
        ge,
        swished,
        g_all,
        small_parts,
        owned,
        part,
        taps,
    )

    project_blocks = across_cores(project_hops)
    keep = tie(keep, project_hops[5], project_hops[6])
    got = swap(give, "shard", 8, 1)
    (first,) = hop_call(keep, got, [jnp.where(chip <= 1, 3, 0)], [[]])
    come = along_z(first, [(0, 1), (3, 2)])
    returned[3], *rest = lax.optimization_barrier((returned[3], *pieces[1:], first))[:-1]
    returned[3] = swap(returned[3], "dp", n_dp, 3)
    pieces[1:] = [swap(piece, "dp", n_dp, m + 1) for m, piece in enumerate(rest)]
    right, left = hop_call(
        keep, got, [jnp.minimum(chip + 2, 3), jnp.maximum(chip - 2, 0)], [[come], [come]]
    )
    right = along_z(right, [(0, 1), (1, 2)])
    left = along_z(left, [(3, 2), (2, 1)])
    right, left = lax.optimization_barrier((right, left, returned[2], *pieces[1:]))[:2]
    right, left = hop_call(
        keep, got, [jnp.minimum(chip + 1, 3), jnp.maximum(chip - 1, 0)], [[right], [left]]
    )
    pieces[0] = tie(pieces[0], right)
    right = along_z(right, RIGHT)
    left = along_z(left, LEFT)
    encoded = encode_call(me, orders, pieces, x_all, project_blocks, owners, owned, part, length)
    right, left = lax.optimization_barrier((right, left, encoded, returned[3]))[:2]
    (reduced,) = hop_call(keep, got, [chip], [[right, left]])

    cut = 160
    low, high = reduced[:cut], reduced[cut:]
    lows = [low, swap(low, "dp", 4, 1), swap(low, "dp", 4, 2)]
    highs = [high, swap(high, "dp", 4, 1), swap(high, "dp", 4, 2)]
    lows.append(swap(lows[1], "dp", 4, 2))
    highs.append(swap(highs[2], "dp", 4, 1))
    cotangent_last = tie(cotangent, reduced)
    frame_grad = frame_grad_call(frames, cotangent_last, gain, returned)
    lows[3], highs[3] = lax.optimization_barrier((lows[3], highs[3], frame_grad))[:2]
    expand_grad, project_grad, gain_grad = unpack_call(
        me, lows, highs, expand_weight, norm_gain.astype(F32)[:, None], owned, part, width
    )
    base = owned + width // wide * part - cut
    tails = jnp.stack([a[base:] for a in highs])
    tails = jnp.take(tails, me ^ jnp.arange(n_dp), axis=0).astype(F32)
    table = jnp.concatenate([tails[:, :, :part], tails[:, :, LANES : LANES + part]], axis=1)
    table = table.transpose(0, 2, 1).reshape(owned, taps + 1)
    return (
        encoded.reshape(frames.shape),
        frame_grad,
        gain_grad.reshape(owned),
        table[:, taps],
        table[:, :taps],
        expand_grad,
        project_grad,
    )


def depthwise(signal, taps_table):
    taps = taps_table.shape[0]
    half = (taps - 1) // 2
    length = signal.shape[1]
    padded = jnp.pad(signal, ((0, 0), (half, half), (0, 0)))
    result = jnp.zeros_like(signal)
    for offset in range(taps):
        result = result + padded[:, offset : offset + length, :] * taps_table[offset]
    return result


def kernel_terms(signal, upstream, taps):
    half = (taps - 1) // 2
    length = signal.shape[1]
    padded = jnp.pad(signal, ((0, 0), (half, half), (0, 0)))
    rows = []
    for offset in range(taps):
        rows.append(jnp.sum(padded[:, offset : offset + length, :] * upstream, axis=(0, 1)))
    return jnp.stack(rows, axis=0)


def chunk_compute(x, g, live, gain, taps, bias, expand_slice, project_slice):
    count, length, width = x.shape
    rows = count * length
    channels = taps.shape[1]
    inputs = x.reshape(rows, width).astype(F32)
    live_rows = live.reshape(rows, 1)
    centred = inputs - jnp.mean(inputs, axis=1, keepdims=True)
    variance = jnp.mean(centred * centred, axis=1, keepdims=True)
    standard = centred * lax.rsqrt(variance + EPS)
    normed = (standard * gain).astype(BF16)
    expanded = jnp.dot(normed, expand_slice, preferred_element_type=F32)
    value = expanded[:, :channels]
    gate = jax.nn.sigmoid(expanded[:, channels:])
    glu = (value * gate * live_rows).astype(BF16).astype(F32).reshape(count, length, channels)
    conv = depthwise(glu, taps).reshape(rows, channels) + bias
    conv_sig = jax.nn.sigmoid(conv)
    swished = (conv * conv_sig).astype(BF16)
    masked = (g.reshape(rows, width).astype(F32) * live_rows).astype(BF16)
    grad_swish = lax.dot_general(
        masked, project_slice, (((1,), (1,)), ((), ())), preferred_element_type=F32
    )
    grad_conv = grad_swish * conv_sig * (1.0 + conv * (1.0 - conv_sig))
    bias_part = jnp.sum(grad_conv, axis=0)
    volume = grad_conv.reshape(count, length, channels)
    kernel_part = kernel_terms(glu, volume, taps.shape[0])
    grad_glu = depthwise(volume, taps[::-1]).reshape(rows, channels) * live_rows
    grad_expanded = jnp.concatenate(
        [grad_glu * gate, grad_glu * value * gate * (1.0 - gate)], axis=1
    ).astype(BF16)
    grad_normed = lax.dot_general(
        grad_expanded, expand_slice, (((1,), (1,)), ((), ())), preferred_element_type=F32
    )
    gain_part = jnp.sum(grad_normed * standard, axis=0)
    return normed, masked, swished, grad_expanded, grad_normed.astype(BF16), (
        gain_part,
        bias_part,
        kernel_part,
    )


def swap(x, axis, size, k):
    return lax.ppermute(x, axis, [(p, p ^ k) for p in range(size)])


def gather_dp(x, n_dp):
    if n_dp == 4:
        half = x.shape[0] // 2
        along_x = swap(x, "dp", 4, 1)
        along_y = swap(x, "dp", 4, 2)
        far = jnp.concatenate(
            [swap(along_x[:half], "dp", 4, 2), swap(along_y[half:], "dp", 4, 1)], axis=0
        )
        return [x, along_x, along_y, far]
    return [x] + [swap(x, "dp", n_dp, k) for k in range(1, n_dp)]


def gather_shard(x, n_shard):
    if n_shard == 8:
        me = lax.axis_index("shard")
        chip, core = me // 2, me % 2
        blocks = [x] + [
            lax.ppermute(x, "shard", [(p, (p + 2 * k) % 8) for p in range(8)]) for k in (1, 2, 3)
        ]
        mine = jnp.stack(blocks)
        mine = jnp.take(mine, (chip - jnp.arange(4)) % 4, axis=0)
        other = swap(mine, "shard", 8, 1)
        pair = jnp.where(core == 0, jnp.stack([mine, other], 1), jnp.stack([other, mine], 1))
        return pair.reshape((8,) + x.shape)
    return lax.all_gather(x, "shard", axis=0)


def reduce_shard(x, n_shard):
    x = x.astype(BF16)
    if n_shard == 8:
        me = lax.axis_index("shard")
        chip, core = me // 2, me % 2
        cube = x.reshape((4, 2) + x.shape[1:])
        keep = jnp.take(cube, core, axis=1)
        give = jnp.take(cube, 1 - core, axis=1)
        both = (keep.astype(F32) + swap(give, "shard", 8, 1).astype(F32)).astype(BF16)
        total = jnp.take(both, chip, axis=0).astype(F32)
        for k in (1, 2, 3):
            piece = jnp.take(both, (chip + k) % 4, axis=0)
            total = total + lax.ppermute(
                piece, "shard", [(p, (p + 2 * k) % 8) for p in range(8)]
            ).astype(F32)
        return total
    return lax.psum_scatter(x, "shard", scatter_dimension=0, tiled=False).astype(F32)


def generic_body(
    frames,
    cotangent,
    lengths,
    send_order,
    norm_gain,
    conv_bias,
    kernel,
    expand_weight,
    project_weight,
):
    n_dp, n_shard = lax.axis_size("dp"), lax.axis_size("shard")
    count, length, width = frames.shape
    per_peer = count // n_dp
    owned, taps = kernel.shape
    part = owned // n_dp
    channels = n_shard * part
    me = lax.axis_index("dp")

    x_own = jnp.take(frames, send_order, axis=0)
    g_own = jnp.take(cotangent, send_order, axis=0)
    len_own = jnp.take(lengths, send_order, axis=0)

    expand_cols = lax.dynamic_index_in_dim(
        expand_weight.reshape(owned, 2, n_shard, n_dp, part), me, axis=3, keepdims=False
    ).reshape(owned, 2 * channels)
    project_rows = lax.dynamic_slice_in_dim(project_weight, me * part, part, axis=0)
    small = jnp.concatenate(
        [
            lax.dynamic_slice_in_dim(kernel, me * part, part, axis=0).reshape(-1),
            lax.dynamic_slice_in_dim(conv_bias, me * part, part, axis=0),
            norm_gain,
        ]
    )
    wide = 2 * channels
    small_rows = 16
    small = jnp.pad(small, (0, small_rows * wide - small.shape[0])).reshape(small_rows, wide)
    n_halves = width // wide
    pack = jnp.concatenate(
        [expand_cols] + [project_rows[:, h * wide : (h + 1) * wide] for h in range(n_halves)] + [small], axis=0
    )
    packs = gather_shard(pack, n_shard)
    expand_slice = packs[:, :owned].reshape(width, wide)
    project_slice = jnp.concatenate(
        [
            packs[:, owned + h * part : owned + (h + 1) * part].reshape(channels, wide)
            for h in range(n_halves)
        ],
        axis=1,
    )
    small_all = packs[:, owned + n_halves * part :].reshape(n_shard, -1).astype(F32)
    taps_table = small_all[:, : part * taps].reshape(channels, taps).T
    bias = small_all[:, part * taps : part * (taps + 1)].reshape(channels)
    gain = small_all[:, part * (taps + 1) : part * (taps + 1) + owned].reshape(width)
    project_full = gather_shard(project_weight, n_shard).reshape(n_shard, n_dp, part, width)

    x_all = gather_dp(x_own, n_dp)
    g_all = gather_dp(g_own, n_dp)
    len_all = [len_own] + [swap(len_own, "dp", n_dp, k) for k in range(1, n_dp)]

    normeds, maskeds, swisheds, grad_expandeds, returned = [], [], [], [], []
    sums = None
    positions = lax.broadcasted_iota(jnp.int32, (count, length), 1)
    for k in range(n_dp):
        live = (positions < len_all[k][:, None]).astype(F32)
        normed, masked, swished, grad_expanded, grad_normed, parts = chunk_compute(
            x_all[k], g_all[k], live, gain, taps_table, bias, expand_slice, project_slice
        )
        normeds.append(normed)
        maskeds.append(masked)
        swisheds.append(swished.reshape(n_dp, per_peer, length, channels))
        grad_expandeds.append(grad_expanded)
        returned.append(grad_normed if k == 0 else swap(grad_normed, "dp", n_dp, k))
        sums = parts if sums is None else tuple(a + b for a, b in zip(sums, parts))

    stack = jnp.stack(swisheds)
    total = None
    for m in range(n_dp):
        piece = lax.dynamic_index_in_dim(stack, me ^ m, axis=1, keepdims=False)
        if m:
            piece = swap(piece, "dp", n_dp, m)
        piece = jnp.stack([piece[k ^ m] for k in range(n_dp)])
        rows = lax.dynamic_index_in_dim(project_full, me ^ m, axis=1, keepdims=False)
        term = jnp.dot(
            piece.reshape(count * length, channels),
            rows.reshape(channels, width),
            preferred_element_type=F32,
        )
        total = term if total is None else total + term
    mine = jnp.stack(
        [
            lax.dynamic_slice_in_dim(x_all[k], me * per_peer, per_peer, axis=0)
            for k in range(n_dp)
        ]
    )
    len_mine = jnp.stack(
        [
            lax.dynamic_slice_in_dim(len_all[k], me * per_peer, per_peer, axis=0)
            for k in range(n_dp)
        ]
    )
    live_mine = (positions < len_mine.reshape(count, 1)).astype(F32)
    encoded = (
        mine.reshape(count, length, width).astype(F32)
        + total.reshape(count, length, width) * live_mine[:, :, None]
    ).astype(BF16)
    encoded = jnp.take(
        encoded.reshape(n_dp, per_peer, length, width), me ^ jnp.arange(n_dp), axis=0
    ).reshape(count, length, width)

    grad_normed = sum(piece.astype(F32) for piece in returned)
    inputs = x_own.reshape(count * length, width).astype(F32)
    centred = inputs - jnp.mean(inputs, axis=1, keepdims=True)
    variance = jnp.mean(centred * centred, axis=1, keepdims=True)
    inverse = lax.rsqrt(variance + EPS)
    standard = centred * inverse
    grad_standard = grad_normed * gain
    grad_inputs = inverse * (
        grad_standard
        - jnp.mean(grad_standard, axis=1, keepdims=True)
        - standard * jnp.mean(grad_standard * standard, axis=1, keepdims=True)
    )
    frame_sorted = (g_own.reshape(count * length, width).astype(F32) + grad_inputs).astype(BF16)
    back = jnp.argmax(
        send_order[None, :] == jnp.arange(count, dtype=jnp.int32)[:, None], axis=1
    )
    frame_grad = jnp.take(frame_sorted.reshape(count, length, width), back, axis=0)

    expand_part = sum(
        lax.dot_general(a, b, (((0,), (0,)), ((), ())), preferred_element_type=F32)
        for a, b in zip(normeds, grad_expandeds)
    )
    project_part = sum(
        lax.dot_general(
            a.reshape(-1, channels), b, (((0,), (0,)), ((), ())), preferred_element_type=F32
        )
        for a, b in zip(swisheds, maskeds)
    )
    gain_part, bias_part, kernel_part = sums
    small_part = jnp.concatenate(
        [
            kernel_part.T.reshape(n_shard, part * taps),
            bias_part.reshape(n_shard, part),
            gain_part.reshape(n_shard, owned),
        ],
        axis=1,
    )
    small_part = jnp.pad(small_part, ((0, 0), (0, small_rows * wide - small_part.shape[1])))
    project_part = project_part.reshape(n_shard, part, width)
    grad_pack = jnp.concatenate(
        [expand_part.reshape(n_shard, owned, wide)]
        + [project_part[:, :, h * wide : (h + 1) * wide] for h in range(n_halves)]
        + [small_part.reshape(n_shard, small_rows, wide)],
        axis=1,
    )
    reduced = reduce_shard(grad_pack, n_shard).astype(BF16)
    gathered = jnp.stack(gather_dp(reduced, n_dp))
    gathered = jnp.take(gathered, me ^ jnp.arange(n_dp), axis=0).astype(F32)
    expand_grad = (
        gathered[:, :owned]
        .reshape(n_dp, owned, 2, n_shard, part)
        .transpose(1, 2, 3, 0, 4)
        .reshape(owned, 2 * width)
    )
    project_grad = jnp.concatenate(
        [
            gathered[:, owned + h * part : owned + (h + 1) * part].reshape(owned, wide)
            for h in range(n_halves)
        ],
        axis=1,
    )
    small_grad = gathered[:, owned + n_halves * part :].reshape(n_dp, -1)
    kernel_grad = small_grad[:, : part * taps].reshape(owned, taps)
    bias_grad = small_grad[:, part * taps : part * (taps + 1)].reshape(owned)
    gain_grad = jnp.sum(small_grad[:, part * (taps + 1) : part * (taps + 1) + owned], axis=0)
    return encoded, frame_grad, gain_grad, bias_grad, kernel_grad, expand_grad, project_grad


def body(*arrays):
    fast = lax.axis_size("dp") == 4 and lax.axis_size("shard") == 8
    return (fast_body if fast else generic_body)(*arrays)


def solution(mesh):
    return jax.shard_map(
        body,
        mesh=mesh,
        in_specs=(
            P(("dp", "shard"), None, None),
            P(("dp", "shard"), None, None),
            P(("dp", "shard")),
            P(("dp", "shard")),
            P("shard"),
            P("shard"),
            P("shard", None),
            P("shard", None),
            P("shard", None),
        ),
        out_specs=(
            P(("dp", "shard"), None, None),
            P(("dp", "shard"), None, None),
            P("shard"),
            P("shard"),
            P("shard", None),
            P("shard", None),
            P("shard", None),
        ),
        check_vma=False,
    )
```

```python
import functools

import jax
import jax.numpy as jnp
from jax import lax
from jax.experimental import pallas as pl
from jax.experimental.pallas import tpu as pltpu
from jax.sharding import PartitionSpec as P

EPS = 1e-05
F32 = jnp.float32
BF16 = jnp.bfloat16
LANES = 128
MARGIN = 16
NT = (((1,), (1,)), ((), ()))
TN = (((0,), (0,)), ((), ()))
VMEM_PACK = 60
VMEM_CHUNK = 60
VMEM_ENCODE = 60
VMEM_FRAME = 60
VMEM_HOP = 60
VMEM_UNPACK = 28
LIGHT = pl.CostEstimate(flops=1, bytes_accessed=1, transcendentals=0)


def route(dims, refs, meta, s, base):
    count, length, taps = dims
    source = lax.axis_index("dp") ^ s
    copies = []
    for q in range(count):
        chosen = base + length * meta[source, count + (lax.axis_index("dp") ^ q)]
        copies.append(
            pltpu.make_async_copy(
                refs["sw"].at[pl.ds(pl.multiple_of(chosen, length), length)],
                refs["pieces"][q].at[pl.ds(pl.multiple_of(s * length, length), length)],
                refs["route_sems"].at[s, q],
            )
        )
    return copies


def one_source(dims, refs, meta, s, base, ready):
    count, length, taps = dims
    rows = count * length
    we, ab, pad, gpad, slope = (refs[n] for n in ("we", "ab", "pad", "gpad", "slope"))
    normed, sw, ge, taps_ref, small = (refs[n] for n in ("normed", "sw", "ge", "taps", "small"))
    width, wide = we.shape
    channels = wide // 2
    tiles = channels // LANES
    own = pl.ds(base, rows)
    step = 64
    ready("we")
    gain = refs["gain"][...]
    ready("x")

    @pl.loop(0, rows // step)
    def _(index):
        at = pl.ds(pl.multiple_of(base + index * step, step), step)
        x = refs["x"][at, :].astype(F32)
        centred = x - jnp.mean(x, axis=1, keepdims=True)
        variance = jnp.mean(centred * centred, axis=1, keepdims=True)
        normed[at, :] = (centred * lax.rsqrt(variance + EPS) * gain).astype(BF16)

    expanded = jnp.dot(normed[own, :], we[...], preferred_element_type=F32)
    for tile in range(2 * tiles):
        ab[tile] = expanded[:, tile * LANES : (tile + 1) * LANES]

    first = (taps - 1) // 2
    positions = lax.broadcasted_iota(jnp.int32, (length, LANES), 0)
    source = lax.axis_index("dp") ^ s

    @pl.loop(0, count)
    def _(u):
        at = pl.ds(pl.multiple_of(u * length, length), length)
        out = pl.ds(pl.multiple_of(base + u * length, length), length)
        live = positions < meta[source, u]
        for tile in range(tiles):
            lanes = pl.ds(tile * LANES, LANES)
            gate = jax.nn.sigmoid(ab[tiles + tile, at, :])
            glu = jnp.where(live, ab[tile, at, :] * gate, 0.0).astype(BF16).astype(F32)
            pad[u, tile, MARGIN : MARGIN + length, :] = glu
            ab[tiles + tile, at, :] = gate
            conv = jnp.broadcast_to(taps_ref[taps : taps + 1, lanes], (length, LANES))
            for t in range(taps):
                conv += taps_ref[t : t + 1, lanes] * pad[u, tile, pl.ds(MARGIN - first + t, length), :]
            sig = jax.nn.sigmoid(conv)
            sw[out, lanes] = jnp.where(live, conv * sig, 0.0).astype(BF16)
            slope[u, tile] = jnp.where(live, sig * (1.0 + conv * (1.0 - sig)), 0.0)

    for copy in route(dims, refs, meta, s, base):
        copy.start()

    ready("g")
    ready("wp")
    grad_swish = lax.dot_general(
        refs["g"][own, :], refs["wp"][...], NT, preferred_element_type=F32
    )
    for u in range(count):
        for tile in range(tiles):
            gpad[u, tile, MARGIN : MARGIN + length, :] = (
                grad_swish[u * length : (u + 1) * length, tile * LANES : (tile + 1) * LANES]
                * slope[u, tile]
            )

    def fold(value):
        return jnp.sum(value.reshape(length // 8, 8, LANES), axis=0)

    @pl.loop(0, count)
    def _(u):
        at = pl.ds(pl.multiple_of(u * length, length), length)
        out = pl.ds(pl.multiple_of(base + u * length, length), length)
        live = positions < meta[source, u]
        for tile in range(tiles):
            lanes = pl.ds(tile * LANES, LANES)
            grad_conv = gpad[u, tile, MARGIN : MARGIN + length, :]
            grad_glu = jnp.zeros((length, LANES), F32)
            for t in range(taps):
                small[tile, t] += fold(
                    pad[u, tile, pl.ds(MARGIN - first + t, length), :] * grad_conv
                )
                grad_glu += (
                    taps_ref[t : t + 1, lanes] * gpad[u, tile, pl.ds(MARGIN + first - t, length), :]
                )
            small[tile, taps] += fold(grad_conv)
            grad_glu = jnp.where(live, grad_glu, 0.0)
            gate = ab[tiles + tile, at, :]
            through = grad_glu * gate
            ge[out, lanes] = through.astype(BF16)
            ge[out, pl.ds(channels + tile * LANES, LANES)] = (
                through * ab[tile, at, :] * (1.0 - gate)
            ).astype(BF16)

    span = 512
    for start in range(0, width, span):
        cols = pl.ds(start, span)
        refs["gn"][own, cols] = lax.dot_general(
            ge[own, :], we[cols, :], NT, preferred_element_type=F32
        ).astype(BF16)


def clear_margins(*padded):
    for ref in padded:
        count, tiles, height, lanes = ref.shape
        zeros = jnp.zeros((MARGIN, lanes), F32)
        for u in range(count):
            for tile in range(tiles):
                ref[u, tile, :MARGIN, :] = zeros
                ref[u, tile, height - MARGIN :, :] = zeros


def source_scratch(count, length, channels):
    tiles = channels // LANES
    padded = pltpu.VMEM((count, tiles, length + 2 * MARGIN, LANES), F32)
    return [
        pltpu.VMEM((2 * tiles, count * length, LANES), F32),
        padded,
        padded,
        pltpu.VMEM((count, tiles, length, LANES), F32),
    ]


def weight_copies(blocks, owned, part, we, wp, small, sems):
    me = lax.axis_index("shard")
    width, wide = we.shape
    halves = width // wide
    move = pltpu.make_async_copy
    first, second = [], []
    for b, block in enumerate(blocks):
        offset = 2 * (b % (len(blocks) // 2)) + b // (len(blocks) // 2)
        owner = me ^ offset
        first.append(
            move(block.at[pl.ds(owned + halves * part, 16)], small.at[owner], sems.at[b, 0])
        )
        rows = pl.ds(pl.multiple_of(owner * owned, owned), owned)
        first.append(move(block.at[pl.ds(0, owned)], we.at[rows], sems.at[b, 1]))
        rows = pl.ds(pl.multiple_of(owner * part, part), part)
        for h in range(halves):
            second.append(
                move(
                    block.at[pl.ds(owned + h * part, part)],
                    wp.at[rows, pl.ds(h * wide, wide)],
                    sems.at[b, 2 + h],
                )
            )
    return first, second


def fill_tables(small, owned, part, taps_ref, gain_ref):
    rows = [small[j].astype(F32) for j in range(small.shape[0])]
    taps_ref[:16] = jnp.concatenate([r[:, :part] for r in rows], axis=1)
    taps_ref[16:] = jnp.concatenate([r[:, LANES : LANES + part] for r in rows], axis=1)
    gain_ref[...] = jnp.concatenate([r[:1, 2 * LANES : 2 * LANES + owned] for r in rows], axis=1)


def weight_scratch(owners, owned, width, wide, taps):
    return [
        pltpu.VMEM((width, wide), BF16),
        pltpu.VMEM((wide // 2, width), BF16),
        pltpu.VMEM((owners, 16, wide), BF16),
        pltpu.VMEM((taps + 1, wide // 2), F32),
        pltpu.SemaphoreType.DMA((owners, 2 + width // wide)),
    ]


def near_kernel(dims, n, owned, meta, *refs):
    count, length, taps = dims
    rows = count * length
    x_hbm, g_hbm, refs = refs[:n], refs[n : 2 * n], refs[2 * n :]
    outs = refs[-24 - n - count : -19]
    blocks = refs[: -24 - n - count]
    normed_hbm, sw_hbm, ge_hbm = outs[:3]
    gn_hbm, small, gain_ref, pieces = outs[3 : 3 + n], outs[3 + n], outs[4 + n], outs[5 + n :]
    x, normed, g, sw, ge, gn, ab, pad, gpad, slope = refs[-19:-9]
    we, wp, shares, taps_ref, weight_sems = refs[-9:-4]
    in_sems, out_sems, route_sems, _ = refs[-4:]
    part = owned * (we.shape[1] // 2) // we.shape[0]
    move = pltpu.make_async_copy

    def place(s):
        return pl.ds(s * rows, rows)

    incoming = {}
    for s in range(n):
        incoming["x", s] = move(x_hbm[s].at[pl.ds(0, rows)], x.at[place(s)], in_sems.at[s, 0])
        incoming["g", s] = move(
            g_hbm[s].at[pl.ds(g_hbm[s].shape[0] - rows, rows)], g.at[place(s)], in_sems.at[s, 1]
        )
    weights = weight_copies(blocks, owned, part, we, wp, shares, weight_sems)
    incoming["x", 0].start()
    for copy in weights[0]:
        copy.start()
    incoming["g", 0].start()
    for copy in weights[1]:
        copy.start()
    for s in range(1, n):
        incoming["x", s].start()
        incoming["g", s].start()
    clear_margins(pad, gpad)
    small[...] = jnp.zeros_like(small)
    views = dict(
        x=x, normed=normed, g=g, we=we, wp=wp, sw=sw, ge=ge, gn=gn, ab=ab, pad=pad, gpad=gpad,
        slope=slope, taps=taps_ref, gain=gain_ref, small=small, pieces=pieces, route_sems=route_sems,
    )

    @pl.loop(0, n)
    def _(s):
        def ready(what):
            if what in ("we", "wp"):
                @pl.when(s == 0)
                def _():
                    for copy in weights[what == "wp"]:
                        copy.wait()
                    if what == "we":
                        fill_tables(shares, owned, part, taps_ref, gain_ref)
            else:
                for at in range(n):
                    @pl.when(s == at)
                    def _():
                        incoming[what, at].wait()

        base = pl.multiple_of(s * rows, rows)
        one_source(dims, views, meta, s, base, ready)
        own = pl.ds(base, rows)
        for i, (source, target) in enumerate(((normed, normed_hbm), (sw, sw_hbm), (ge, ge_hbm))):
            move(source.at[own], target.at[own], out_sems.at[s, i]).start()
        for at in range(n):
            @pl.when(s == at)
            def _():
                move(gn.at[place(at)], gn_hbm[at], out_sems.at[at, 3]).start()

    for s in range(n):
        for i, (source, target) in enumerate(((normed, normed_hbm), (sw, sw_hbm), (ge, ge_hbm))):
            move(source.at[place(s)], target.at[place(s)], out_sems.at[s, i]).wait()
        move(gn.at[place(s)], gn_hbm[s], out_sems.at[s, 3]).wait()
        for copy in route(dims, views, meta, s, s * rows):
            copy.wait()


def near_call(ints, xs, gs, blocks, owned, dims):
    count, length, taps = dims
    n = len(xs)
    rows, width = count * length, xs[0].shape[1]
    wide = blocks[0].shape[1]
    channels = wide // 2
    owners = len(blocks)
    anywhere = pl.BlockSpec(memory_space=pl.ANY)
    return pl.pallas_call(
        functools.partial(near_kernel, dims, n, owned),
        out_shape=(
            jax.ShapeDtypeStruct((n * rows, width), BF16),
            jax.ShapeDtypeStruct((n * rows, channels), BF16),
            jax.ShapeDtypeStruct((n * rows, wide), BF16),
        )
        + (jax.ShapeDtypeStruct((rows, width), BF16),) * n
        + (
            jax.ShapeDtypeStruct((channels // LANES, taps + 1, 8, LANES), F32),
            jax.ShapeDtypeStruct((1, width), F32),
        )
        + (jax.ShapeDtypeStruct((rows, channels), BF16),) * count,
        in_specs=[in_smem()] + [anywhere] * (2 * n + owners),
        out_specs=(anywhere,) * (3 + n) + (in_vmem(), in_vmem()) + (anywhere,) * count,
        scratch_shapes=[
            pltpu.VMEM((n * rows, width), BF16),
            pltpu.VMEM((n * rows, width), BF16),
            pltpu.VMEM((n * rows, width), BF16),
            pltpu.VMEM((n * rows, channels), BF16),
            pltpu.VMEM((n * rows, wide), BF16),
            pltpu.VMEM((n * rows, width), BF16),
        ]
        + source_scratch(count, length, channels)
        + weight_scratch(owners, owned, width, wide, taps)
        + [
            pltpu.SemaphoreType.DMA((n, 2)),
            pltpu.SemaphoreType.DMA((n, 4)),
            pltpu.SemaphoreType.DMA((n, count)),
            pltpu.SemaphoreType.DMA,
        ],
        compiler_params=vmem_params(VMEM_CHUNK),
        cost_estimate=LIGHT,
        name="near_sources",
    )(ints, *xs, *gs, *blocks)


def far_kernel(dims, n, owned, meta, *refs):
    count, length, taps = dims
    rows = count * length
    core = lax.axis_index("shard") % 2
    x_hbm, normed_hbm, sw_hbm, ge_hbm = refs[:4]
    g_hbm, near_small = refs[4 : 5 + n], refs[5 + n]
    blocks, outs, refs = refs[6 + n : -25 - 2 * count], refs[-25 - count : -22], refs[-22:]
    gn_hbm, keep_hbm, give_hbm, pieces = outs[0], outs[1], outs[2], outs[3:]
    x, normed, g, sw, ge, gn, ab, pad, gpad, slope = refs[:10]
    we, wp, shares, taps_ref, weight_sems = refs[10:15]
    gain_ref, small, block, in_sems, out_sems, route_sems, _ = refs[15:]
    width, wide = we.shape
    channels = wide // 2
    tiles = channels // LANES
    chips = width // owned // 2
    halves = width // wide
    part = channels // (2 * chips)
    move = pltpu.make_async_copy
    base = n * rows
    near, last = pl.ds(0, base), pl.ds(base, rows)
    tail = [pl.ds(ref.shape[0] - rows, rows) for ref in g_hbm]
    incoming = dict(
        x=[move(x_hbm.at[pl.ds(0, rows)], x.at[last], in_sems.at[0])],
        g=[move(g_hbm[n].at[tail[n]], g.at[last], in_sems.at[2])],
    )
    incoming["we"], incoming["wp"] = weight_copies(
        blocks, owned, part, we, wp, shares, weight_sems
    )
    later = [
        move(normed_hbm, normed.at[near], in_sems.at[4]),
        move(sw_hbm, sw.at[near], in_sems.at[5]),
        move(ge_hbm, ge.at[near], in_sems.at[6]),
    ]
    later += [
        move(g_hbm[s].at[tail[s]], g.at[pl.ds(s * rows, rows)], in_sems.at[7 + s])
        for s in range(n)
    ]
    for copy in incoming["x"] + incoming["we"] + incoming["g"] + incoming["wp"] + later:
        copy.start()

    def ready(what):
        for copy in incoming[what]:
            copy.wait()
        if what == "we":
            fill_tables(shares, owned, part, taps_ref, gain_ref)

    clear_margins(pad, gpad)
    small[...] = near_small[...]
    views = dict(
        x=x, normed=normed, g=g, we=we, wp=wp, sw=sw, ge=ge, gn=gn, ab=ab, pad=pad, gpad=gpad,
        slope=slope, taps=taps_ref, gain=gain_ref, small=small, pieces=pieces, route_sems=route_sems,
    )
    one_source(dims, views, meta, n, base, ready)
    gn_out = move(gn.at[last], gn_hbm, out_sems.at[2])
    gn_out.start()
    routed = route(dims, views, meta, n, base)
    for copy in later:
        copy.wait()

    sums = jnp.sum(small[...], axis=2)
    sums = jnp.concatenate([sums[tile] for tile in range(tiles)], axis=1)
    span = 2 * owned
    bottom = owned + halves * part
    for chip in range(chips):
        total = lax.dot_general(
            normed[:, chip * span : (chip + 1) * span], ge[...], TN, preferred_element_type=F32
        ).astype(BF16)
        for which in range(2):
            block[which, chip, :owned] = total[which * owned : (which + 1) * owned]
    for h in range(halves):
        total = lax.dot_general(
            sw[...], g[:, h * wide : (h + 1) * wide], TN, preferred_element_type=F32
        ).astype(BF16)
        for owner in range(2 * chips):
            block[owner % 2, owner // 2, owned + h * part : owned + (h + 1) * part] = total[
                owner * part : (owner + 1) * part
            ]
    fill = jnp.zeros((16, LANES - part), F32)
    blank = jnp.zeros((16, wide - 2 * LANES), F32)
    for owner in range(2 * chips):
        table = sums[:, owner * part : (owner + 1) * part]
        line = jnp.concatenate([table[:16], fill, table[16:], fill, blank], axis=1)
        block[owner % 2, owner // 2, bottom:] = line.astype(BF16)
    outward = [
        move(block.at[1 - core], give_hbm, out_sems.at[0]),
        move(block.at[core], keep_hbm, out_sems.at[1]),
    ]
    for copy in outward:
        copy.start()
    for copy in outward + routed + [gn_out]:
        copy.wait()


def far_call(ints, x, near, gs, blocks, before, owned, dims):
    count, length, taps = dims
    n = len(gs) - 1
    rows = count * length
    width, wide = x.shape[1], blocks[0].shape[1]
    channels = wide // 2
    tiles = channels // LANES
    owners = len(blocks)
    chips = owners // 2
    halves = width // wide
    height = owned + halves * (channels // owners) + 16
    anywhere = pl.BlockSpec(memory_space=pl.ANY)
    normed, sw, ge, small = near
    every = (n + 1) * rows
    return pl.pallas_call(
        functools.partial(far_kernel, dims, n, owned),
        out_shape=(jax.ShapeDtypeStruct((rows, width), BF16),)
        + (jax.ShapeDtypeStruct((chips, height, wide), BF16),) * 2
        + (jax.ShapeDtypeStruct(before[0].shape, BF16),) * count,
        in_specs=[in_smem()] + [anywhere] * (5 + n) + [in_vmem()] + [anywhere] * (owners + count),
        out_specs=(anywhere,) * (3 + count),
        input_output_aliases={7 + n + owners + m: 3 + m for m in range(count)},
        scratch_shapes=[
            pltpu.VMEM((every, width), BF16),
            pltpu.VMEM((every, width), BF16),
            pltpu.VMEM((every, width), BF16),
            pltpu.VMEM((every, channels), BF16),
            pltpu.VMEM((every, wide), BF16),
            pltpu.VMEM((every, width), BF16),
        ]
        + source_scratch(count, length, channels)
        + weight_scratch(owners, owned, width, wide, taps)
        + [
            pltpu.VMEM((1, width), F32),
            pltpu.VMEM((tiles, taps + 1, 8, LANES), F32),
            pltpu.VMEM((2, chips, height, wide), BF16),
            pltpu.SemaphoreType.DMA((7 + n,)),
            pltpu.SemaphoreType.DMA((3,)),
            pltpu.SemaphoreType.DMA((n + 1, count)),
            pltpu.SemaphoreType.DMA,
        ],
        compiler_params=vmem_params(VMEM_CHUNK),
        cost_estimate=LIGHT,
        name="far_source",
    )(ints, x, normed, sw, ge, *gs, small, *blocks, *before)


def vmem_params(mib):
    return pltpu.CompilerParams(vmem_limit_bytes=mib * 1024 * 1024)


def in_vmem():
    return pl.BlockSpec(memory_space=pltpu.VMEM)


def in_smem():
    return pl.BlockSpec(memory_space=pltpu.SMEM)


def owned_column(channel, index, owned, part):
    return (channel // part) * owned + index * part + channel % part


def pack_kernel(expand_hbm, project_hbm, kernel_ref, bias_ref, gain_ref, x_hbm, g_hbm, *refs):
    pack_ref, both_hbm, copies_hbm, both, expand_ref, whole, sems = refs
    rows_in = x_hbm.shape[0]
    inward = [
        pltpu.make_async_copy(x_hbm, both.at[pl.ds(0, rows_in)], sems.at[2]),
        pltpu.make_async_copy(g_hbm, both.at[pl.ds(rows_in, rows_in)], sems.at[3]),
    ]
    owned, width = project_hbm.shape
    wide = pack_ref.shape[1]
    channels = wide // 2
    part = owned * channels // width
    index = lax.axis_index("dp")
    rows = pl.ds(pl.multiple_of(index * part, part), part)
    chips = copies_hbm.shape[0]
    copies = [
        pltpu.make_async_copy(expand_hbm, expand_ref, sems.at[0]),
        pltpu.make_async_copy(project_hbm, whole, sems.at[1]),
    ]
    for copy in inward + copies:
        copy.start()
    row = lax.broadcasted_iota(jnp.int32, (width, channels), 0)
    col = lax.broadcasted_iota(jnp.int32, (1, channels), 1)
    pick = jnp.where(row == owned_column(col, index, owned, part), 1.0, 0.0).astype(BF16)
    mine = lax.broadcasted_iota(jnp.int32, (owned, LANES), 1) + index * part
    mine = jnp.where(lax.broadcasted_iota(jnp.int32, (owned, LANES), 0) == mine, 1.0, 0.0)
    mine = mine.astype(BF16)
    table = jnp.concatenate(
        [
            jnp.dot(kernel_ref[...], mine, preferred_element_type=F32),
            jnp.dot(bias_ref[...].reshape(1, owned), mine, preferred_element_type=F32),
        ],
        axis=0,
    )
    base = owned + width // wide * part
    gain = jnp.broadcast_to(gain_ref[...].reshape(1, owned).astype(F32), (16, owned))
    blank = jnp.zeros((16, wide - 2 * LANES - owned), F32)
    pack_ref[base:, :] = jnp.concatenate(
        [table[:16], table[16:], gain, blank], axis=1
    ).astype(BF16)
    for copy in inward:
        copy.wait()
    outward = [pltpu.make_async_copy(both, both_hbm, sems.at[4])]
    outward[0].start()
    for copy in copies:
        copy.wait()
    for i in range(chips):
        outward.append(pltpu.make_async_copy(whole, copies_hbm.at[i], sems.at[5 + i]))
        outward[-1].start()
    block = whole[rows, :]
    for h in range(2):
        pack_ref[:owned, h * channels : (h + 1) * channels] = jnp.dot(
            expand_ref[:, h * width : (h + 1) * width], pick, preferred_element_type=F32
        ).astype(BF16)
    for h in range(width // wide):
        pack_ref[owned + h * part : owned + (h + 1) * part, :] = block[:, h * wide : (h + 1) * wide]
    for copy in outward:
        copy.wait()


def pack_call(expand_weight, project_weight, kernel, bias, gain, x, g, part, wide):
    owned, width = project_weight.shape
    height = owned + width // wide * part + 16
    chips = width // owned // 2
    rows = x.shape[0]
    anywhere = pl.BlockSpec(memory_space=pl.ANY)
    return pl.pallas_call(
        pack_kernel,
        out_shape=(
            jax.ShapeDtypeStruct((height, wide), BF16),
            jax.ShapeDtypeStruct((2 * rows, width), BF16),
            jax.ShapeDtypeStruct((chips, owned, width), BF16),
        ),
        in_specs=[anywhere] * 2 + [in_vmem()] * 3 + [anywhere] * 2,
        out_specs=(in_vmem(), anywhere, anywhere),
        scratch_shapes=[
            pltpu.VMEM((2 * rows, width), BF16),
            pltpu.VMEM(expand_weight.shape, BF16),
            pltpu.VMEM((owned, width), BF16),
            pltpu.SemaphoreType.DMA((5 + chips,)),
        ],
        compiler_params=vmem_params(VMEM_PACK),
        cost_estimate=LIGHT,
        name="pack",
    )(expand_weight, project_weight, kernel.T, bias, gain, x, g)


def encode_kernel(dims, meta, *refs):
    n, length, owned = dims
    frames = refs[:n]
    pieces, blocks, refs = refs[n : 2 * n], refs[2 * n : 2 * n + 2], refs[2 * n + 2 :]
    out_ref, cat, weight, residual, sems = refs
    shard = lax.axis_index("shard")
    channels = pieces[0].shape[1]
    part = owned // n
    me = lax.axis_index("dp")

    def rows(at, size):
        return pl.ds(pl.multiple_of(at * size, size), size)

    moves = []
    for which, block in enumerate(blocks):
        for chip in range(block.shape[0]):
            owner = 2 * chip + ((shard % 2) ^ which)
            for i in range(n):
                start = pl.multiple_of(i * channels + owner * part, part)
                moves.append((block.at[chip, pl.ds(i * part, part)], weight.at[pl.ds(start, part)]))
    for k in range(n):
        moves.append(
            (
                frames[k].at[rows(meta[me ^ k, n + me], length)],
                residual.at[rows(me ^ k, length)],
            )
        )
    for m in range(n):
        lanes = pl.ds(pl.multiple_of((me ^ m) * channels, channels), channels)
        for k in range(n):
            source = pieces[m].at[pl.ds(k * length, length)]
            moves.append((source, cat.at[rows(me ^ m ^ k, length), lanes]))
    copies = [
        pltpu.make_async_copy(source, target, sems.at[i])
        for i, (source, target) in enumerate(moves)
    ]
    for copy in copies:
        copy.start()
    for copy in copies:
        copy.wait()
    span = 512
    for start in range(0, cat.shape[1], span):
        cols = slice(start, start + span)
        term = jnp.dot(cat[...], weight[:, cols], preferred_element_type=F32)
        out_ref[:, cols] = (residual[:, cols].astype(F32) + term).astype(BF16)


def encode_call(ints, pieces, frames, blocks, length):
    n = len(frames)
    owned, width = blocks[0].shape[1:]
    anywhere = pl.BlockSpec(memory_space=pl.ANY)
    return pl.pallas_call(
        functools.partial(encode_kernel, (n, length, owned)),
        out_shape=jax.ShapeDtypeStruct((n * length, width), BF16),
        in_specs=[in_smem()] + [anywhere] * (2 * n + len(blocks)),
        out_specs=in_vmem(),
        scratch_shapes=[
            pltpu.VMEM((n * length, width), BF16),
            pltpu.VMEM((width, width), BF16),
            pltpu.VMEM((n * length, width), BF16),
            pltpu.SemaphoreType.DMA((width // owned * n + n + n * n,)),
        ],
        compiler_params=vmem_params(VMEM_ENCODE),
        cost_estimate=LIGHT,
        name="encode",
    )(ints, *frames, *pieces, *blocks)


def frame_grad_kernel(n, x_ref, g_ref, gain_ref, *refs):
    out_ref = refs[n]
    x = x_ref[...].astype(F32)
    centred = x - jnp.mean(x, axis=1, keepdims=True)
    inverse = lax.rsqrt(jnp.mean(centred * centred, axis=1, keepdims=True) + EPS)
    standard = centred * inverse
    grad = sum(ref[...].astype(F32) for ref in refs[:n]) * gain_ref[...]
    grad_in = inverse * (
        grad
        - jnp.mean(grad, axis=1, keepdims=True)
        - standard * jnp.mean(grad * standard, axis=1, keepdims=True)
    )
    out_ref[...] = (g_ref[...].astype(F32) + grad_in).astype(BF16)


def frame_grad_call(x, g, gain, returned):
    count, length, width = x.shape
    rows = count * length
    step = 64
    block = pl.BlockSpec((step, width), lambda s: (s, 0))
    out = pl.pallas_call(
        functools.partial(frame_grad_kernel, len(returned)),
        out_shape=jax.ShapeDtypeStruct((rows, width), BF16),
        grid=(rows // step,),
        in_specs=[block, block, pl.BlockSpec((1, width), lambda s: (0, 0))]
        + [block] * len(returned),
        out_specs=block,
        compiler_params=vmem_params(VMEM_FRAME),
        cost_estimate=LIGHT,
        name="frame_grad",
    )(x.reshape(rows, width), g.reshape(rows, width), gain, *returned)
    return out.reshape(count, length, width)


def unpack_kernel(dims, *refs):
    n, owned, part = dims
    blocks, refs = (refs[:n], refs[n : 2 * n]), refs[2 * n :]
    weight_ref, gain_ref, expand_ref, project_ref, gain_out, cat, grads, project, sems = refs
    channels = blocks[0][0].shape[1]
    wide = 2 * channels
    width = cat.shape[2]
    halves = width // wide
    me = lax.axis_index("dp")
    for k in range(n):
        lanes = pl.ds(pl.multiple_of((me ^ k) * channels, channels), channels)
        rows = pl.ds(pl.multiple_of((me ^ k) * part, part), part)
        for half in range(2):
            block = blocks[half][k]
            cat[half, :, lanes] = block[:owned]
            for h in range(halves):
                start = h * wide + half * channels
                project[rows, start : start + channels] = block[
                    owned + h * part : owned + (h + 1) * part
                ].astype(F32)
    copies = [pltpu.make_async_copy(project, project_ref, sems.at[2, 0])]
    copies[0].start()
    along = jnp.zeros((owned, 1), F32)
    span = 512
    for start in range(0, width, span):
        row = lax.broadcasted_iota(jnp.int32, (width, span), 0)
        col = lax.broadcasted_iota(jnp.int32, (1, span), 1) + start
        place = col % owned // part * channels + col // owned * part + col % part
        spread = jnp.where(row == place, 1.0, 0.0).astype(BF16)
        for half in range(2):
            cols = pl.ds(half * width + start, span)
            grad = jnp.dot(cat[half], spread, preferred_element_type=F32)
            grads[:, cols] = grad
            copy = pltpu.make_async_copy(
                grads.at[:, cols], expand_ref.at[:, cols], sems.at[half, start // span]
            )
            copy.start()
            copies.append(copy)
            along += jnp.sum(grad * weight_ref[:, cols].astype(F32), axis=1, keepdims=True)
    row = jnp.transpose(jnp.broadcast_to(along, (owned, LANES)))[:1]
    gain_out[...] = row / gain_ref[...].astype(F32)
    for copy in copies:
        copy.wait()


def unpack_call(low, high, weight, gain, owned, part, width):
    anywhere = pl.BlockSpec(memory_space=pl.ANY)
    return pl.pallas_call(
        functools.partial(unpack_kernel, (len(low), owned, part)),
        out_shape=(
            jax.ShapeDtypeStruct((owned, 2 * width), F32),
            jax.ShapeDtypeStruct((owned, width), F32),
            jax.ShapeDtypeStruct((1, owned), F32),
        ),
        in_specs=[in_vmem()] * (2 * len(low) + 2),
        out_specs=(anywhere, anywhere, in_vmem()),
        scratch_shapes=[
            pltpu.VMEM((2, owned, width), BF16),
            pltpu.VMEM((owned, 2 * width), F32),
            pltpu.VMEM((owned, width), F32),
            pltpu.SemaphoreType.DMA((3, width // 512)),
        ],
        compiler_params=vmem_params(VMEM_UNPACK),
        cost_estimate=LIGHT,
        name="unpack",
    )(*low, *high, weight, gain)


def tie(value, *after):
    return lax.optimization_barrier((value,) + after)[0]


def gather_owners(x):
    blocks = [x] + [swap(x, "shard", 8, 2 * m) for m in (1, 2, 3)]
    return blocks + [swap(block, "shard", 8, 1) for block in blocks]


def add_cores_kernel(keep_hbm, got_hbm, out_hbm, keep, got, sems):
    n = keep.shape[0]
    move = pltpu.make_async_copy
    inward = [
        (move(keep_hbm.at[i], keep.at[i], sems.at[i, 0]), move(got_hbm.at[i], got.at[i], sems.at[i, 1]))
        for i in range(n)
    ]
    outward = [move(keep.at[i], out_hbm.at[i], sems.at[i, 2]) for i in range(n)]
    for i in range(n):
        for copy in inward[i]:
            copy.start()
    for i in range(n):
        for copy in inward[i]:
            copy.wait()
        keep[i] = (keep[i].astype(F32) + got[i].astype(F32)).astype(BF16)
        outward[i].start()
    for copy in outward:
        copy.wait()


def add_cores(keep, got):
    anywhere = pl.BlockSpec(memory_space=pl.ANY)
    return pl.pallas_call(
        add_cores_kernel,
        out_shape=jax.ShapeDtypeStruct(keep.shape, BF16),
        in_specs=[anywhere] * 2,
        out_specs=anywhere,
        scratch_shapes=[
            pltpu.VMEM(keep.shape, BF16),
            pltpu.VMEM(keep.shape, BF16),
            pltpu.SemaphoreType.DMA((keep.shape[0], 3)),
        ],
        compiler_params=vmem_params(VMEM_HOP),
        cost_estimate=LIGHT,
        name="add_cores",
    )(keep, got)


def add_chips_kernel(come_ref, *refs):
    total = jnp.sum(come_ref[...].astype(F32), axis=0).astype(BF16)
    channels = refs[0].shape[1]
    for half, ref in enumerate(refs):
        ref[...] = total[:, half * channels : (half + 1) * channels]


def add_chips(come):
    rows, wide = come.shape[1:]
    return pl.pallas_call(
        add_chips_kernel,
        out_shape=(jax.ShapeDtypeStruct((rows, wide // 2), BF16),) * 2,
        in_specs=[in_vmem()],
        out_specs=(in_vmem(),) * 2,
        compiler_params=vmem_params(VMEM_HOP),
        cost_estimate=LIGHT,
        name="add_chips",
    )(come)


def fast_body(
    frames,
    cotangent,
    lengths,
    send_order,
    norm_gain,
    conv_bias,
    kernel,
    expand_weight,
    project_weight,
):
    n_dp, n_shard = lax.axis_size("dp"), lax.axis_size("shard")
    count, length, width = frames.shape
    owned, taps = kernel.shape
    part = owned // n_dp
    wide = 2 * n_shard * part
    rows = count * length
    dims = (count, length, taps)
    ints = jnp.concatenate([lengths, send_order])
    ints = lax.all_to_all(jnp.broadcast_to(ints, (n_dp, 2 * count)), "dp", 0, 0, tiled=True)
    x_own = frames.reshape(rows, width)
    g_own = cotangent.reshape(rows, width)
    pack, both, project = pack_call(
        expand_weight, project_weight, kernel, conv_bias, norm_gain, x_own, g_own, part, wide
    )
    pack, both, ints = lax.optimization_barrier((pack, both, ints))
    both_x = swap(both, "dp", 4, 1)
    both_y = swap(both, "dp", 4, 2)
    packs = [pack] + [swap(pack, "shard", 8, 2 * m) for m in (1, 2, 3)]
    *packs, both_x, both_y = lax.optimization_barrier((*packs, both_x, both_y))
    packs += [swap(block, "shard", 8, 1) for block in packs]
    x_all = [x_own, both_x, both_y, swap(both_x[:rows], "dp", 4, 2)]
    g_all = [g_own, both_x, both_y, swap(both_y[rows:], "dp", 4, 1)]
    line = [[2 * c + i for c in range(n_shard // 2)] for i in range(2)]
    project = tie(project, *packs[1:4])
    project = lax.all_to_all(project, "shard", 0, 0, axis_index_groups=line, tiled=True)

    near = near_call(ints, x_all[:3], g_all[:3], packs, owned, dims)
    returned = [near[3]] + [swap(near[3 + k], "dp", n_dp, k) for k in (1, 2)]
    gain = near[7]
    far = far_call(ints, x_all[3], near[:3] + near[6:7], g_all, packs, near[8:], owned, dims)

    keep, give = far[1:3]
    give, keep = lax.optimization_barrier((give, keep, project, *returned[1:3]))[:2]
    sums = add_cores(keep, swap(give, "shard", 8, 1))
    come = lax.all_to_all(sums, "shard", 0, 0, axis_index_groups=line, tiled=True)
    last, *pieces = lax.optimization_barrier((far[0], *far[3:], sums))[:-1]
    returned.append(swap(last, "dp", n_dp, 3))
    pieces = [pieces[0]] + [swap(pieces[m], "dp", n_dp, m) for m in (1, 2, 3)]
    project = [project, swap(project, "shard", 8, 1)]
    encoded = encode_call(ints, pieces, x_all, project, length)
    frame_grad = frame_grad_call(frames, tie(cotangent, sums), gain, returned)

    gathered = [
        [half] + [swap(half, "dp", 4, k) for k in (1, 2, 3)]
        for half in add_chips(tie(come, encoded, frame_grad))
    ]
    base = owned + width // wide * part
    table = jnp.stack([a[base:] for a in gathered[0]])
    table = jnp.take(table, lax.axis_index("dp") ^ jnp.arange(n_dp), axis=0).astype(F32)
    table = jnp.concatenate([table[:, :, :part], table[:, :, LANES : LANES + part]], axis=1)
    table = table.transpose(0, 2, 1).reshape(owned, taps + 1)
    expand_grad, project_grad, along = unpack_call(
        *gathered, expand_weight, norm_gain[None], owned, part, width
    )
    return (
        encoded.reshape(frames.shape),
        frame_grad,
        along.reshape(owned),
        table[:, taps],
        table[:, :taps],
        expand_grad,
        project_grad,
    )


def depthwise(signal, taps_table):
    taps = taps_table.shape[0]
    half = (taps - 1) // 2
    length = signal.shape[1]
    padded = jnp.pad(signal, ((0, 0), (half, half), (0, 0)))
    result = jnp.zeros_like(signal)
    for offset in range(taps):
        result = result + padded[:, offset : offset + length, :] * taps_table[offset]
    return result


def kernel_terms(signal, upstream, taps):
    half = (taps - 1) // 2
    length = signal.shape[1]
    padded = jnp.pad(signal, ((0, 0), (half, half), (0, 0)))
    rows = []
    for offset in range(taps):
        rows.append(jnp.sum(padded[:, offset : offset + length, :] * upstream, axis=(0, 1)))
    return jnp.stack(rows, axis=0)


def chunk_compute(x, g, live, gain, taps, bias, expand_slice, project_slice):
    count, length, width = x.shape
    rows = count * length
    channels = taps.shape[1]
    inputs = x.reshape(rows, width).astype(F32)
    live_rows = live.reshape(rows, 1)
    centred = inputs - jnp.mean(inputs, axis=1, keepdims=True)
    variance = jnp.mean(centred * centred, axis=1, keepdims=True)
    standard = centred * lax.rsqrt(variance + EPS)
    normed = (standard * gain).astype(BF16)
    expanded = jnp.dot(normed, expand_slice, preferred_element_type=F32)
    value = expanded[:, :channels]
    gate = jax.nn.sigmoid(expanded[:, channels:])
    glu = (value * gate * live_rows).astype(BF16).astype(F32).reshape(count, length, channels)
    conv = depthwise(glu, taps).reshape(rows, channels) + bias
    conv_sig = jax.nn.sigmoid(conv)
    swished = (conv * conv_sig).astype(BF16)
    masked = (g.reshape(rows, width).astype(F32) * live_rows).astype(BF16)
    grad_swish = lax.dot_general(
        masked, project_slice, (((1,), (1,)), ((), ())), preferred_element_type=F32
    )
    grad_conv = grad_swish * conv_sig * (1.0 + conv * (1.0 - conv_sig))
    bias_part = jnp.sum(grad_conv, axis=0)
    volume = grad_conv.reshape(count, length, channels)
    kernel_part = kernel_terms(glu, volume, taps.shape[0])
    grad_glu = depthwise(volume, taps[::-1]).reshape(rows, channels) * live_rows
    grad_expanded = jnp.concatenate(
        [grad_glu * gate, grad_glu * value * gate * (1.0 - gate)], axis=1
    ).astype(BF16)
    grad_normed = lax.dot_general(
        grad_expanded, expand_slice, (((1,), (1,)), ((), ())), preferred_element_type=F32
    )
    gain_part = jnp.sum(grad_normed * standard, axis=0)
    return normed, masked, swished, grad_expanded, grad_normed.astype(BF16), (
        gain_part,
        bias_part,
        kernel_part,
    )


def swap(x, axis, size, k):
    return lax.ppermute(x, axis, [(p, p ^ k) for p in range(size)])


def gather_dp(x, n_dp):
    if n_dp == 4:
        half = x.shape[0] // 2
        along_x = swap(x, "dp", 4, 1)
        along_y = swap(x, "dp", 4, 2)
        far = jnp.concatenate(
            [swap(along_x[:half], "dp", 4, 2), swap(along_y[half:], "dp", 4, 1)], axis=0
        )
        return [x, along_x, along_y, far]
    return [x] + [swap(x, "dp", n_dp, k) for k in range(1, n_dp)]


def gather_shard(x, n_shard):
    if n_shard == 8:
        me = lax.axis_index("shard")
        chip, core = me // 2, me % 2
        blocks = [x] + [
            lax.ppermute(x, "shard", [(p, (p + 2 * k) % 8) for p in range(8)]) for k in (1, 2, 3)
        ]
        mine = jnp.stack(blocks)
        mine = jnp.take(mine, (chip - jnp.arange(4)) % 4, axis=0)
        other = swap(mine, "shard", 8, 1)
        pair = jnp.where(core == 0, jnp.stack([mine, other], 1), jnp.stack([other, mine], 1))
        return pair.reshape((8,) + x.shape)
    return lax.all_gather(x, "shard", axis=0)


def reduce_shard(x, n_shard):
    x = x.astype(BF16)
    if n_shard == 8:
        me = lax.axis_index("shard")
        chip, core = me // 2, me % 2
        cube = x.reshape((4, 2) + x.shape[1:])
        keep = jnp.take(cube, core, axis=1)
        give = jnp.take(cube, 1 - core, axis=1)
        both = (keep.astype(F32) + swap(give, "shard", 8, 1).astype(F32)).astype(BF16)
        total = jnp.take(both, chip, axis=0).astype(F32)
        for k in (1, 2, 3):
            piece = jnp.take(both, (chip + k) % 4, axis=0)
            total = total + lax.ppermute(
                piece, "shard", [(p, (p + 2 * k) % 8) for p in range(8)]
            ).astype(F32)
        return total
    return lax.psum_scatter(x, "shard", scatter_dimension=0, tiled=False).astype(F32)


def generic_body(
    frames,
    cotangent,
    lengths,
    send_order,
    norm_gain,
    conv_bias,
    kernel,
    expand_weight,
    project_weight,
):
    n_dp, n_shard = lax.axis_size("dp"), lax.axis_size("shard")
    count, length, width = frames.shape
    per_peer = count // n_dp
    owned, taps = kernel.shape
    part = owned // n_dp
    channels = n_shard * part
    me = lax.axis_index("dp")

    x_own = jnp.take(frames, send_order, axis=0)
    g_own = jnp.take(cotangent, send_order, axis=0)
    len_own = jnp.take(lengths, send_order, axis=0)

    expand_cols = lax.dynamic_index_in_dim(
        expand_weight.reshape(owned, 2, n_shard, n_dp, part), me, axis=3, keepdims=False
    ).reshape(owned, 2 * channels)
    project_rows = lax.dynamic_slice_in_dim(project_weight, me * part, part, axis=0)
    small = jnp.concatenate(
        [
            lax.dynamic_slice_in_dim(kernel, me * part, part, axis=0).reshape(-1),
            lax.dynamic_slice_in_dim(conv_bias, me * part, part, axis=0),
            norm_gain,
        ]
    )
    wide = 2 * channels
    small_rows = 16
    small = jnp.pad(small, (0, small_rows * wide - small.shape[0])).reshape(small_rows, wide)
    n_halves = width // wide
    pack = jnp.concatenate(
        [expand_cols] + [project_rows[:, h * wide : (h + 1) * wide] for h in range(n_halves)] + [small], axis=0
    )
    packs = gather_shard(pack, n_shard)
    expand_slice = packs[:, :owned].reshape(width, wide)
    project_slice = jnp.concatenate(
        [
            packs[:, owned + h * part : owned + (h + 1) * part].reshape(channels, wide)
            for h in range(n_halves)
        ],
        axis=1,
    )
    small_all = packs[:, owned + n_halves * part :].reshape(n_shard, -1).astype(F32)
    taps_table = small_all[:, : part * taps].reshape(channels, taps).T
    bias = small_all[:, part * taps : part * (taps + 1)].reshape(channels)
    gain = small_all[:, part * (taps + 1) : part * (taps + 1) + owned].reshape(width)
    project_full = gather_shard(project_weight, n_shard).reshape(n_shard, n_dp, part, width)

    x_all = gather_dp(x_own, n_dp)
    g_all = gather_dp(g_own, n_dp)
    len_all = [len_own] + [swap(len_own, "dp", n_dp, k) for k in range(1, n_dp)]

    normeds, maskeds, swisheds, grad_expandeds, returned = [], [], [], [], []
    sums = None
    positions = lax.broadcasted_iota(jnp.int32, (count, length), 1)
    for k in range(n_dp):
        live = (positions < len_all[k][:, None]).astype(F32)
        normed, masked, swished, grad_expanded, grad_normed, parts = chunk_compute(
            x_all[k], g_all[k], live, gain, taps_table, bias, expand_slice, project_slice
        )
        normeds.append(normed)
        maskeds.append(masked)
        swisheds.append(swished.reshape(n_dp, per_peer, length, channels))
        grad_expandeds.append(grad_expanded)
        returned.append(grad_normed if k == 0 else swap(grad_normed, "dp", n_dp, k))
        sums = parts if sums is None else tuple(a + b for a, b in zip(sums, parts))

    stack = jnp.stack(swisheds)
    total = None
    for m in range(n_dp):
        piece = lax.dynamic_index_in_dim(stack, me ^ m, axis=1, keepdims=False)
        if m:
            piece = swap(piece, "dp", n_dp, m)
        piece = jnp.stack([piece[k ^ m] for k in range(n_dp)])
        rows = lax.dynamic_index_in_dim(project_full, me ^ m, axis=1, keepdims=False)
        term = jnp.dot(
            piece.reshape(count * length, channels),
            rows.reshape(channels, width),
            preferred_element_type=F32,
        )
        total = term if total is None else total + term
    mine = jnp.stack(
        [
            lax.dynamic_slice_in_dim(x_all[k], me * per_peer, per_peer, axis=0)
            for k in range(n_dp)
        ]
    )
    len_mine = jnp.stack(
        [
            lax.dynamic_slice_in_dim(len_all[k], me * per_peer, per_peer, axis=0)
            for k in range(n_dp)
        ]
    )
    live_mine = (positions < len_mine.reshape(count, 1)).astype(F32)
    encoded = (
        mine.reshape(count, length, width).astype(F32)
        + total.reshape(count, length, width) * live_mine[:, :, None]
    ).astype(BF16)
    encoded = jnp.take(
        encoded.reshape(n_dp, per_peer, length, width), me ^ jnp.arange(n_dp), axis=0
    ).reshape(count, length, width)

    grad_normed = sum(piece.astype(F32) for piece in returned)
    inputs = x_own.reshape(count * length, width).astype(F32)
    centred = inputs - jnp.mean(inputs, axis=1, keepdims=True)
    variance = jnp.mean(centred * centred, axis=1, keepdims=True)
    inverse = lax.rsqrt(variance + EPS)
    standard = centred * inverse
    grad_standard = grad_normed * gain
    grad_inputs = inverse * (
        grad_standard
        - jnp.mean(grad_standard, axis=1, keepdims=True)
        - standard * jnp.mean(grad_standard * standard, axis=1, keepdims=True)
    )
    frame_sorted = (g_own.reshape(count * length, width).astype(F32) + grad_inputs).astype(BF16)
    back = jnp.argmax(
        send_order[None, :] == jnp.arange(count, dtype=jnp.int32)[:, None], axis=1
    )
    frame_grad = jnp.take(frame_sorted.reshape(count, length, width), back, axis=0)

    expand_part = sum(
        lax.dot_general(a, b, (((0,), (0,)), ((), ())), preferred_element_type=F32)
        for a, b in zip(normeds, grad_expandeds)
    )
    project_part = sum(
        lax.dot_general(
            a.reshape(-1, channels), b, (((0,), (0,)), ((), ())), preferred_element_type=F32
        )
        for a, b in zip(swisheds, maskeds)
    )
    gain_part, bias_part, kernel_part = sums
    small_part = jnp.concatenate(
        [
            kernel_part.T.reshape(n_shard, part * taps),
            bias_part.reshape(n_shard, part),
            gain_part.reshape(n_shard, owned),
        ],
        axis=1,
    )
    small_part = jnp.pad(small_part, ((0, 0), (0, small_rows * wide - small_part.shape[1])))
    project_part = project_part.reshape(n_shard, part, width)
    grad_pack = jnp.concatenate(
        [expand_part.reshape(n_shard, owned, wide)]
        + [project_part[:, :, h * wide : (h + 1) * wide] for h in range(n_halves)]
        + [small_part.reshape(n_shard, small_rows, wide)],
        axis=1,
    )
    reduced = reduce_shard(grad_pack, n_shard).astype(BF16)
    gathered = jnp.stack(gather_dp(reduced, n_dp))
    gathered = jnp.take(gathered, me ^ jnp.arange(n_dp), axis=0).astype(F32)
    expand_grad = (
        gathered[:, :owned]
        .reshape(n_dp, owned, 2, n_shard, part)
        .transpose(1, 2, 3, 0, 4)
        .reshape(owned, 2 * width)
    )
    project_grad = jnp.concatenate(
        [
            gathered[:, owned + h * part : owned + (h + 1) * part].reshape(owned, wide)
            for h in range(n_halves)
        ],
        axis=1,
    )
    small_grad = gathered[:, owned + n_halves * part :].reshape(n_dp, -1)
    kernel_grad = small_grad[:, : part * taps].reshape(owned, taps)
    bias_grad = small_grad[:, part * taps : part * (taps + 1)].reshape(owned)
    gain_grad = jnp.sum(small_grad[:, part * (taps + 1) : part * (taps + 1) + owned], axis=0)
    return encoded, frame_grad, gain_grad, bias_grad, kernel_grad, expand_grad, project_grad


def body(*arrays):
    fast = lax.axis_size("dp") == 4 and lax.axis_size("shard") == 8
    return (fast_body if fast else generic_body)(*arrays)


def solution(mesh):
    return jax.shard_map(
        body,
        mesh=mesh,
        in_specs=(
            P(("dp", "shard"), None, None),
            P(("dp", "shard"), None, None),
            P(("dp", "shard")),
            P(("dp", "shard")),
            P("shard"),
            P("shard"),
            P("shard", None),
            P("shard", None),
            P("shard", None),
        ),
        out_specs=(
            P(("dp", "shard"), None, None),
            P(("dp", "shard"), None, None),
            P("shard"),
            P("shard"),
            P("shard", None),
            P("shard", None),
            P("shard", None),
        ),
        check_vma=False,
    )
```

```python
import functools

import jax
import jax.numpy as jnp
from jax import lax
from jax.experimental import pallas as pl
from jax.experimental.pallas import tpu as pltpu
from jax.sharding import PartitionSpec as P

EPS = 1e-05
F32 = jnp.float32
BF16 = jnp.bfloat16
LANES = 128
MARGIN = 16
NT = (((1,), (1,)), ((), ()))
TN = (((0,), (0,)), ((), ()))
VMEM_PACK = 63
VMEM_CHUNK = 63
VMEM_ENCODE = 63
VMEM_FRAME = 63
VMEM_HOP = 63
VMEM_UNPACK = 28
LIGHT = pl.CostEstimate(flops=1, bytes_accessed=1, transcendentals=0)


def route(dims, refs, meta, s, base):
    count, length, taps = dims
    source = lax.axis_index("dp") ^ s
    copies = []
    for q in range(count):
        chosen = base + length * meta[source, count + (lax.axis_index("dp") ^ q)]
        copies.append(
            pltpu.make_async_copy(
                refs["sw"].at[pl.ds(pl.multiple_of(chosen, length), length)],
                refs["pieces"][q].at[pl.ds(pl.multiple_of(s * length, length), length)],
                refs["route_sems"].at[s, q],
            )
        )
    return copies


def one_source(dims, refs, meta, s, base, ready):
    count, length, taps = dims
    rows = count * length
    we, ab, pad, gpad, slope = (refs[n] for n in ("we", "ab", "pad", "gpad", "slope"))
    normed, sw, ge, taps_ref, small = (refs[n] for n in ("normed", "sw", "ge", "taps", "small"))
    width, wide = we.shape
    channels = wide // 2
    tiles = channels // LANES
    own = pl.ds(base, rows)
    step = 64
    ready("we")
    gain = refs["gain"][...]
    ready("x")

    @pl.loop(0, rows // step)
    def _(index):
        at = pl.ds(pl.multiple_of(base + index * step, step), step)
        x = refs["x"][at, :].astype(F32)
        centred = x - jnp.mean(x, axis=1, keepdims=True)
        variance = jnp.mean(centred * centred, axis=1, keepdims=True)
        normed[at, :] = (centred * lax.rsqrt(variance + EPS) * gain).astype(BF16)

    expanded = jnp.dot(normed[own, :], we[...], preferred_element_type=F32)
    for tile in range(2 * tiles):
        ab[tile] = expanded[:, tile * LANES : (tile + 1) * LANES]

    first = (taps - 1) // 2
    positions = lax.broadcasted_iota(jnp.int32, (length, LANES), 0)
    source = lax.axis_index("dp") ^ s

    @pl.loop(0, count)
    def _(u):
        at = pl.ds(pl.multiple_of(u * length, length), length)
        out = pl.ds(pl.multiple_of(base + u * length, length), length)
        live = positions < meta[source, u]
        for tile in range(tiles):
            lanes = pl.ds(tile * LANES, LANES)
            gate = jax.nn.sigmoid(ab[tiles + tile, at, :])
            glu = jnp.where(live, ab[tile, at, :] * gate, 0.0).astype(BF16).astype(F32)
            pad[u, tile, MARGIN : MARGIN + length, :] = glu
            ab[tiles + tile, at, :] = gate
            conv = jnp.broadcast_to(taps_ref[taps : taps + 1, lanes], (length, LANES))
            for t in range(taps):
                conv += taps_ref[t : t + 1, lanes] * pad[u, tile, pl.ds(MARGIN - first + t, length), :]
            sig = jax.nn.sigmoid(conv)
            sw[out, lanes] = jnp.where(live, conv * sig, 0.0).astype(BF16)
            slope[u, tile] = jnp.where(live, sig * (1.0 + conv * (1.0 - sig)), 0.0)

    for copy in route(dims, refs, meta, s, base):
        copy.start()

    ready("g")
    ready("wp")
    grad_swish = lax.dot_general(
        refs["g"][own, :], refs["wp"][...], NT, preferred_element_type=F32
    )
    for u in range(count):
        for tile in range(tiles):
            gpad[u, tile, MARGIN : MARGIN + length, :] = (
                grad_swish[u * length : (u + 1) * length, tile * LANES : (tile + 1) * LANES]
                * slope[u, tile]
            )

    def fold(value):
        return jnp.sum(value.reshape(length // 8, 8, LANES), axis=0)

    @pl.loop(0, count)
    def _(u):
        at = pl.ds(pl.multiple_of(u * length, length), length)
        out = pl.ds(pl.multiple_of(base + u * length, length), length)
        live = positions < meta[source, u]
        for tile in range(tiles):
            lanes = pl.ds(tile * LANES, LANES)
            grad_conv = gpad[u, tile, MARGIN : MARGIN + length, :]
            grad_glu = jnp.zeros((length, LANES), F32)
            for t in range(taps):
                small[tile, t] += fold(
                    pad[u, tile, pl.ds(MARGIN - first + t, length), :] * grad_conv
                )
                grad_glu += (
                    taps_ref[t : t + 1, lanes] * gpad[u, tile, pl.ds(MARGIN + first - t, length), :]
                )
            small[tile, taps] += fold(grad_conv)
            grad_glu = jnp.where(live, grad_glu, 0.0)
            gate = ab[tiles + tile, at, :]
            through = grad_glu * gate
            ge[out, lanes] = through.astype(BF16)
            ge[out, pl.ds(channels + tile * LANES, LANES)] = (
                through * ab[tile, at, :] * (1.0 - gate)
            ).astype(BF16)

    span = 512
    for start in range(0, width, span):
        cols = pl.ds(start, span)
        refs["gn"][own, cols] = lax.dot_general(
            ge[own, :], we[cols, :], NT, preferred_element_type=F32
        ).astype(BF16)


def clear_margins(*padded):
    for ref in padded:
        count, tiles, height, lanes = ref.shape
        zeros = jnp.zeros((MARGIN, lanes), F32)
        for u in range(count):
            for tile in range(tiles):
                ref[u, tile, :MARGIN, :] = zeros
                ref[u, tile, height - MARGIN :, :] = zeros


def source_scratch(count, length, channels):
    tiles = channels // LANES
    padded = pltpu.VMEM((count, tiles, length + 2 * MARGIN, LANES), F32)
    return [
        pltpu.VMEM((2 * tiles, count * length, LANES), F32),
        padded,
        padded,
        pltpu.VMEM((count, tiles, length, LANES), F32),
    ]


def weight_copies(blocks, owned, part, we, wp, small, sems):
    me = lax.axis_index("shard")
    width, wide = we.shape
    halves = width // wide
    move = pltpu.make_async_copy
    first, second = [], []
    for b, block in enumerate(blocks):
        offset = 2 * (b % (len(blocks) // 2)) + b // (len(blocks) // 2)
        owner = me ^ offset
        first.append(
            move(block.at[pl.ds(owned + halves * part, 16)], small.at[owner], sems.at[b, 0])
        )
        rows = pl.ds(pl.multiple_of(owner * owned, owned), owned)
        first.append(move(block.at[pl.ds(0, owned)], we.at[rows], sems.at[b, 1]))
        rows = pl.ds(pl.multiple_of(owner * part, part), part)
        for h in range(halves):
            second.append(
                move(
                    block.at[pl.ds(owned + h * part, part)],
                    wp.at[rows, pl.ds(h * wide, wide)],
                    sems.at[b, 2 + h],
                )
            )
    return first, second


def fill_tables(small, owned, part, taps_ref, gain_ref):
    rows = [small[j].astype(F32) for j in range(small.shape[0])]
    taps_ref[:16] = jnp.concatenate([r[:, :part] for r in rows], axis=1)
    taps_ref[16:] = jnp.concatenate([r[:, LANES : LANES + part] for r in rows], axis=1)
    gain_ref[...] = jnp.concatenate([r[:1, 2 * LANES : 2 * LANES + owned] for r in rows], axis=1)


def weight_scratch(owners, owned, width, wide, taps):
    return [
        pltpu.VMEM((width, wide), BF16),
        pltpu.VMEM((wide // 2, width), BF16),
        pltpu.VMEM((owners, 16, wide), BF16),
        pltpu.VMEM((taps + 1, wide // 2), F32),
        pltpu.SemaphoreType.DMA((owners, 2 + width // wide)),
    ]


def near_kernel(dims, n, owned, meta, *refs):
    count, length, taps = dims
    rows = count * length
    x_hbm, g_hbm, refs = refs[:n], refs[n : 2 * n], refs[2 * n :]
    outs = refs[-24 - n - count : -19]
    blocks = refs[: -24 - n - count]
    normed_hbm, sw_hbm, ge_hbm = outs[:3]
    gn_hbm, small, gain_ref, pieces = outs[3 : 3 + n], outs[3 + n], outs[4 + n], outs[5 + n :]
    x, normed, g, sw, ge, gn, ab, pad, gpad, slope = refs[-19:-9]
    we, wp, shares, taps_ref, weight_sems = refs[-9:-4]
    in_sems, out_sems, route_sems, _ = refs[-4:]
    part = owned * (we.shape[1] // 2) // we.shape[0]
    move = pltpu.make_async_copy

    def place(s):
        return pl.ds(s * rows, rows)

    incoming = {}
    for s in range(n):
        incoming["x", s] = move(x_hbm[s].at[pl.ds(0, rows)], x.at[place(s)], in_sems.at[s, 0])
        incoming["g", s] = move(
            g_hbm[s].at[pl.ds(g_hbm[s].shape[0] - rows, rows)], g.at[place(s)], in_sems.at[s, 1]
        )
    weights = weight_copies(blocks, owned, part, we, wp, shares, weight_sems)
    incoming["x", 0].start()
    for copy in weights[0]:
        copy.start()
    incoming["g", 0].start()
    for copy in weights[1]:
        copy.start()
    for s in range(1, n):
        incoming["x", s].start()
        incoming["g", s].start()
    clear_margins(pad, gpad)
    small[...] = jnp.zeros_like(small)
    views = dict(
        x=x, normed=normed, g=g, we=we, wp=wp, sw=sw, ge=ge, gn=gn, ab=ab, pad=pad, gpad=gpad,
        slope=slope, taps=taps_ref, gain=gain_ref, small=small, pieces=pieces, route_sems=route_sems,
    )

    @pl.loop(0, n)
    def _(s):
        def ready(what):
            if what in ("we", "wp"):
                @pl.when(s == 0)
                def _():
                    for copy in weights[what == "wp"]:
                        copy.wait()
                    if what == "we":
                        fill_tables(shares, owned, part, taps_ref, gain_ref)
            else:
                for at in range(n):
                    @pl.when(s == at)
                    def _():
                        incoming[what, at].wait()

        base = pl.multiple_of(s * rows, rows)
        one_source(dims, views, meta, s, base, ready)
        own = pl.ds(base, rows)
        for i, (source, target) in enumerate(((normed, normed_hbm), (sw, sw_hbm), (ge, ge_hbm))):
            move(source.at[own], target.at[own], out_sems.at[s, i]).start()
        for at in range(n):
            @pl.when(s == at)
            def _():
                move(gn.at[place(at)], gn_hbm[at], out_sems.at[at, 3]).start()

    for s in range(n):
        for i, (source, target) in enumerate(((normed, normed_hbm), (sw, sw_hbm), (ge, ge_hbm))):
            move(source.at[place(s)], target.at[place(s)], out_sems.at[s, i]).wait()
        move(gn.at[place(s)], gn_hbm[s], out_sems.at[s, 3]).wait()
        for copy in route(dims, views, meta, s, s * rows):
            copy.wait()


def near_call(ints, xs, gs, blocks, owned, dims):
    count, length, taps = dims
    n = len(xs)
    rows, width = count * length, xs[0].shape[1]
    wide = blocks[0].shape[1]
    channels = wide // 2
    owners = len(blocks)
    anywhere = pl.BlockSpec(memory_space=pl.ANY)
    return pl.pallas_call(
        functools.partial(near_kernel, dims, n, owned),
        out_shape=(
            jax.ShapeDtypeStruct((n * rows, width), BF16),
            jax.ShapeDtypeStruct((n * rows, channels), BF16),
            jax.ShapeDtypeStruct((n * rows, wide), BF16),
        )
        + (jax.ShapeDtypeStruct((rows, width), BF16),) * n
        + (
            jax.ShapeDtypeStruct((channels // LANES, taps + 1, 8, LANES), F32),
            jax.ShapeDtypeStruct((1, width), F32),
        )
        + (jax.ShapeDtypeStruct((rows, channels), BF16),) * count,
        in_specs=[in_smem()] + [anywhere] * (2 * n + owners),
        out_specs=(anywhere,) * (3 + n) + (in_vmem(), in_vmem()) + (anywhere,) * count,
        scratch_shapes=[
            pltpu.VMEM((n * rows, width), BF16),
            pltpu.VMEM((n * rows, width), BF16),
            pltpu.VMEM((n * rows, width), BF16),
            pltpu.VMEM((n * rows, channels), BF16),
            pltpu.VMEM((n * rows, wide), BF16),
            pltpu.VMEM((n * rows, width), BF16),
        ]
        + source_scratch(count, length, channels)
        + weight_scratch(owners, owned, width, wide, taps)
        + [
            pltpu.SemaphoreType.DMA((n, 2)),
            pltpu.SemaphoreType.DMA((n, 4)),
            pltpu.SemaphoreType.DMA((n, count)),
            pltpu.SemaphoreType.DMA,
        ],
        compiler_params=vmem_params(VMEM_CHUNK),
        cost_estimate=LIGHT,
        name="near_sources",
    )(ints, *xs, *gs, *blocks)


def far_kernel(dims, n, owned, meta, *refs):
    count, length, taps = dims
    rows = count * length
    core = lax.axis_index("shard") % 2
    x_hbm, normed_hbm, sw_hbm, ge_hbm = refs[:4]
    g_hbm, near_small = refs[4 : 5 + n], refs[5 + n]
    blocks, outs, refs = refs[6 + n : -25 - 2 * count], refs[-25 - count : -22], refs[-22:]
    gn_hbm, keep_hbm, give_hbm, pieces = outs[0], outs[1], outs[2], outs[3:]
    x, normed, g, sw, ge, gn, ab, pad, gpad, slope = refs[:10]
    we, wp, shares, taps_ref, weight_sems = refs[10:15]
    gain_ref, small, block, in_sems, out_sems, route_sems, _ = refs[15:]
    width, wide = we.shape
    channels = wide // 2
    tiles = channels // LANES
    chips = width // owned // 2
    halves = width // wide
    part = channels // (2 * chips)
    move = pltpu.make_async_copy
    base = n * rows
    near, last = pl.ds(0, base), pl.ds(base, rows)
    tail = [pl.ds(ref.shape[0] - rows, rows) for ref in g_hbm]
    incoming = dict(
        x=[move(x_hbm.at[pl.ds(0, rows)], x.at[last], in_sems.at[0])],
        g=[move(g_hbm[n].at[tail[n]], g.at[last], in_sems.at[2])],
    )
    incoming["we"], incoming["wp"] = weight_copies(
        blocks, owned, part, we, wp, shares, weight_sems
    )
    later = [
        move(normed_hbm, normed.at[near], in_sems.at[4]),
        move(sw_hbm, sw.at[near], in_sems.at[5]),
        move(ge_hbm, ge.at[near], in_sems.at[6]),
    ]
    later += [
        move(g_hbm[s].at[tail[s]], g.at[pl.ds(s * rows, rows)], in_sems.at[7 + s])
        for s in range(n)
    ]
    for copy in incoming["x"] + incoming["we"] + incoming["g"] + incoming["wp"] + later:
        copy.start()

    def ready(what):
        for copy in incoming[what]:
            copy.wait()
        if what == "we":
            fill_tables(shares, owned, part, taps_ref, gain_ref)

    clear_margins(pad, gpad)
    small[...] = near_small[...]
    views = dict(
        x=x, normed=normed, g=g, we=we, wp=wp, sw=sw, ge=ge, gn=gn, ab=ab, pad=pad, gpad=gpad,
        slope=slope, taps=taps_ref, gain=gain_ref, small=small, pieces=pieces, route_sems=route_sems,
    )
    one_source(dims, views, meta, n, base, ready)
    gn_out = move(gn.at[last], gn_hbm, out_sems.at[2])
    gn_out.start()
    routed = route(dims, views, meta, n, base)
    for copy in later:
        copy.wait()

    sums = jnp.sum(small[...], axis=2)
    sums = jnp.concatenate([sums[tile] for tile in range(tiles)], axis=1)
    span = 2 * owned
    bottom = owned + halves * part
    for chip in range(chips):
        total = lax.dot_general(
            normed[:, chip * span : (chip + 1) * span], ge[...], TN, preferred_element_type=F32
        ).astype(BF16)
        for which in range(2):
            block[which, chip, :owned] = total[which * owned : (which + 1) * owned]
    for h in range(halves):
        total = lax.dot_general(
            sw[...], g[:, h * wide : (h + 1) * wide], TN, preferred_element_type=F32
        ).astype(BF16)
        for owner in range(2 * chips):
            block[owner % 2, owner // 2, owned + h * part : owned + (h + 1) * part] = total[
                owner * part : (owner + 1) * part
            ]
    fill = jnp.zeros((16, LANES - part), F32)
    blank = jnp.zeros((16, wide - 2 * LANES), F32)
    for owner in range(2 * chips):
        table = sums[:, owner * part : (owner + 1) * part]
        line = jnp.concatenate([table[:16], fill, table[16:], fill, blank], axis=1)
        block[owner % 2, owner // 2, bottom:] = line.astype(BF16)
    outward = [
        move(block.at[1 - core], give_hbm, out_sems.at[0]),
        move(block.at[core], keep_hbm, out_sems.at[1]),
    ]
    for copy in outward:
        copy.start()
    for copy in outward + routed + [gn_out]:
        copy.wait()


def far_call(ints, x, near, gs, blocks, before, owned, dims):
    count, length, taps = dims
    n = len(gs) - 1
    rows = count * length
    width, wide = x.shape[1], blocks[0].shape[1]
    channels = wide // 2
    tiles = channels // LANES
    owners = len(blocks)
    chips = owners // 2
    halves = width // wide
    height = owned + halves * (channels // owners) + 16
    anywhere = pl.BlockSpec(memory_space=pl.ANY)
    normed, sw, ge, small = near
    every = (n + 1) * rows
    return pl.pallas_call(
        functools.partial(far_kernel, dims, n, owned),
        out_shape=(jax.ShapeDtypeStruct((rows, width), BF16),)
        + (jax.ShapeDtypeStruct((chips, height, wide), BF16),) * 2
        + (jax.ShapeDtypeStruct(before[0].shape, BF16),) * count,
        in_specs=[in_smem()] + [anywhere] * (5 + n) + [in_vmem()] + [anywhere] * (owners + count),
        out_specs=(anywhere,) * (3 + count),
        input_output_aliases={7 + n + owners + m: 3 + m for m in range(count)},
        scratch_shapes=[
            pltpu.VMEM((every, width), BF16),
            pltpu.VMEM((every, width), BF16),
            pltpu.VMEM((every, width), BF16),
            pltpu.VMEM((every, channels), BF16),
            pltpu.VMEM((every, wide), BF16),
            pltpu.VMEM((every, width), BF16),
        ]
        + source_scratch(count, length, channels)
        + weight_scratch(owners, owned, width, wide, taps)
        + [
            pltpu.VMEM((1, width), F32),
            pltpu.VMEM((tiles, taps + 1, 8, LANES), F32),
            pltpu.VMEM((2, chips, height, wide), BF16),
            pltpu.SemaphoreType.DMA((7 + n,)),
            pltpu.SemaphoreType.DMA((3,)),
            pltpu.SemaphoreType.DMA((n + 1, count)),
            pltpu.SemaphoreType.DMA,
        ],
        compiler_params=vmem_params(VMEM_CHUNK),
        cost_estimate=LIGHT,
        name="far_source",
    )(ints, x, normed, sw, ge, *gs, small, *blocks, *before)


def vmem_params(mib):
    return pltpu.CompilerParams(vmem_limit_bytes=mib * 1024 * 1024)


def in_vmem():
    return pl.BlockSpec(memory_space=pltpu.VMEM)


def in_smem():
    return pl.BlockSpec(memory_space=pltpu.SMEM)


def owned_column(channel, index, owned, part):
    return (channel // part) * owned + index * part + channel % part


def pack_kernel(expand_hbm, project_hbm, kernel_ref, bias_ref, gain_ref, x_hbm, g_hbm, *refs):
    pack_ref, both_hbm, copies_hbm, both, expand_ref, whole, sems = refs
    rows_in = x_hbm.shape[0]
    inward = [
        pltpu.make_async_copy(x_hbm, both.at[pl.ds(0, rows_in)], sems.at[2]),
        pltpu.make_async_copy(g_hbm, both.at[pl.ds(rows_in, rows_in)], sems.at[3]),
    ]
    owned, width = project_hbm.shape
    wide = pack_ref.shape[1]
    channels = wide // 2
    part = owned * channels // width
    index = lax.axis_index("dp")
    rows = pl.ds(pl.multiple_of(index * part, part), part)
    chips = copies_hbm.shape[0]
    copies = [
        pltpu.make_async_copy(expand_hbm, expand_ref, sems.at[0]),
        pltpu.make_async_copy(project_hbm, whole, sems.at[1]),
    ]
    for copy in inward + copies:
        copy.start()
    row = lax.broadcasted_iota(jnp.int32, (width, channels), 0)
    col = lax.broadcasted_iota(jnp.int32, (1, channels), 1)
    pick = jnp.where(row == owned_column(col, index, owned, part), 1.0, 0.0).astype(BF16)
    mine = lax.broadcasted_iota(jnp.int32, (owned, LANES), 1) + index * part
    mine = jnp.where(lax.broadcasted_iota(jnp.int32, (owned, LANES), 0) == mine, 1.0, 0.0)
    mine = mine.astype(BF16)
    table = jnp.concatenate(
        [
            jnp.dot(kernel_ref[...], mine, preferred_element_type=F32),
            jnp.dot(bias_ref[...].reshape(1, owned), mine, preferred_element_type=F32),
        ],
        axis=0,
    )
    base = owned + width // wide * part
    gain = jnp.broadcast_to(gain_ref[...].reshape(1, owned).astype(F32), (16, owned))
    blank = jnp.zeros((16, wide - 2 * LANES - owned), F32)
    pack_ref[base:, :] = jnp.concatenate(
        [table[:16], table[16:], gain, blank], axis=1
    ).astype(BF16)
    for copy in inward:
        copy.wait()
    outward = [pltpu.make_async_copy(both, both_hbm, sems.at[4])]
    outward[0].start()
    for copy in copies:
        copy.wait()
    for i in range(chips):
        outward.append(pltpu.make_async_copy(whole, copies_hbm.at[i], sems.at[5 + i]))
        outward[-1].start()
    block = whole[rows, :]
    for h in range(2):
        pack_ref[:owned, h * channels : (h + 1) * channels] = jnp.dot(
            expand_ref[:, h * width : (h + 1) * width], pick, preferred_element_type=F32
        ).astype(BF16)
    for h in range(width // wide):
        pack_ref[owned + h * part : owned + (h + 1) * part, :] = block[:, h * wide : (h + 1) * wide]
    for copy in outward:
        copy.wait()


def pack_call(expand_weight, project_weight, kernel, bias, gain, x, g, part, wide):
    owned, width = project_weight.shape
    height = owned + width // wide * part + 16
    chips = width // owned // 2
    rows = x.shape[0]
    anywhere = pl.BlockSpec(memory_space=pl.ANY)
    return pl.pallas_call(
        pack_kernel,
        out_shape=(
            jax.ShapeDtypeStruct((height, wide), BF16),
            jax.ShapeDtypeStruct((2 * rows, width), BF16),
            jax.ShapeDtypeStruct((chips, owned, width), BF16),
        ),
        in_specs=[anywhere] * 2 + [in_vmem()] * 3 + [anywhere] * 2,
        out_specs=(in_vmem(), anywhere, anywhere),
        scratch_shapes=[
            pltpu.VMEM((2 * rows, width), BF16),
            pltpu.VMEM(expand_weight.shape, BF16),
            pltpu.VMEM((owned, width), BF16),
            pltpu.SemaphoreType.DMA((5 + chips,)),
        ],
        compiler_params=vmem_params(VMEM_PACK),
        cost_estimate=LIGHT,
        name="pack",
    )(expand_weight, project_weight, kernel.T, bias, gain, x, g)


def encode_kernel(dims, meta, *refs):
    n, length, owned = dims
    frames = refs[:n]
    pieces, blocks, refs = refs[n : 2 * n], refs[2 * n : 2 * n + 2], refs[2 * n + 2 :]
    out_ref, cat, weight, residual, sems = refs
    shard = lax.axis_index("shard")
    channels = pieces[0].shape[1]
    part = owned // n
    me = lax.axis_index("dp")

    def rows(at, size):
        return pl.ds(pl.multiple_of(at * size, size), size)

    moves = []
    for which, block in enumerate(blocks):
        for chip in range(block.shape[0]):
            owner = 2 * chip + ((shard % 2) ^ which)
            for i in range(n):
                start = pl.multiple_of(i * channels + owner * part, part)
                moves.append((block.at[chip, pl.ds(i * part, part)], weight.at[pl.ds(start, part)]))
    for k in range(n):
        moves.append(
            (
                frames[k].at[rows(meta[me ^ k, n + me], length)],
                residual.at[rows(me ^ k, length)],
            )
        )
    for m in range(n):
        lanes = pl.ds(pl.multiple_of((me ^ m) * channels, channels), channels)
        for k in range(n):
            source = pieces[m].at[pl.ds(k * length, length)]
            moves.append((source, cat.at[rows(me ^ m ^ k, length), lanes]))
    copies = [
        pltpu.make_async_copy(source, target, sems.at[i])
        for i, (source, target) in enumerate(moves)
    ]
    for copy in copies:
        copy.start()
    for copy in copies:
        copy.wait()
    span = 512
    for start in range(0, cat.shape[1], span):
        cols = slice(start, start + span)
        term = jnp.dot(cat[...], weight[:, cols], preferred_element_type=F32)
        out_ref[:, cols] = (residual[:, cols].astype(F32) + term).astype(BF16)


def encode_call(ints, pieces, frames, blocks, length):
    n = len(frames)
    owned, width = blocks[0].shape[1:]
    anywhere = pl.BlockSpec(memory_space=pl.ANY)
    return pl.pallas_call(
        functools.partial(encode_kernel, (n, length, owned)),
        out_shape=jax.ShapeDtypeStruct((n * length, width), BF16),
        in_specs=[in_smem()] + [anywhere] * (2 * n + len(blocks)),
        out_specs=in_vmem(),
        scratch_shapes=[
            pltpu.VMEM((n * length, width), BF16),
            pltpu.VMEM((width, width), BF16),
            pltpu.VMEM((n * length, width), BF16),
            pltpu.SemaphoreType.DMA((width // owned * n + n + n * n,)),
        ],
        compiler_params=vmem_params(VMEM_ENCODE),
        cost_estimate=LIGHT,
        name="encode",
    )(ints, *frames, *pieces, *blocks)


def frame_grad_kernel(n, x_ref, g_ref, gain_ref, *refs):
    out_ref = refs[n]
    x = x_ref[...].astype(F32)
    centred = x - jnp.mean(x, axis=1, keepdims=True)
    inverse = lax.rsqrt(jnp.mean(centred * centred, axis=1, keepdims=True) + EPS)
    standard = centred * inverse
    grad = sum(ref[...].astype(F32) for ref in refs[:n]) * gain_ref[...]
    grad_in = inverse * (
        grad
        - jnp.mean(grad, axis=1, keepdims=True)
        - standard * jnp.mean(grad * standard, axis=1, keepdims=True)
    )
    out_ref[...] = (g_ref[...].astype(F32) + grad_in).astype(BF16)


def frame_grad_call(x, g, gain, returned):
    count, length, width = x.shape
    rows = count * length
    step = 64
    block = pl.BlockSpec((step, width), lambda s: (s, 0))
    out = pl.pallas_call(
        functools.partial(frame_grad_kernel, len(returned)),
        out_shape=jax.ShapeDtypeStruct((rows, width), BF16),
        grid=(rows // step,),
        in_specs=[block, block, pl.BlockSpec((1, width), lambda s: (0, 0))]
        + [block] * len(returned),
        out_specs=block,
        compiler_params=vmem_params(VMEM_FRAME),
        cost_estimate=LIGHT,
        name="frame_grad",
    )(x.reshape(rows, width), g.reshape(rows, width), gain, *returned)
    return out.reshape(count, length, width)


def unpack_kernel(dims, *refs):
    n, owned, part, half = dims
    blocks, (weight_ref, before, gain_ref) = refs[:n], refs[n : n + 3]
    expand_ref, project_ref, gain_out, cat, grads, project, sems = refs[-7:]
    channels = blocks[0].shape[1]
    width = cat.shape[1]
    wide = 2 * channels
    halves = width // wide
    me = lax.axis_index("dp")
    for k in range(n):
        cat[:, pl.ds(pl.multiple_of((me ^ k) * channels, channels), channels)] = blocks[k][:owned]
        rows = pl.ds(pl.multiple_of((me ^ k) * part, part), part)
        for h in range(halves):
            project[h, rows, :] = blocks[k][owned + h * part : owned + (h + 1) * part].astype(F32)
    copies = [
        pltpu.make_async_copy(
            project.at[h],
            project_ref.at[:, pl.ds(h * wide + half * channels, channels)],
            sems.at[0, h],
        )
        for h in range(halves)
    ]
    for copy in copies:
        copy.start()
    along = before[...]
    span = 512
    for i, start in enumerate(range(0, width, span)):
        row = lax.broadcasted_iota(jnp.int32, (width, span), 0)
        col = lax.broadcasted_iota(jnp.int32, (1, span), 1) + start
        place = col % owned // part * channels + col // owned * part + col % part
        spread = jnp.where(row == place, 1.0, 0.0).astype(BF16)
        grad = jnp.dot(cat[...], spread, preferred_element_type=F32)
        grads[i] = grad
        copy = pltpu.make_async_copy(
            grads.at[i],
            expand_ref.at[:, pl.ds(half * width + start, span)],
            sems.at[1, i],
        )
        copy.start()
        copies.append(copy)
        along += jnp.sum(
            grad * weight_ref[:, start : start + span].astype(F32), axis=1, keepdims=True
        )
    if half == 0:
        gain_out[...] = along
    else:
        row = jnp.transpose(jnp.broadcast_to(along, (owned, LANES)))[:1]
        gain_out[...] = row / gain_ref[...].astype(F32)
    for copy in copies:
        copy.wait()


def unpack_call(half, blocks, weight, before, gain, outputs, owned, part, width):
    n = len(blocks)
    channels = blocks[0].shape[1]
    halves = width // (2 * channels)
    anywhere = pl.BlockSpec(memory_space=pl.ANY)
    return pl.pallas_call(
        functools.partial(unpack_kernel, (n, owned, part, half)),
        out_shape=(
            jax.ShapeDtypeStruct((owned, 2 * width), F32),
            jax.ShapeDtypeStruct((owned, width), F32),
            jax.ShapeDtypeStruct((1, owned) if half else (owned, 1), F32),
        ),
        grid=(1,),
        in_specs=[in_vmem()] * n
        + [pl.BlockSpec((owned, width), lambda s: (0, half)), in_vmem(), in_vmem()]
        + [anywhere] * len(outputs),
        out_specs=(anywhere, anywhere, in_vmem()),
        scratch_shapes=[
            pltpu.VMEM((owned, width), BF16),
            pltpu.VMEM((width // 512, owned, 512), F32),
            pltpu.VMEM((halves, owned, channels), F32),
            pltpu.SemaphoreType.DMA((2, max(halves, width // 512))),
        ],
        input_output_aliases={n + 3 + i: i for i in range(len(outputs))},
        compiler_params=vmem_params(VMEM_UNPACK),
        cost_estimate=LIGHT,
        name="unpack",
    )(*blocks, weight, before, gain, *outputs)


def tie(value, *after):
    return lax.optimization_barrier((value,) + after)[0]


def gather_owners(x):
    blocks = [x] + [swap(x, "shard", 8, 2 * m) for m in (1, 2, 3)]
    return blocks + [swap(block, "shard", 8, 1) for block in blocks]


def add_cores_kernel(keep_hbm, got_hbm, *refs):
    n = len(refs) - 3
    outs, (keep, got, sems) = refs[:n], refs[n:]
    chip = lax.axis_index("shard") // 2
    copies = [
        (
            pltpu.make_async_copy(keep_hbm.at[chip ^ m], keep.at[m], sems.at[m, 0]),
            pltpu.make_async_copy(got_hbm.at[chip ^ m], got.at[m], sems.at[m, 1]),
        )
        for m in range(n)
    ]
    order = list(range(1, n)) + [0]
    for m in order:
        for copy in copies[m]:
            copy.start()
    for m in order:
        for copy in copies[m]:
            copy.wait()
        outs[m][...] = (keep[m].astype(F32) + got[m].astype(F32)).astype(BF16)


def add_cores(keep, got):
    n = keep.shape[0]
    anywhere = pl.BlockSpec(memory_space=pl.ANY)
    return pl.pallas_call(
        add_cores_kernel,
        out_shape=(jax.ShapeDtypeStruct(keep.shape[1:], BF16),) * n,
        in_specs=[anywhere] * 2,
        out_specs=(in_vmem(),) * n,
        scratch_shapes=[
            pltpu.VMEM(keep.shape, BF16),
            pltpu.VMEM(keep.shape, BF16),
            pltpu.SemaphoreType.DMA((n, 2)),
        ],
        compiler_params=vmem_params(VMEM_HOP),
        cost_estimate=LIGHT,
        name="add_cores",
    )(keep, got)


def add_chips_kernel(n, *refs):
    total = sum(ref[...].astype(F32) for ref in refs[:n]).astype(BF16)
    channels = refs[n].shape[1]
    for half, ref in enumerate(refs[n:]):
        ref[...] = total[:, half * channels : (half + 1) * channels]


def add_chips(come):
    rows, wide = come[0].shape
    return pl.pallas_call(
        functools.partial(add_chips_kernel, len(come)),
        out_shape=(jax.ShapeDtypeStruct((rows, wide // 2), BF16),) * 2,
        in_specs=[in_vmem()] * len(come),
        out_specs=(in_vmem(),) * 2,
        compiler_params=vmem_params(VMEM_HOP),
        cost_estimate=LIGHT,
        name="add_chips",
    )(*come)


def fast_body(
    frames,
    cotangent,
    lengths,
    send_order,
    norm_gain,
    conv_bias,
    kernel,
    expand_weight,
    project_weight,
):
    n_dp, n_shard = lax.axis_size("dp"), lax.axis_size("shard")
    count, length, width = frames.shape
    owned, taps = kernel.shape
    part = owned // n_dp
    wide = 2 * n_shard * part
    rows = count * length
    dims = (count, length, taps)
    x_own = frames.reshape(rows, width)
    g_own = cotangent.reshape(rows, width)
    pack, both, project = pack_call(
        expand_weight, project_weight, kernel, conv_bias, norm_gain, x_own, g_own, part, wide
    )
    ints = jnp.concatenate([lengths, send_order])
    ints = lax.all_to_all(jnp.broadcast_to(ints, (n_dp, 2 * count)), "dp", 0, 0, tiled=True)
    pack, both, ints = lax.optimization_barrier((pack, both, ints))
    both_x = swap(both, "dp", 4, 1)
    both_y = swap(both, "dp", 4, 2)
    packs = [pack] + [swap(pack, "shard", 8, 2 * m) for m in (1, 2, 3)]
    *packs, both_x, both_y = lax.optimization_barrier((*packs, both_x, both_y))
    packs += [swap(block, "shard", 8, 1) for block in packs]
    x_all = [x_own, both_x, both_y, swap(both_x[:rows], "dp", 4, 2)]
    g_all = [g_own, both_x, both_y, swap(both_y[rows:], "dp", 4, 1)]
    line = [[2 * c + i for c in range(n_shard // 2)] for i in range(2)]
    project = tie(project, *packs[1:4])
    project = lax.all_to_all(project, "shard", 0, 0, axis_index_groups=line, tiled=True)

    near = near_call(ints, x_all[:3], g_all[:3], packs, owned, dims)
    returned = [near[3]] + [swap(near[3 + k], "dp", n_dp, k) for k in (1, 2)]
    gain = near[7]
    far = far_call(ints, x_all[3], near[:3] + near[6:7], g_all, packs, near[8:], owned, dims)

    keep, give = far[1:3]
    give, keep = lax.optimization_barrier((give, keep, project, *returned[1:3]))[:2]
    sums = add_cores(keep, swap(give, "shard", 8, 1))
    come = [sums[0]] + [swap(sums[m], "shard", 8, 2 * m) for m in (1, 2, 3)]
    last, *pieces = lax.optimization_barrier((far[0], *far[3:], sums[1]))[:-1]
    returned.append(swap(last, "dp", n_dp, 3))
    pieces = [pieces[0]] + [swap(pieces[m], "dp", n_dp, m) for m in (1, 2, 3)]
    project = [project, swap(tie(project, sums[1]), "shard", 8, 1)]

    pieces[0] = tie(pieces[0], come[1])
    encoded = encode_call(ints, pieces, x_all, project, length)
    frame_grad = frame_grad_call(frames, tie(cotangent, come[1]), gain, returned)

    come[0] = tie(come[0], encoded, frame_grad)
    gathered = [[half] + [swap(half, "dp", 4, k) for k in (1, 2, 3)] for half in add_chips(come)]
    base = owned + width // wide * part
    table = jnp.stack([a[base:] for a in gathered[0]])
    table = jnp.take(table, lax.axis_index("dp") ^ jnp.arange(n_dp), axis=0).astype(F32)
    table = jnp.concatenate([table[:, :, :part], table[:, :, LANES : LANES + part]], axis=1)
    table = table.transpose(0, 2, 1).reshape(owned, taps + 1)
    outputs, along = (), jnp.zeros((owned, 1), F32)
    for half in range(2):
        *outputs, along = unpack_call(
            half, gathered[half], expand_weight, along, norm_gain[None], outputs, owned, part, width
        )
    expand_grad, project_grad = outputs
    return (
        encoded.reshape(frames.shape),
        frame_grad,
        along.reshape(owned),
        table[:, taps],
        table[:, :taps],
        expand_grad,
        project_grad,
    )


def depthwise(signal, taps_table):
    taps = taps_table.shape[0]
    half = (taps - 1) // 2
    length = signal.shape[1]
    padded = jnp.pad(signal, ((0, 0), (half, half), (0, 0)))
    result = jnp.zeros_like(signal)
    for offset in range(taps):
        result = result + padded[:, offset : offset + length, :] * taps_table[offset]
    return result


def kernel_terms(signal, upstream, taps):
    half = (taps - 1) // 2
    length = signal.shape[1]
    padded = jnp.pad(signal, ((0, 0), (half, half), (0, 0)))
    rows = []
    for offset in range(taps):
        rows.append(jnp.sum(padded[:, offset : offset + length, :] * upstream, axis=(0, 1)))
    return jnp.stack(rows, axis=0)


def chunk_compute(x, g, live, gain, taps, bias, expand_slice, project_slice):
    count, length, width = x.shape
    rows = count * length
    channels = taps.shape[1]
    inputs = x.reshape(rows, width).astype(F32)
    live_rows = live.reshape(rows, 1)
    centred = inputs - jnp.mean(inputs, axis=1, keepdims=True)
    variance = jnp.mean(centred * centred, axis=1, keepdims=True)
    standard = centred * lax.rsqrt(variance + EPS)
    normed = (standard * gain).astype(BF16)
    expanded = jnp.dot(normed, expand_slice, preferred_element_type=F32)
    value = expanded[:, :channels]
    gate = jax.nn.sigmoid(expanded[:, channels:])
    glu = (value * gate * live_rows).astype(BF16).astype(F32).reshape(count, length, channels)
    conv = depthwise(glu, taps).reshape(rows, channels) + bias
    conv_sig = jax.nn.sigmoid(conv)
    swished = (conv * conv_sig).astype(BF16)
    masked = (g.reshape(rows, width).astype(F32) * live_rows).astype(BF16)
    grad_swish = lax.dot_general(
        masked, project_slice, (((1,), (1,)), ((), ())), preferred_element_type=F32
    )
    grad_conv = grad_swish * conv_sig * (1.0 + conv * (1.0 - conv_sig))
    bias_part = jnp.sum(grad_conv, axis=0)
    volume = grad_conv.reshape(count, length, channels)
    kernel_part = kernel_terms(glu, volume, taps.shape[0])
    grad_glu = depthwise(volume, taps[::-1]).reshape(rows, channels) * live_rows
    grad_expanded = jnp.concatenate(
        [grad_glu * gate, grad_glu * value * gate * (1.0 - gate)], axis=1
    ).astype(BF16)
    grad_normed = lax.dot_general(
        grad_expanded, expand_slice, (((1,), (1,)), ((), ())), preferred_element_type=F32
    )
    gain_part = jnp.sum(grad_normed * standard, axis=0)
    return normed, masked, swished, grad_expanded, grad_normed.astype(BF16), (
        gain_part,
        bias_part,
        kernel_part,
    )


def swap(x, axis, size, k):
    return lax.ppermute(x, axis, [(p, p ^ k) for p in range(size)])


def gather_dp(x, n_dp):
    if n_dp == 4:
        half = x.shape[0] // 2
        along_x = swap(x, "dp", 4, 1)
        along_y = swap(x, "dp", 4, 2)
        far = jnp.concatenate(
            [swap(along_x[:half], "dp", 4, 2), swap(along_y[half:], "dp", 4, 1)], axis=0
        )
        return [x, along_x, along_y, far]
    return [x] + [swap(x, "dp", n_dp, k) for k in range(1, n_dp)]


def gather_shard(x, n_shard):
    if n_shard == 8:
        me = lax.axis_index("shard")
        chip, core = me // 2, me % 2
        blocks = [x] + [
            lax.ppermute(x, "shard", [(p, (p + 2 * k) % 8) for p in range(8)]) for k in (1, 2, 3)
        ]
        mine = jnp.stack(blocks)
        mine = jnp.take(mine, (chip - jnp.arange(4)) % 4, axis=0)
        other = swap(mine, "shard", 8, 1)
        pair = jnp.where(core == 0, jnp.stack([mine, other], 1), jnp.stack([other, mine], 1))
        return pair.reshape((8,) + x.shape)
    return lax.all_gather(x, "shard", axis=0)


def reduce_shard(x, n_shard):
    x = x.astype(BF16)
    if n_shard == 8:
        me = lax.axis_index("shard")
        chip, core = me // 2, me % 2
        cube = x.reshape((4, 2) + x.shape[1:])
        keep = jnp.take(cube, core, axis=1)
        give = jnp.take(cube, 1 - core, axis=1)
        both = (keep.astype(F32) + swap(give, "shard", 8, 1).astype(F32)).astype(BF16)
        total = jnp.take(both, chip, axis=0).astype(F32)
        for k in (1, 2, 3):
            piece = jnp.take(both, (chip + k) % 4, axis=0)
            total = total + lax.ppermute(
                piece, "shard", [(p, (p + 2 * k) % 8) for p in range(8)]
            ).astype(F32)
        return total
    return lax.psum_scatter(x, "shard", scatter_dimension=0, tiled=False).astype(F32)


def generic_body(
    frames,
    cotangent,
    lengths,
    send_order,
    norm_gain,
    conv_bias,
    kernel,
    expand_weight,
    project_weight,
):
    n_dp, n_shard = lax.axis_size("dp"), lax.axis_size("shard")
    count, length, width = frames.shape
    per_peer = count // n_dp
    owned, taps = kernel.shape
    part = owned // n_dp
    channels = n_shard * part
    me = lax.axis_index("dp")

    x_own = jnp.take(frames, send_order, axis=0)
    g_own = jnp.take(cotangent, send_order, axis=0)
    len_own = jnp.take(lengths, send_order, axis=0)

    expand_cols = lax.dynamic_index_in_dim(
        expand_weight.reshape(owned, 2, n_shard, n_dp, part), me, axis=3, keepdims=False
    ).reshape(owned, 2 * channels)
    project_rows = lax.dynamic_slice_in_dim(project_weight, me * part, part, axis=0)
    small = jnp.concatenate(
        [
            lax.dynamic_slice_in_dim(kernel, me * part, part, axis=0).reshape(-1),
            lax.dynamic_slice_in_dim(conv_bias, me * part, part, axis=0),
            norm_gain,
        ]
    )
    wide = 2 * channels
    small_rows = 16
    small = jnp.pad(small, (0, small_rows * wide - small.shape[0])).reshape(small_rows, wide)
    n_halves = width // wide
    pack = jnp.concatenate(
        [expand_cols] + [project_rows[:, h * wide : (h + 1) * wide] for h in range(n_halves)] + [small], axis=0
    )
    packs = gather_shard(pack, n_shard)
    expand_slice = packs[:, :owned].reshape(width, wide)
    project_slice = jnp.concatenate(
        [
            packs[:, owned + h * part : owned + (h + 1) * part].reshape(channels, wide)
            for h in range(n_halves)
        ],
        axis=1,
    )
    small_all = packs[:, owned + n_halves * part :].reshape(n_shard, -1).astype(F32)
    taps_table = small_all[:, : part * taps].reshape(channels, taps).T
    bias = small_all[:, part * taps : part * (taps + 1)].reshape(channels)
    gain = small_all[:, part * (taps + 1) : part * (taps + 1) + owned].reshape(width)
    project_full = gather_shard(project_weight, n_shard).reshape(n_shard, n_dp, part, width)

    x_all = gather_dp(x_own, n_dp)
    g_all = gather_dp(g_own, n_dp)
    len_all = [len_own] + [swap(len_own, "dp", n_dp, k) for k in range(1, n_dp)]

    normeds, maskeds, swisheds, grad_expandeds, returned = [], [], [], [], []
    sums = None
    positions = lax.broadcasted_iota(jnp.int32, (count, length), 1)
    for k in range(n_dp):
        live = (positions < len_all[k][:, None]).astype(F32)
        normed, masked, swished, grad_expanded, grad_normed, parts = chunk_compute(
            x_all[k], g_all[k], live, gain, taps_table, bias, expand_slice, project_slice
        )
        normeds.append(normed)
        maskeds.append(masked)
        swisheds.append(swished.reshape(n_dp, per_peer, length, channels))
        grad_expandeds.append(grad_expanded)
        returned.append(grad_normed if k == 0 else swap(grad_normed, "dp", n_dp, k))
        sums = parts if sums is None else tuple(a + b for a, b in zip(sums, parts))

    stack = jnp.stack(swisheds)
    total = None
    for m in range(n_dp):
        piece = lax.dynamic_index_in_dim(stack, me ^ m, axis=1, keepdims=False)
        if m:
            piece = swap(piece, "dp", n_dp, m)
        piece = jnp.stack([piece[k ^ m] for k in range(n_dp)])
        rows = lax.dynamic_index_in_dim(project_full, me ^ m, axis=1, keepdims=False)
        term = jnp.dot(
            piece.reshape(count * length, channels),
            rows.reshape(channels, width),
            preferred_element_type=F32,
        )
        total = term if total is None else total + term
    mine = jnp.stack(
        [
            lax.dynamic_slice_in_dim(x_all[k], me * per_peer, per_peer, axis=0)
            for k in range(n_dp)
        ]
    )
    len_mine = jnp.stack(
        [
            lax.dynamic_slice_in_dim(len_all[k], me * per_peer, per_peer, axis=0)
            for k in range(n_dp)
        ]
    )
    live_mine = (positions < len_mine.reshape(count, 1)).astype(F32)
    encoded = (
        mine.reshape(count, length, width).astype(F32)
        + total.reshape(count, length, width) * live_mine[:, :, None]
    ).astype(BF16)
    encoded = jnp.take(
        encoded.reshape(n_dp, per_peer, length, width), me ^ jnp.arange(n_dp), axis=0
    ).reshape(count, length, width)

    grad_normed = sum(piece.astype(F32) for piece in returned)
    inputs = x_own.reshape(count * length, width).astype(F32)
    centred = inputs - jnp.mean(inputs, axis=1, keepdims=True)
    variance = jnp.mean(centred * centred, axis=1, keepdims=True)
    inverse = lax.rsqrt(variance + EPS)
    standard = centred * inverse
    grad_standard = grad_normed * gain
    grad_inputs = inverse * (
        grad_standard
        - jnp.mean(grad_standard, axis=1, keepdims=True)
        - standard * jnp.mean(grad_standard * standard, axis=1, keepdims=True)
    )
    frame_sorted = (g_own.reshape(count * length, width).astype(F32) + grad_inputs).astype(BF16)
    back = jnp.argmax(
        send_order[None, :] == jnp.arange(count, dtype=jnp.int32)[:, None], axis=1
    )
    frame_grad = jnp.take(frame_sorted.reshape(count, length, width), back, axis=0)

    expand_part = sum(
        lax.dot_general(a, b, (((0,), (0,)), ((), ())), preferred_element_type=F32)
        for a, b in zip(normeds, grad_expandeds)
    )
    project_part = sum(
        lax.dot_general(
            a.reshape(-1, channels), b, (((0,), (0,)), ((), ())), preferred_element_type=F32
        )
        for a, b in zip(swisheds, maskeds)
    )
    gain_part, bias_part, kernel_part = sums
    small_part = jnp.concatenate(
        [
            kernel_part.T.reshape(n_shard, part * taps),
            bias_part.reshape(n_shard, part),
            gain_part.reshape(n_shard, owned),
        ],
        axis=1,
    )
    small_part = jnp.pad(small_part, ((0, 0), (0, small_rows * wide - small_part.shape[1])))
    project_part = project_part.reshape(n_shard, part, width)
    grad_pack = jnp.concatenate(
        [expand_part.reshape(n_shard, owned, wide)]
        + [project_part[:, :, h * wide : (h + 1) * wide] for h in range(n_halves)]
        + [small_part.reshape(n_shard, small_rows, wide)],
        axis=1,
    )
    reduced = reduce_shard(grad_pack, n_shard).astype(BF16)
    gathered = jnp.stack(gather_dp(reduced, n_dp))
    gathered = jnp.take(gathered, me ^ jnp.arange(n_dp), axis=0).astype(F32)
    expand_grad = (
        gathered[:, :owned]
        .reshape(n_dp, owned, 2, n_shard, part)
        .transpose(1, 2, 3, 0, 4)
        .reshape(owned, 2 * width)
    )
    project_grad = jnp.concatenate(
        [
            gathered[:, owned + h * part : owned + (h + 1) * part].reshape(owned, wide)
            for h in range(n_halves)
        ],
        axis=1,
    )
    small_grad = gathered[:, owned + n_halves * part :].reshape(n_dp, -1)
    kernel_grad = small_grad[:, : part * taps].reshape(owned, taps)
    bias_grad = small_grad[:, part * taps : part * (taps + 1)].reshape(owned)
    gain_grad = jnp.sum(small_grad[:, part * (taps + 1) : part * (taps + 1) + owned], axis=0)
    return encoded, frame_grad, gain_grad, bias_grad, kernel_grad, expand_grad, project_grad


def body(*arrays):
    fast = lax.axis_size("dp") == 4 and lax.axis_size("shard") == 8
    return (fast_body if fast else generic_body)(*arrays)


def solution(mesh):
    return jax.shard_map(
        body,
        mesh=mesh,
        in_specs=(
            P(("dp", "shard"), None, None),
            P(("dp", "shard"), None, None),
            P(("dp", "shard")),
            P(("dp", "shard")),
            P("shard"),
            P("shard"),
            P("shard", None),
            P("shard", None),
            P("shard", None),
        ),
        out_specs=(
            P(("dp", "shard"), None, None),
            P(("dp", "shard"), None, None),
            P("shard"),
            P("shard"),
            P("shard", None),
            P("shard", None),
            P("shard", None),
        ),
        check_vma=False,
    )
```

```python
import functools

import jax
import jax.numpy as jnp
from jax import lax
from jax.experimental import pallas as pl
from jax.experimental.pallas import tpu as pltpu
from jax.sharding import PartitionSpec as P

EPS = 1e-05
F32 = jnp.float32
BF16 = jnp.bfloat16
LANES = 128
MARGIN = 16
NT = (((1,), (1,)), ((), ()))
TN = (((0,), (0,)), ((), ()))
VMEM_PACK = 63
VMEM_CHUNK = 63
VMEM_ENCODE = 63
VMEM_FRAME = 63
VMEM_HOP = 63
VMEM_UNPACK = 28
LIGHT = pl.CostEstimate(flops=1, bytes_accessed=1, transcendentals=0)


def route(dims, sw, meta, s, base, targets, sems):
    count, length, taps = dims
    me = lax.axis_index("dp")
    copies = []
    for i, (q, target) in enumerate(targets):
        chosen = base + length * meta[me ^ s, count + (me ^ q)]
        source = sw.at[pl.ds(pl.multiple_of(chosen, length), length)]
        copies.append(pltpu.make_async_copy(source, target, sems.at[i]))
    return copies


def one_source(dims, refs, meta, s, base, ready):
    count, length, taps = dims
    rows = count * length
    we, ab, pad, gpad, slope = (refs[n] for n in ("we", "ab", "pad", "gpad", "slope"))
    normed, sw, ge, taps_ref, small = (refs[n] for n in ("normed", "sw", "ge", "taps", "small"))
    width, wide = we.shape
    channels = wide // 2
    tiles = channels // LANES
    own = pl.ds(base, rows)
    step = 256
    ready("we")
    gain = refs["gain"][...]
    ready("x")

    @pl.loop(0, rows // step)
    def _(index):
        at = pl.ds(pl.multiple_of(base + index * step, step), step)
        x = refs["x"][at, :].astype(F32)
        centred = x - jnp.mean(x, axis=1, keepdims=True)
        variance = jnp.mean(centred * centred, axis=1, keepdims=True)
        normed[at, :] = (centred * lax.rsqrt(variance + EPS) * gain).astype(BF16)

    expanded = jnp.dot(normed[own, :], we[...], preferred_element_type=F32)
    for tile in range(2 * tiles):
        ab[tile] = expanded[:, tile * LANES : (tile + 1) * LANES]

    first = (taps - 1) // 2
    positions = lax.broadcasted_iota(jnp.int32, (length, LANES), 0)
    source = lax.axis_index("dp") ^ s

    @pl.loop(0, count)
    def _(u):
        at = pl.ds(pl.multiple_of(u * length, length), length)
        out = pl.ds(pl.multiple_of(base + u * length, length), length)
        live = positions < meta[source, u]
        for tile in range(tiles):
            lanes = pl.ds(tile * LANES, LANES)
            gate = jax.nn.sigmoid(ab[tiles + tile, at, :])
            glu = jnp.where(live, ab[tile, at, :] * gate, 0.0).astype(BF16).astype(F32)
            pad[u, tile, MARGIN : MARGIN + length, :] = glu
            ab[tiles + tile, at, :] = gate
            conv = jnp.broadcast_to(taps_ref[taps : taps + 1, lanes], (length, LANES))
            for t in range(taps):
                conv += taps_ref[t : t + 1, lanes] * pad[u, tile, pl.ds(MARGIN - first + t, length), :]
            sig = jax.nn.sigmoid(conv)
            sw[out, lanes] = jnp.where(live, conv * sig, 0.0).astype(BF16)
            slope[u, tile] = jnp.where(live, sig * (1.0 + conv * (1.0 - sig)), 0.0)

    for copy in refs["route"](s, base):
        copy.start()

    ready("g")
    ready("wp")
    grad_swish = lax.dot_general(
        refs["g"][own, :], refs["wp"][...], NT, preferred_element_type=F32
    )
    for u in range(count):
        for tile in range(tiles):
            gpad[u, tile, MARGIN : MARGIN + length, :] = (
                grad_swish[u * length : (u + 1) * length, tile * LANES : (tile + 1) * LANES]
                * slope[u, tile]
            )

    def fold(value):
        return jnp.sum(value.reshape(length // 8, 8, LANES), axis=0)

    @pl.loop(0, count)
    def _(u):
        at = pl.ds(pl.multiple_of(u * length, length), length)
        out = pl.ds(pl.multiple_of(base + u * length, length), length)
        live = positions < meta[source, u]
        for tile in range(tiles):
            lanes = pl.ds(tile * LANES, LANES)
            grad_conv = gpad[u, tile, MARGIN : MARGIN + length, :]
            grad_glu = jnp.zeros((length, LANES), F32)
            for t in range(taps):
                small[tile, t] += fold(
                    pad[u, tile, pl.ds(MARGIN - first + t, length), :] * grad_conv
                )
                grad_glu += (
                    taps_ref[t : t + 1, lanes] * gpad[u, tile, pl.ds(MARGIN + first - t, length), :]
                )
            small[tile, taps] += fold(grad_conv)
            grad_glu = jnp.where(live, grad_glu, 0.0)
            gate = ab[tiles + tile, at, :]
            through = grad_glu * gate
            ge[out, lanes] = through.astype(BF16)
            ge[out, pl.ds(channels + tile * LANES, LANES)] = (
                through * ab[tile, at, :] * (1.0 - gate)
            ).astype(BF16)

    span = 512
    for start in range(0, width, span):
        cols = pl.ds(start, span)
        refs["gn"][own, cols] = lax.dot_general(
            ge[own, :], we[cols, :], NT, preferred_element_type=F32
        ).astype(BF16)


def clear_margins(*padded):
    for ref in padded:
        count, tiles, height, lanes = ref.shape
        zeros = jnp.zeros((MARGIN, lanes), F32)
        for u in range(count):
            for tile in range(tiles):
                ref[u, tile, :MARGIN, :] = zeros
                ref[u, tile, height - MARGIN :, :] = zeros


def source_scratch(count, length, channels):
    tiles = channels // LANES
    padded = pltpu.VMEM((count, tiles, length + 2 * MARGIN, LANES), F32)
    return [
        pltpu.VMEM((2 * tiles, count * length, LANES), F32),
        padded,
        padded,
        pltpu.VMEM((count, tiles, length, LANES), F32),
    ]


def weight_copies(blocks, owned, part, we, wp, small, sems):
    me = lax.axis_index("shard")
    width, wide = we.shape
    halves = width // wide
    move = pltpu.make_async_copy
    first, second = [], []
    for b, block in enumerate(blocks):
        offset = 2 * (b % (len(blocks) // 2)) + b // (len(blocks) // 2)
        owner = me ^ offset
        first.append(
            move(block.at[pl.ds(owned + halves * part, 16)], small.at[owner], sems.at[b, 0])
        )
        rows = pl.ds(pl.multiple_of(owner * owned, owned), owned)
        first.append(move(block.at[pl.ds(0, owned)], we.at[rows], sems.at[b, 1]))
        rows = pl.ds(pl.multiple_of(owner * part, part), part)
        for h in range(halves):
            second.append(
                move(
                    block.at[pl.ds(owned + h * part, part)],
                    wp.at[rows, pl.ds(h * wide, wide)],
                    sems.at[b, 2 + h],
                )
            )
    return first, second


def fill_tables(small, owned, part, taps_ref, gain_ref):
    rows = [small[j].astype(F32) for j in range(small.shape[0])]
    taps_ref[:16] = jnp.concatenate([r[:, :part] for r in rows], axis=1)
    taps_ref[16:] = jnp.concatenate([r[:, LANES : LANES + part] for r in rows], axis=1)
    gain_ref[...] = jnp.concatenate([r[:1, 2 * LANES : 2 * LANES + owned] for r in rows], axis=1)


def weight_scratch(owners, owned, width, wide, taps):
    return [
        pltpu.VMEM((width, wide), BF16),
        pltpu.VMEM((wide // 2, width), BF16),
        pltpu.VMEM((owners, 16, wide), BF16),
        pltpu.VMEM((taps + 1, wide // 2), F32),
        pltpu.SemaphoreType.DMA((owners, 2 + width // wide)),
    ]


def near_kernel(dims, n, owned, meta, *refs):
    count, length, taps = dims
    rows = count * length
    x_hbm, g_hbm, refs = refs[:n], refs[n : 2 * n], refs[2 * n :]
    outs = refs[-24 - n : -19]
    blocks = refs[: -24 - n]
    normed_hbm, sw_hbm, ge_hbm = outs[:3]
    gn_hbm, small, gain_ref = outs[3 : 3 + n], outs[3 + n], outs[4 + n]
    x, normed, g, sw, ge, gn, ab, pad, gpad, slope = refs[-19:-9]
    we, wp, shares, taps_ref, weight_sems = refs[-9:-4]
    in_sems, out_sems, route_sems, _ = refs[-4:]
    part = owned * (we.shape[1] // 2) // we.shape[0]
    move = pltpu.make_async_copy

    def place(s):
        return pl.ds(s * rows, rows)

    incoming = {}
    for s in range(n):
        incoming["x", s] = move(x_hbm[s].at[pl.ds(0, rows)], x.at[place(s)], in_sems.at[s, 0])
        incoming["g", s] = move(
            g_hbm[s].at[pl.ds(g_hbm[s].shape[0] - rows, rows)], g.at[place(s)], in_sems.at[s, 1]
        )
    weights = weight_copies(blocks, owned, part, we, wp, shares, weight_sems)
    incoming["x", 0].start()
    for copy in weights[0]:
        copy.start()
    incoming["g", 0].start()
    for copy in weights[1]:
        copy.start()
    for s in range(1, n):
        incoming["x", s].start()
        incoming["g", s].start()
    clear_margins(pad, gpad)
    small[...] = jnp.zeros_like(small)
    views = dict(
        x=x, normed=normed, g=g, we=we, wp=wp, sw=sw, ge=ge, gn=gn, ab=ab, pad=pad, gpad=gpad,
        slope=slope, taps=taps_ref, gain=gain_ref, small=small, route=lambda s, base: [],
    )

    @pl.loop(0, n)
    def _(s):
        def ready(what):
            if what in ("we", "wp"):
                @pl.when(s == 0)
                def _():
                    for copy in weights[what == "wp"]:
                        copy.wait()
                    if what == "we":
                        fill_tables(shares, owned, part, taps_ref, gain_ref)
            else:
                for at in range(n):
                    @pl.when(s == at)
                    def _():
                        incoming[what, at].wait()

        base = pl.multiple_of(s * rows, rows)
        one_source(dims, views, meta, s, base, ready)
        own = pl.ds(base, rows)
        for i, (source, target) in enumerate(((normed, normed_hbm), (sw, sw_hbm), (ge, ge_hbm))):
            move(source.at[own], target.at[own], out_sems.at[s, i]).start()
        for at in range(n):
            @pl.when(s == at)
            def _():
                move(gn.at[place(at)], gn_hbm[at], out_sems.at[at, 3]).start()

    for s in range(n):
        for i, (source, target) in enumerate(((normed, normed_hbm), (sw, sw_hbm), (ge, ge_hbm))):
            move(source.at[place(s)], target.at[place(s)], out_sems.at[s, i]).wait()
        move(gn.at[place(s)], gn_hbm[s].at[pl.ds(0, rows)], out_sems.at[s, 3]).wait()


def near_call(ints, xs, gs, blocks, owned, dims):
    count, length, taps = dims
    n = len(xs)
    rows, width = count * length, xs[0].shape[1]
    wide = blocks[0].shape[1]
    channels = wide // 2
    owners = len(blocks)
    anywhere = pl.BlockSpec(memory_space=pl.ANY)
    return pl.pallas_call(
        functools.partial(near_kernel, dims, n, owned),
        out_shape=(
            jax.ShapeDtypeStruct((n * rows, width), BF16),
            jax.ShapeDtypeStruct((n * rows, channels), BF16),
            jax.ShapeDtypeStruct((n * rows, wide), BF16),
        )
        + (jax.ShapeDtypeStruct((rows, width), BF16),) * n
        + (
            jax.ShapeDtypeStruct((channels // LANES, taps + 1, 8, LANES), F32),
            jax.ShapeDtypeStruct((1, width), F32),
        ),
        in_specs=[in_smem()] + [anywhere] * (2 * n + owners),
        out_specs=(anywhere,) * (3 + n) + (in_vmem(), in_vmem()),
        scratch_shapes=[
            pltpu.VMEM((n * rows, width), BF16),
            pltpu.VMEM((n * rows, width), BF16),
            pltpu.VMEM((n * rows, width), BF16),
            pltpu.VMEM((n * rows, channels), BF16),
            pltpu.VMEM((n * rows, wide), BF16),
            pltpu.VMEM((n * rows, width), BF16),
        ]
        + source_scratch(count, length, channels)
        + weight_scratch(owners, owned, width, wide, taps)
        + [
            pltpu.SemaphoreType.DMA((n, 2)),
            pltpu.SemaphoreType.DMA((n, 4)),
            pltpu.SemaphoreType.DMA((n, count)),
            pltpu.SemaphoreType.DMA,
        ],
        compiler_params=vmem_params(VMEM_CHUNK),
        cost_estimate=LIGHT,
        name="near_sources",
    )(ints, *xs, *gs, *blocks)


def far_kernel(dims, n, owned, meta, *refs):
    count, length, taps = dims
    rows = count * length
    core = lax.axis_index("shard") % 2
    x_hbm, normed_hbm, sw_hbm, ge_hbm = refs[:4]
    g_hbm, near_small = refs[4 : 5 + n], refs[5 + n]
    blocks, outs, refs = refs[6 + n : -25 - n], refs[-25 - n : -22], refs[-22:]
    gn_hbm, keep_hbm, give_hbm, own_hbm, single_hbm = *outs[:4], outs[4:]
    x, normed, g, sw, ge, gn, ab, pad, gpad, slope = refs[:10]
    we, wp, shares, taps_ref, weight_sems = refs[10:15]
    gain_ref, small, block, in_sems, out_sems, route_sems, _ = refs[15:]
    width, wide = we.shape
    channels = wide // 2
    tiles = channels // LANES
    chips = width // owned // 2
    halves = width // wide
    part = channels // (2 * chips)
    move = pltpu.make_async_copy
    base = n * rows
    near, last = pl.ds(0, base), pl.ds(base, rows)
    tail = [pl.ds(ref.shape[0] - rows, rows) for ref in g_hbm]
    incoming = dict(
        x=[move(x_hbm.at[pl.ds(0, rows)], x.at[last], in_sems.at[0])],
        g=[move(g_hbm[n].at[tail[n]], g.at[last], in_sems.at[2])],
    )
    incoming["we"], incoming["wp"] = weight_copies(
        blocks, owned, part, we, wp, shares, weight_sems
    )
    later = [
        move(normed_hbm, normed.at[near], in_sems.at[4]),
        move(sw_hbm, sw.at[near], in_sems.at[5]),
        move(ge_hbm, ge.at[near], in_sems.at[6]),
    ]
    later += [
        move(g_hbm[s].at[tail[s]], g.at[pl.ds(s * rows, rows)], in_sems.at[7 + s])
        for s in range(n)
    ]
    for copy in incoming["x"] + incoming["we"] + incoming["g"] + incoming["wp"] + later:
        copy.start()

    def ready(what):
        for copy in incoming[what]:
            copy.wait()
        if what == "we":
            fill_tables(shares, owned, part, taps_ref, gain_ref)

    clear_margins(pad, gpad)
    small[...] = near_small[...]

    def pieces(s, base):
        cols = pl.ds(s * channels, channels)
        targets = [(0, own_hbm.at[:, cols]), (n, gn_hbm.at[pl.ds(rows, length), cols])]
        targets += [(1 + i, ref.at[:, cols]) for i, ref in enumerate(single_hbm)]
        return route(dims, sw, meta, s, base, targets, route_sems.at[s])

    views = dict(
        x=x, normed=normed, g=g, we=we, wp=wp, sw=sw, ge=ge, gn=gn, ab=ab, pad=pad, gpad=gpad,
        slope=slope, taps=taps_ref, gain=gain_ref, small=small, route=pieces,
    )
    one_source(dims, views, meta, n, base, ready)
    gn_out = move(gn.at[last], gn_hbm.at[pl.ds(0, rows)], out_sems.at[0])
    gn_out.start()
    routed = pieces(n, base)
    for copy in later:
        copy.wait()
    for s in range(n):
        for copy in pieces(s, s * rows):
            copy.start()
            routed.append(copy)

    sums = jnp.sum(small[...], axis=2)
    sums = jnp.concatenate([sums[tile] for tile in range(tiles)], axis=1)
    span = 2 * owned
    bottom = owned + halves * part
    for h in range(halves):
        total = lax.dot_general(
            sw[...], g[:, h * wide : (h + 1) * wide], TN, preferred_element_type=F32
        ).astype(BF16)
        for owner in range(2 * chips):
            block[owner % 2, owner // 2, owned + h * part : owned + (h + 1) * part] = total[
                owner * part : (owner + 1) * part
            ]
    fill = jnp.zeros((16, LANES - part), F32)
    blank = jnp.zeros((16, wide - 2 * LANES), F32)
    for owner in range(2 * chips):
        table = sums[:, owner * part : (owner + 1) * part]
        line = jnp.concatenate([table[:16], fill, table[16:], fill, blank], axis=1)
        block[owner % 2, owner // 2, bottom:] = line.astype(BF16)
    outward = []
    for chip in range(chips):
        total = lax.dot_general(
            normed[:, chip * span : (chip + 1) * span], ge[...], TN, preferred_element_type=F32
        ).astype(BF16)
        for which in range(2):
            block[which, chip, :owned] = total[which * owned : (which + 1) * owned]
        for i, (which, target) in enumerate(((1 - core, give_hbm), (core, keep_hbm))):
            outward.append(
                move(block.at[which, chip], target.at[chip], out_sems.at[1 + 2 * chip + i])
            )
            outward[-1].start()
    for copy in outward + routed + [gn_out]:
        copy.wait()


def far_call(ints, x, near, gs, blocks, owned, dims):
    count, length, taps = dims
    n = len(gs) - 1
    rows = count * length
    width, wide = x.shape[1], blocks[0].shape[1]
    channels = wide // 2
    tiles = channels // LANES
    owners = len(blocks)
    chips = owners // 2
    halves = width // wide
    height = owned + halves * (channels // owners) + 16
    anywhere = pl.BlockSpec(memory_space=pl.ANY)
    normed, sw, ge, small = near
    every = (n + 1) * rows
    return pl.pallas_call(
        functools.partial(far_kernel, dims, n, owned),
        out_shape=(jax.ShapeDtypeStruct((rows + length, width), BF16),)
        + (jax.ShapeDtypeStruct((chips, height, wide), BF16),) * 2
        + (jax.ShapeDtypeStruct((length, width), BF16),)
        + (jax.ShapeDtypeStruct((length, width), BF16),) * (n - 1),
        in_specs=[in_smem()] + [anywhere] * (5 + n) + [in_vmem()] + [anywhere] * owners,
        out_specs=(anywhere,) * (3 + n),
        scratch_shapes=[
            pltpu.VMEM((every, width), BF16),
            pltpu.VMEM((every, width), BF16),
            pltpu.VMEM((every, width), BF16),
            pltpu.VMEM((every, channels), BF16),
            pltpu.VMEM((every, wide), BF16),
            pltpu.VMEM((every, width), BF16),
        ]
        + source_scratch(count, length, channels)
        + weight_scratch(owners, owned, width, wide, taps)
        + [
            pltpu.VMEM((1, width), F32),
            pltpu.VMEM((tiles, taps + 1, 8, LANES), F32),
            pltpu.VMEM((2, chips, height, wide), BF16),
            pltpu.SemaphoreType.DMA((7 + n,)),
            pltpu.SemaphoreType.DMA((1 + 2 * chips,)),
            pltpu.SemaphoreType.DMA((n + 1, count)),
            pltpu.SemaphoreType.DMA,
        ],
        compiler_params=vmem_params(VMEM_CHUNK),
        cost_estimate=LIGHT,
        name="far_source",
    )(ints, x, normed, sw, ge, *gs, small, *blocks)


def vmem_params(mib):
    return pltpu.CompilerParams(vmem_limit_bytes=mib * 1024 * 1024)


def in_vmem():
    return pl.BlockSpec(memory_space=pltpu.VMEM)


def in_smem():
    return pl.BlockSpec(memory_space=pltpu.SMEM)


def owned_column(channel, index, owned, part):
    return (channel // part) * owned + index * part + channel % part


def pack_kernel(expand_hbm, project_hbm, kernel_ref, bias_ref, gain_ref, x_hbm, g_hbm, *refs):
    pack_ref, both_hbm, copies_hbm, both, expand_ref, whole, sems = refs
    rows_in = x_hbm.shape[0]
    inward = [
        pltpu.make_async_copy(x_hbm, both.at[pl.ds(0, rows_in)], sems.at[2, 0]),
        pltpu.make_async_copy(g_hbm, both.at[pl.ds(rows_in, rows_in)], sems.at[3, 0]),
    ]
    owned, width = project_hbm.shape
    wide = pack_ref.shape[1]
    channels = wide // 2
    part = owned * channels // width
    index = lax.axis_index("dp")
    rows = pl.ds(pl.multiple_of(index * part, part), part)
    chips = copies_hbm.shape[0]
    copies = [
        pltpu.make_async_copy(expand_hbm, expand_ref, sems.at[0, 0]),
        pltpu.make_async_copy(project_hbm, whole, sems.at[1, 0]),
    ]
    for copy in inward + copies:
        copy.start()
    row = lax.broadcasted_iota(jnp.int32, (width, channels), 0)
    col = lax.broadcasted_iota(jnp.int32, (1, channels), 1)
    pick = jnp.where(row == owned_column(col, index, owned, part), 1.0, 0.0).astype(BF16)
    mine = lax.broadcasted_iota(jnp.int32, (owned, LANES), 1) + index * part
    mine = jnp.where(lax.broadcasted_iota(jnp.int32, (owned, LANES), 0) == mine, 1.0, 0.0)
    mine = mine.astype(BF16)
    table = jnp.concatenate(
        [
            jnp.dot(kernel_ref[...], mine, preferred_element_type=F32),
            jnp.dot(bias_ref[...].reshape(1, owned), mine, preferred_element_type=F32),
        ],
        axis=0,
    )
    base = owned + width // wide * part
    gain = jnp.broadcast_to(gain_ref[...].reshape(1, owned).astype(F32), (16, owned))
    blank = jnp.zeros((16, wide - 2 * LANES - owned), F32)
    pack_ref[base:, :] = jnp.concatenate(
        [table[:16], table[16:], gain, blank], axis=1
    ).astype(BF16)
    for copy in inward:
        copy.wait()
    outward = [pltpu.make_async_copy(both, both_hbm, sems.at[4, 0])]
    outward[0].start()
    for copy in copies:
        copy.wait()
    for i in range(chips):
        for k in range(1, owned // part):
            outward.append(
                pltpu.make_async_copy(
                    whole.at[pl.ds(pl.multiple_of((index ^ k) * part, part), part)],
                    copies_hbm.at[i, pl.ds((k - 1) * part, part)],
                    sems.at[5 + i, k],
                )
            )
            outward[-1].start()
    block = whole[rows, :]
    for h in range(2):
        pack_ref[:owned, h * channels : (h + 1) * channels] = jnp.dot(
            expand_ref[:, h * width : (h + 1) * width], pick, preferred_element_type=F32
        ).astype(BF16)
    for h in range(width // wide):
        pack_ref[owned + h * part : owned + (h + 1) * part, :] = block[:, h * wide : (h + 1) * wide]
    for copy in outward:
        copy.wait()


def pack_call(expand_weight, project_weight, kernel, bias, gain, x, g, part, wide):
    owned, width = project_weight.shape
    height = owned + width // wide * part + 16
    chips = width // owned // 2
    rows = x.shape[0]
    anywhere = pl.BlockSpec(memory_space=pl.ANY)
    return pl.pallas_call(
        pack_kernel,
        out_shape=(
            jax.ShapeDtypeStruct((height, wide), BF16),
            jax.ShapeDtypeStruct((2 * rows, width), BF16),
            jax.ShapeDtypeStruct((chips, owned - part, width), BF16),
        ),
        in_specs=[anywhere] * 2 + [in_vmem()] * 3 + [anywhere] * 2,
        out_specs=(in_vmem(), anywhere, anywhere),
        scratch_shapes=[
            pltpu.VMEM((2 * rows, width), BF16),
            pltpu.VMEM(expand_weight.shape, BF16),
            pltpu.VMEM((owned, width), BF16),
            pltpu.SemaphoreType.DMA((5 + chips, owned // part)),
        ],
        compiler_params=vmem_params(VMEM_PACK),
        cost_estimate=LIGHT,
        name="pack",
    )(expand_weight, project_weight, kernel.T, bias, gain, x, g)


def encode_kernel(dims, meta, *refs):
    n, length, owned = dims
    frames = refs[:n]
    pieces, below, blocks = refs[n : 2 * n - 1], refs[2 * n - 1], refs[2 * n : 2 * n + 2]
    packs, (out_ref, cat, weight, residual, sems) = refs[2 * n + 2 : -5], refs[-5:]
    shard = lax.axis_index("shard")
    channels = cat.shape[1] // n
    part = owned // n
    me = lax.axis_index("dp")

    def rows(at, size):
        return pl.ds(pl.multiple_of(at * size, size), size)

    moves = []
    for which, block in enumerate(blocks):
        for chip in range(block.shape[0]):
            owner = 2 * chip + ((shard % 2) ^ which)
            for k in range(1, n):
                start = pl.multiple_of((me ^ k) * channels + owner * part, part)
                source = block.at[chip, pl.ds((k - 1) * part, part)]
                moves.append((source, weight.at[pl.ds(start, part)]))
    wide = packs[0].shape[1]
    for b, block in enumerate(packs):
        owner = shard ^ (2 * (b % (len(packs) // 2)) + b // (len(packs) // 2))
        start = pl.multiple_of(me * channels + owner * part, part)
        for h in range(weight.shape[1] // wide):
            source = block.at[pl.ds(owned + h * part, part)]
            moves.append((source, weight.at[pl.ds(start, part), pl.ds(h * wide, wide)]))
    for k in range(n):
        moves.append(
            (
                frames[k].at[rows(meta[me ^ k, n + me], length)],
                residual.at[rows(me ^ k, length)],
            )
        )
    for m in range(n):
        lanes = pl.ds(pl.multiple_of((me ^ m) * channels, channels), channels)
        for k in range(n):
            cols = pl.ds(k * channels, channels)
            if m < n - 1:
                source = pieces[m].at[:, cols]
            else:
                source = below.at[pl.ds(n * length, length), cols]
            moves.append((source, cat.at[rows(me ^ m ^ k, length), lanes]))
    copies = [
        pltpu.make_async_copy(source, target, sems.at[i])
        for i, (source, target) in enumerate(moves)
    ]
    for copy in copies:
        copy.start()
    for copy in copies:
        copy.wait()
    span = 512
    for start in range(0, cat.shape[1], span):
        cols = slice(start, start + span)
        term = jnp.dot(cat[...], weight[:, cols], preferred_element_type=F32)
        out_ref[:, cols] = (residual[:, cols].astype(F32) + term).astype(BF16)


def encode_call(ints, pieces, below, frames, blocks, packs, length):
    n = len(frames)
    width = blocks[0].shape[2]
    owned = width // len(packs)
    halves = width // packs[0].shape[1]
    anywhere = pl.BlockSpec(memory_space=pl.ANY)
    return pl.pallas_call(
        functools.partial(encode_kernel, (n, length, owned)),
        out_shape=jax.ShapeDtypeStruct((n * length, width), BF16),
        in_specs=[in_smem()] + [anywhere] * (2 * n + len(blocks) + len(packs)),
        out_specs=in_vmem(),
        scratch_shapes=[
            pltpu.VMEM((n * length, width), BF16),
            pltpu.VMEM((width, width), BF16),
            pltpu.VMEM((n * length, width), BF16),
            pltpu.SemaphoreType.DMA((len(packs) * (n - 1 + halves) + n + n * n,)),
        ],
        compiler_params=vmem_params(VMEM_ENCODE),
        cost_estimate=LIGHT,
        name="encode",
    )(ints, *frames, *pieces, below, *blocks, *packs)


def frame_grad_kernel(n, x_ref, g_ref, gain_ref, *refs):
    out_ref = refs[n]
    x = x_ref[...].astype(F32)
    centred = x - jnp.mean(x, axis=1, keepdims=True)
    inverse = lax.rsqrt(jnp.mean(centred * centred, axis=1, keepdims=True) + EPS)
    standard = centred * inverse
    grad = sum(ref[...].astype(F32) for ref in refs[:n]) * gain_ref[...]
    grad_in = inverse * (
        grad
        - jnp.mean(grad, axis=1, keepdims=True)
        - standard * jnp.mean(grad * standard, axis=1, keepdims=True)
    )
    out_ref[...] = (g_ref[...].astype(F32) + grad_in).astype(BF16)


def frame_grad_call(x, g, gain, returned):
    count, length, width = x.shape
    rows = count * length
    step = 64
    block = pl.BlockSpec((step, width), lambda s: (s, 0))
    out = pl.pallas_call(
        functools.partial(frame_grad_kernel, len(returned)),
        out_shape=jax.ShapeDtypeStruct((rows, width), BF16),
        grid=(rows // step,),
        in_specs=[block, block, pl.BlockSpec((1, width), lambda s: (0, 0))]
        + [block] * len(returned),
        out_specs=block,
        compiler_params=vmem_params(VMEM_FRAME),
        cost_estimate=LIGHT,
        name="frame_grad",
    )(x.reshape(rows, width), g.reshape(rows, width), gain, *returned)
    return out.reshape(count, length, width)


def unpack_kernel(dims, *refs):
    n, owned, part, half = dims
    blocks, (weight_ref, before, gain_ref) = refs[:n], refs[n : n + 3]
    expand_ref, project_ref, gain_out, cat, grads, project, sems = refs[-7:]
    channels = blocks[0].shape[1]
    width = cat.shape[1]
    wide = 2 * channels
    halves = width // wide
    me = lax.axis_index("dp")
    for k in range(n):
        cat[:, pl.ds(pl.multiple_of((me ^ k) * channels, channels), channels)] = blocks[k][:owned]
        rows = pl.ds(pl.multiple_of((me ^ k) * part, part), part)
        for h in range(halves):
            project[h, rows, :] = blocks[k][owned + h * part : owned + (h + 1) * part].astype(F32)
    copies = [
        pltpu.make_async_copy(
            project.at[h],
            project_ref.at[:, pl.ds(h * wide + half * channels, channels)],
            sems.at[0, h],
        )
        for h in range(halves)
    ]
    for copy in copies:
        copy.start()
    along = before[...]
    span = 512
    for i, start in enumerate(range(0, width, span)):
        row = lax.broadcasted_iota(jnp.int32, (width, span), 0)
        col = lax.broadcasted_iota(jnp.int32, (1, span), 1) + start
        place = col % owned // part * channels + col // owned * part + col % part
        spread = jnp.where(row == place, 1.0, 0.0).astype(BF16)
        grad = jnp.dot(cat[...], spread, preferred_element_type=F32)
        grads[i] = grad
        copy = pltpu.make_async_copy(
            grads.at[i],
            expand_ref.at[:, pl.ds(half * width + start, span)],
            sems.at[1, i],
        )
        copy.start()
        copies.append(copy)
        along += jnp.sum(
            grad * weight_ref[:, start : start + span].astype(F32), axis=1, keepdims=True
        )
    if half == 0:
        gain_out[...] = along
    else:
        row = jnp.transpose(jnp.broadcast_to(along, (owned, LANES)))[:1]
        gain_out[...] = row / gain_ref[...].astype(F32)
    for copy in copies:
        copy.wait()


def unpack_call(half, blocks, weight, before, gain, outputs, owned, part, width):
    n = len(blocks)
    channels = blocks[0].shape[1]
    halves = width // (2 * channels)
    anywhere = pl.BlockSpec(memory_space=pl.ANY)
    return pl.pallas_call(
        functools.partial(unpack_kernel, (n, owned, part, half)),
        out_shape=(
            jax.ShapeDtypeStruct((owned, 2 * width), F32),
            jax.ShapeDtypeStruct((owned, width), F32),
            jax.ShapeDtypeStruct((1, owned) if half else (owned, 1), F32),
        ),
        grid=(1,),
        in_specs=[in_vmem()] * n
        + [pl.BlockSpec((owned, width), lambda s: (0, half)), in_vmem(), in_vmem()]
        + [anywhere] * len(outputs),
        out_specs=(anywhere, anywhere, in_vmem()),
        scratch_shapes=[
            pltpu.VMEM((owned, width), BF16),
            pltpu.VMEM((width // 512, owned, 512), F32),
            pltpu.VMEM((halves, owned, channels), F32),
            pltpu.SemaphoreType.DMA((2, max(halves, width // 512))),
        ],
        input_output_aliases={n + 3 + i: i for i in range(len(outputs))},
        compiler_params=vmem_params(VMEM_UNPACK),
        cost_estimate=LIGHT,
        name="unpack",
    )(*blocks, weight, before, gain, *outputs)


def tie(value, *after):
    return lax.optimization_barrier((value,) + after)[0]


def gather_owners(x):
    blocks = [x] + [swap(x, "shard", 8, 2 * m) for m in (1, 2, 3)]
    return blocks + [swap(block, "shard", 8, 1) for block in blocks]


def add_cores_kernel(keep_hbm, got_hbm, *refs):
    n = len(refs) - 3
    outs, (keep, got, sems) = refs[:n], refs[n:]
    chip = lax.axis_index("shard") // 2
    move = pltpu.make_async_copy
    order = list(range(1, n)) + [0]
    inward = [
        (
            move(keep_hbm.at[chip ^ m], keep.at[m], sems.at[m, 0]),
            move(got_hbm.at[chip ^ m], got.at[m], sems.at[m, 1]),
        )
        for m in range(n)
    ]
    outward = [move(keep.at[m], outs[m], sems.at[m, 2]) for m in range(n)]
    for m in order:
        for copy in inward[m]:
            copy.start()
    for m in order:
        for copy in inward[m]:
            copy.wait()
        keep[m] = (keep[m].astype(F32) + got[m].astype(F32)).astype(BF16)
        outward[m].start()
    for copy in outward:
        copy.wait()


def add_cores(keep, got):
    n = keep.shape[0]
    anywhere = pl.BlockSpec(memory_space=pl.ANY)
    return pl.pallas_call(
        add_cores_kernel,
        out_shape=(jax.ShapeDtypeStruct(keep.shape[1:], BF16),) * n,
        in_specs=[anywhere] * 2,
        out_specs=(anywhere,) * n,
        scratch_shapes=[
            pltpu.VMEM(keep.shape, BF16),
            pltpu.VMEM(keep.shape, BF16),
            pltpu.SemaphoreType.DMA((n, 3)),
        ],
        compiler_params=vmem_params(VMEM_HOP),
        cost_estimate=LIGHT,
        name="add_cores",
    )(keep, got)


def add_chips_kernel(n, *refs):
    total = sum(ref[...].astype(F32) for ref in refs[:n]).astype(BF16)
    channels = refs[n].shape[1]
    for half, ref in enumerate(refs[n:]):
        ref[...] = total[:, half * channels : (half + 1) * channels]


def add_chips(come):
    rows, wide = come[0].shape
    return pl.pallas_call(
        functools.partial(add_chips_kernel, len(come)),
        out_shape=(jax.ShapeDtypeStruct((rows, wide // 2), BF16),) * 2,
        in_specs=[in_vmem()] * len(come),
        out_specs=(in_vmem(),) * 2,
        compiler_params=vmem_params(VMEM_HOP),
        cost_estimate=LIGHT,
        name="add_chips",
    )(*come)


def fast_body(
    frames,
    cotangent,
    lengths,
    send_order,
    norm_gain,
    conv_bias,
    kernel,
    expand_weight,
    project_weight,
):
    n_dp, n_shard = lax.axis_size("dp"), lax.axis_size("shard")
    count, length, width = frames.shape
    owned, taps = kernel.shape
    part = owned // n_dp
    wide = 2 * n_shard * part
    rows = count * length
    dims = (count, length, taps)
    x_own = frames.reshape(rows, width)
    g_own = cotangent.reshape(rows, width)
    pack, both, project = pack_call(
        expand_weight, project_weight, kernel, conv_bias, norm_gain, x_own, g_own, part, wide
    )
    ints = jnp.concatenate([lengths, send_order])
    ints = lax.all_to_all(jnp.broadcast_to(ints, (n_dp, 2 * count)), "dp", 0, 0, tiled=True)
    pack, both, ints = lax.optimization_barrier((pack, both, ints))
    both_x = swap(both, "dp", 4, 1)
    both_y = swap(both, "dp", 4, 2)
    packs = [pack] + [swap(pack, "shard", 8, 2 * m) for m in (1, 2, 3)]
    *packs, both_x, both_y = lax.optimization_barrier((*packs, both_x, both_y))
    packs += [swap(block, "shard", 8, 1) for block in packs]
    x_all = [x_own, both_x, both_y, swap(both_x[:rows], "dp", 4, 2)]
    g_all = [g_own, both_x, both_y, swap(both_y[rows:], "dp", 4, 1)]
    line = [[2 * c + i for c in range(n_shard // 2)] for i in range(2)]
    project = tie(project, *packs[1:4])
    project = lax.all_to_all(project, "shard", 0, 0, axis_index_groups=line, tiled=True)

    near = near_call(ints, x_all[:3], g_all[:3], packs, owned, dims)
    returned = [near[3]] + [swap(near[3 + k], "dp", n_dp, k) for k in (1, 2)]
    gain = near[7]
    far = far_call(ints, x_all[3], near[:3] + near[6:7], g_all, packs, owned, dims)

    keep, give = lax.optimization_barrier((*far[1:3], project, *returned[1:3]))[:2]
    sums = add_cores(keep, swap(give, "shard", 8, 1))
    come = [sums[0]] + [swap(sums[m], "shard", 8, 2 * m) for m in (1, 2, 3)]
    below, *single = lax.optimization_barrier((far[0], *far[4:], sums[1]))[:-1]
    single = [swap(piece, "dp", n_dp, 1 + i) for i, piece in enumerate(single)]
    returned.append(swap(below, "dp", n_dp, 3))
    project = [project, swap(tie(project, sums[1]), "shard", 8, 1)]
    pieces = [tie(far[3], come[1])] + single
    encoded = encode_call(ints, pieces, returned[3], x_all, project, packs, length)
    frame_grad = frame_grad_call(frames, tie(cotangent, come[1]), gain, returned)
    come[0] = tie(come[0], encoded, frame_grad)

    come[0] = tie(come[0], encoded, frame_grad)
    gathered = [[half] + [swap(half, "dp", 4, k) for k in (1, 2, 3)] for half in add_chips(come)]
    base = owned + width // wide * part
    table = jnp.stack([a[base:] for a in gathered[0]])
    table = jnp.take(table, lax.axis_index("dp") ^ jnp.arange(n_dp), axis=0).astype(F32)
    table = jnp.concatenate([table[:, :, :part], table[:, :, LANES : LANES + part]], axis=1)
    table = table.transpose(0, 2, 1).reshape(owned, taps + 1)
    outputs, along = (), jnp.zeros((owned, 1), F32)
    for half in range(2):
        *outputs, along = unpack_call(
            half, gathered[half], expand_weight, along, norm_gain[None], outputs, owned, part, width
        )
    expand_grad, project_grad = outputs
    return (
        encoded.reshape(frames.shape),
        frame_grad,
        along.reshape(owned),
        table[:, taps],
        table[:, :taps],
        expand_grad,
        project_grad,
    )


def depthwise(signal, taps_table):
    taps = taps_table.shape[0]
    half = (taps - 1) // 2
    length = signal.shape[1]
    padded = jnp.pad(signal, ((0, 0), (half, half), (0, 0)))
    result = jnp.zeros_like(signal)
    for offset in range(taps):
        result = result + padded[:, offset : offset + length, :] * taps_table[offset]
    return result


def kernel_terms(signal, upstream, taps):
    half = (taps - 1) // 2
    length = signal.shape[1]
    padded = jnp.pad(signal, ((0, 0), (half, half), (0, 0)))
    rows = []
    for offset in range(taps):
        rows.append(jnp.sum(padded[:, offset : offset + length, :] * upstream, axis=(0, 1)))
    return jnp.stack(rows, axis=0)


def chunk_compute(x, g, live, gain, taps, bias, expand_slice, project_slice):
    count, length, width = x.shape
    rows = count * length
    channels = taps.shape[1]
    inputs = x.reshape(rows, width).astype(F32)
    live_rows = live.reshape(rows, 1)
    centred = inputs - jnp.mean(inputs, axis=1, keepdims=True)
    variance = jnp.mean(centred * centred, axis=1, keepdims=True)
    standard = centred * lax.rsqrt(variance + EPS)
    normed = (standard * gain).astype(BF16)
    expanded = jnp.dot(normed, expand_slice, preferred_element_type=F32)
    value = expanded[:, :channels]
    gate = jax.nn.sigmoid(expanded[:, channels:])
    glu = (value * gate * live_rows).astype(BF16).astype(F32).reshape(count, length, channels)
    conv = depthwise(glu, taps).reshape(rows, channels) + bias
    conv_sig = jax.nn.sigmoid(conv)
    swished = (conv * conv_sig).astype(BF16)
    masked = (g.reshape(rows, width).astype(F32) * live_rows).astype(BF16)
    grad_swish = lax.dot_general(
        masked, project_slice, (((1,), (1,)), ((), ())), preferred_element_type=F32
    )
    grad_conv = grad_swish * conv_sig * (1.0 + conv * (1.0 - conv_sig))
    bias_part = jnp.sum(grad_conv, axis=0)
    volume = grad_conv.reshape(count, length, channels)
    kernel_part = kernel_terms(glu, volume, taps.shape[0])
    grad_glu = depthwise(volume, taps[::-1]).reshape(rows, channels) * live_rows
    grad_expanded = jnp.concatenate(
        [grad_glu * gate, grad_glu * value * gate * (1.0 - gate)], axis=1
    ).astype(BF16)
    grad_normed = lax.dot_general(
        grad_expanded, expand_slice, (((1,), (1,)), ((), ())), preferred_element_type=F32
    )
    gain_part = jnp.sum(grad_normed * standard, axis=0)
    return normed, masked, swished, grad_expanded, grad_normed.astype(BF16), (
        gain_part,
        bias_part,
        kernel_part,
    )


def swap(x, axis, size, k):
    return lax.ppermute(x, axis, [(p, p ^ k) for p in range(size)])


def gather_dp(x, n_dp):
    if n_dp == 4:
        half = x.shape[0] // 2
        along_x = swap(x, "dp", 4, 1)
        along_y = swap(x, "dp", 4, 2)
        far = jnp.concatenate(
            [swap(along_x[:half], "dp", 4, 2), swap(along_y[half:], "dp", 4, 1)], axis=0
        )
        return [x, along_x, along_y, far]
    return [x] + [swap(x, "dp", n_dp, k) for k in range(1, n_dp)]


def gather_shard(x, n_shard):
    if n_shard == 8:
        me = lax.axis_index("shard")
        chip, core = me // 2, me % 2
        blocks = [x] + [
            lax.ppermute(x, "shard", [(p, (p + 2 * k) % 8) for p in range(8)]) for k in (1, 2, 3)
        ]
        mine = jnp.stack(blocks)
        mine = jnp.take(mine, (chip - jnp.arange(4)) % 4, axis=0)
        other = swap(mine, "shard", 8, 1)
        pair = jnp.where(core == 0, jnp.stack([mine, other], 1), jnp.stack([other, mine], 1))
        return pair.reshape((8,) + x.shape)
    return lax.all_gather(x, "shard", axis=0)


def reduce_shard(x, n_shard):
    x = x.astype(BF16)
    if n_shard == 8:
        me = lax.axis_index("shard")
        chip, core = me // 2, me % 2
        cube = x.reshape((4, 2) + x.shape[1:])
        keep = jnp.take(cube, core, axis=1)
        give = jnp.take(cube, 1 - core, axis=1)
        both = (keep.astype(F32) + swap(give, "shard", 8, 1).astype(F32)).astype(BF16)
        total = jnp.take(both, chip, axis=0).astype(F32)
        for k in (1, 2, 3):
            piece = jnp.take(both, (chip + k) % 4, axis=0)
            total = total + lax.ppermute(
                piece, "shard", [(p, (p + 2 * k) % 8) for p in range(8)]
            ).astype(F32)
        return total
    return lax.psum_scatter(x, "shard", scatter_dimension=0, tiled=False).astype(F32)


def generic_body(
    frames,
    cotangent,
    lengths,
    send_order,
    norm_gain,
    conv_bias,
    kernel,
    expand_weight,
    project_weight,
):
    n_dp, n_shard = lax.axis_size("dp"), lax.axis_size("shard")
    count, length, width = frames.shape
    per_peer = count // n_dp
    owned, taps = kernel.shape
    part = owned // n_dp
    channels = n_shard * part
    me = lax.axis_index("dp")

    x_own = jnp.take(frames, send_order, axis=0)
    g_own = jnp.take(cotangent, send_order, axis=0)
    len_own = jnp.take(lengths, send_order, axis=0)

    expand_cols = lax.dynamic_index_in_dim(
        expand_weight.reshape(owned, 2, n_shard, n_dp, part), me, axis=3, keepdims=False
    ).reshape(owned, 2 * channels)
    project_rows = lax.dynamic_slice_in_dim(project_weight, me * part, part, axis=0)
    small = jnp.concatenate(
        [
            lax.dynamic_slice_in_dim(kernel, me * part, part, axis=0).reshape(-1),
            lax.dynamic_slice_in_dim(conv_bias, me * part, part, axis=0),
            norm_gain,
        ]
    )
    wide = 2 * channels
    small_rows = 16
    small = jnp.pad(small, (0, small_rows * wide - small.shape[0])).reshape(small_rows, wide)
    n_halves = width // wide
    pack = jnp.concatenate(
        [expand_cols] + [project_rows[:, h * wide : (h + 1) * wide] for h in range(n_halves)] + [small], axis=0
    )
    packs = gather_shard(pack, n_shard)
    expand_slice = packs[:, :owned].reshape(width, wide)
    project_slice = jnp.concatenate(
        [
            packs[:, owned + h * part : owned + (h + 1) * part].reshape(channels, wide)
            for h in range(n_halves)
        ],
        axis=1,
    )
    small_all = packs[:, owned + n_halves * part :].reshape(n_shard, -1).astype(F32)
    taps_table = small_all[:, : part * taps].reshape(channels, taps).T
    bias = small_all[:, part * taps : part * (taps + 1)].reshape(channels)
    gain = small_all[:, part * (taps + 1) : part * (taps + 1) + owned].reshape(width)
    project_full = gather_shard(project_weight, n_shard).reshape(n_shard, n_dp, part, width)

    x_all = gather_dp(x_own, n_dp)
    g_all = gather_dp(g_own, n_dp)
    len_all = [len_own] + [swap(len_own, "dp", n_dp, k) for k in range(1, n_dp)]

    normeds, maskeds, swisheds, grad_expandeds, returned = [], [], [], [], []
    sums = None
    positions = lax.broadcasted_iota(jnp.int32, (count, length), 1)
    for k in range(n_dp):
        live = (positions < len_all[k][:, None]).astype(F32)
        normed, masked, swished, grad_expanded, grad_normed, parts = chunk_compute(
            x_all[k], g_all[k], live, gain, taps_table, bias, expand_slice, project_slice
        )
        normeds.append(normed)
        maskeds.append(masked)
        swisheds.append(swished.reshape(n_dp, per_peer, length, channels))
        grad_expandeds.append(grad_expanded)
        returned.append(grad_normed if k == 0 else swap(grad_normed, "dp", n_dp, k))
        sums = parts if sums is None else tuple(a + b for a, b in zip(sums, parts))

    stack = jnp.stack(swisheds)
    total = None
    for m in range(n_dp):
        piece = lax.dynamic_index_in_dim(stack, me ^ m, axis=1, keepdims=False)
        if m:
            piece = swap(piece, "dp", n_dp, m)
        piece = jnp.stack([piece[k ^ m] for k in range(n_dp)])
        rows = lax.dynamic_index_in_dim(project_full, me ^ m, axis=1, keepdims=False)
        term = jnp.dot(
            piece.reshape(count * length, channels),
            rows.reshape(channels, width),
            preferred_element_type=F32,
        )
        total = term if total is None else total + term
    mine = jnp.stack(
        [
            lax.dynamic_slice_in_dim(x_all[k], me * per_peer, per_peer, axis=0)
            for k in range(n_dp)
        ]
    )
    len_mine = jnp.stack(
        [
            lax.dynamic_slice_in_dim(len_all[k], me * per_peer, per_peer, axis=0)
            for k in range(n_dp)
        ]
    )
    live_mine = (positions < len_mine.reshape(count, 1)).astype(F32)
    encoded = (
        mine.reshape(count, length, width).astype(F32)
        + total.reshape(count, length, width) * live_mine[:, :, None]
    ).astype(BF16)
    encoded = jnp.take(
        encoded.reshape(n_dp, per_peer, length, width), me ^ jnp.arange(n_dp), axis=0
    ).reshape(count, length, width)

    grad_normed = sum(piece.astype(F32) for piece in returned)
    inputs = x_own.reshape(count * length, width).astype(F32)
    centred = inputs - jnp.mean(inputs, axis=1, keepdims=True)
    variance = jnp.mean(centred * centred, axis=1, keepdims=True)
    inverse = lax.rsqrt(variance + EPS)
    standard = centred * inverse
    grad_standard = grad_normed * gain
    grad_inputs = inverse * (
        grad_standard
        - jnp.mean(grad_standard, axis=1, keepdims=True)
        - standard * jnp.mean(grad_standard * standard, axis=1, keepdims=True)
    )
    frame_sorted = (g_own.reshape(count * length, width).astype(F32) + grad_inputs).astype(BF16)
    back = jnp.argmax(
        send_order[None, :] == jnp.arange(count, dtype=jnp.int32)[:, None], axis=1
    )
    frame_grad = jnp.take(frame_sorted.reshape(count, length, width), back, axis=0)

    expand_part = sum(
        lax.dot_general(a, b, (((0,), (0,)), ((), ())), preferred_element_type=F32)
        for a, b in zip(normeds, grad_expandeds)
    )
    project_part = sum(
        lax.dot_general(
            a.reshape(-1, channels), b, (((0,), (0,)), ((), ())), preferred_element_type=F32
        )
        for a, b in zip(swisheds, maskeds)
    )
    gain_part, bias_part, kernel_part = sums
    small_part = jnp.concatenate(
        [
            kernel_part.T.reshape(n_shard, part * taps),
            bias_part.reshape(n_shard, part),
            gain_part.reshape(n_shard, owned),
        ],
        axis=1,
    )
    small_part = jnp.pad(small_part, ((0, 0), (0, small_rows * wide - small_part.shape[1])))
    project_part = project_part.reshape(n_shard, part, width)
    grad_pack = jnp.concatenate(
        [expand_part.reshape(n_shard, owned, wide)]
        + [project_part[:, :, h * wide : (h + 1) * wide] for h in range(n_halves)]
        + [small_part.reshape(n_shard, small_rows, wide)],
        axis=1,
    )
    reduced = reduce_shard(grad_pack, n_shard).astype(BF16)
    gathered = jnp.stack(gather_dp(reduced, n_dp))
    gathered = jnp.take(gathered, me ^ jnp.arange(n_dp), axis=0).astype(F32)
    expand_grad = (
        gathered[:, :owned]
        .reshape(n_dp, owned, 2, n_shard, part)
        .transpose(1, 2, 3, 0, 4)
        .reshape(owned, 2 * width)
    )
    project_grad = jnp.concatenate(
        [
            gathered[:, owned + h * part : owned + (h + 1) * part].reshape(owned, wide)
            for h in range(n_halves)
        ],
        axis=1,
    )
    small_grad = gathered[:, owned + n_halves * part :].reshape(n_dp, -1)
    kernel_grad = small_grad[:, : part * taps].reshape(owned, taps)
    bias_grad = small_grad[:, part * taps : part * (taps + 1)].reshape(owned)
    gain_grad = jnp.sum(small_grad[:, part * (taps + 1) : part * (taps + 1) + owned], axis=0)
    return encoded, frame_grad, gain_grad, bias_grad, kernel_grad, expand_grad, project_grad


def body(*arrays):
    fast = lax.axis_size("dp") == 4 and lax.axis_size("shard") == 8
    return (fast_body if fast else generic_body)(*arrays)


def solution(mesh):
    return jax.shard_map(
        body,
        mesh=mesh,
        in_specs=(
            P(("dp", "shard"), None, None),
            P(("dp", "shard"), None, None),
            P(("dp", "shard")),
            P(("dp", "shard")),
            P("shard"),
            P("shard"),
            P("shard", None),
            P("shard", None),
            P("shard", None),
        ),
        out_specs=(
            P(("dp", "shard"), None, None),
            P(("dp", "shard"), None, None),
            P("shard"),
            P("shard"),
            P("shard", None),
            P("shard", None),
            P("shard", None),
        ),
        check_vma=False,
    )
```

```python
import functools

import jax
import jax.numpy as jnp
from jax import lax
from jax.experimental import pallas as pl
from jax.experimental.pallas import tpu as pltpu
from jax.sharding import PartitionSpec as P

EPS = 1e-05
F32 = jnp.float32
BF16 = jnp.bfloat16
LANES = 128
MARGIN = 16
NT = (((1,), (1,)), ((), ()))
TN = (((0,), (0,)), ((), ()))
VMEM_PACK = 63
VMEM_CHUNK = 63
VMEM_ENCODE = 63
VMEM_FRAME = 63
VMEM_HOP = 63
VMEM_UNPACK = 28
LIGHT = pl.CostEstimate(flops=1, bytes_accessed=1, transcendentals=0)


def route(dims, sw, meta, s, base, targets, sems):
    count, length, taps = dims
    me = lax.axis_index("dp")
    copies = []
    for i, (q, target) in enumerate(targets):
        chosen = base + length * meta[me ^ s, count + (me ^ q)]
        source = sw.at[pl.ds(pl.multiple_of(chosen, length), length)]
        copies.append(pltpu.make_async_copy(source, target, sems.at[i]))
    return copies


def one_source(dims, refs, meta, s, base, ready):
    count, length, taps = dims
    rows = count * length
    we, ab, pad, gpad, slope = (refs[n] for n in ("we", "ab", "pad", "gpad", "slope"))
    normed, sw, ge, taps_ref, small = (refs[n] for n in ("normed", "sw", "ge", "taps", "small"))
    width, wide = we.shape
    channels = wide // 2
    tiles = channels // LANES
    own = pl.ds(base, rows)
    step = 256
    ready("tables")
    gain = refs["gain"][...]
    ready("x")

    @pl.loop(0, rows // step)
    def _(index):
        at = pl.ds(pl.multiple_of(base + index * step, step), step)
        x = refs["x"][at, :].astype(F32)
        centred = x - jnp.mean(x, axis=1, keepdims=True)
        variance = jnp.mean(centred * centred, axis=1, keepdims=True)
        normed[at, :] = (centred * lax.rsqrt(variance + EPS) * gain).astype(BF16)

    ready("we")
    expanded = jnp.dot(normed[own, :], we[...], preferred_element_type=F32)
    for tile in range(2 * tiles):
        ab[tile] = expanded[:, tile * LANES : (tile + 1) * LANES]

    first = (taps - 1) // 2
    positions = lax.broadcasted_iota(jnp.int32, (length, LANES), 0)
    source = lax.axis_index("dp") ^ s

    @pl.loop(0, count)
    def _(u):
        at = pl.ds(pl.multiple_of(u * length, length), length)
        out = pl.ds(pl.multiple_of(base + u * length, length), length)
        live = positions < meta[source, u]
        for tile in range(tiles):
            lanes = pl.ds(tile * LANES, LANES)
            gate = jax.nn.sigmoid(ab[tiles + tile, at, :])
            glu = jnp.where(live, ab[tile, at, :] * gate, 0.0).astype(BF16).astype(F32)
            pad[u, tile, MARGIN : MARGIN + length, :] = glu
            ab[tiles + tile, at, :] = gate
            conv = jnp.broadcast_to(taps_ref[taps : taps + 1, lanes], (length, LANES))
            for t in range(taps):
                conv += taps_ref[t : t + 1, lanes] * pad[u, tile, pl.ds(MARGIN - first + t, length), :]
            sig = jax.nn.sigmoid(conv)
            sw[out, lanes] = jnp.where(live, conv * sig, 0.0).astype(BF16)
            slope[u, tile] = jnp.where(live, sig * (1.0 + conv * (1.0 - sig)), 0.0)

    for copy in refs["route"](s, base):
        copy.start()

    ready("g")
    ready("wp")
    grad_swish = lax.dot_general(
        refs["g"][own, :], refs["wp"][...], NT, preferred_element_type=F32
    )
    for u in range(count):
        for tile in range(tiles):
            gpad[u, tile, MARGIN : MARGIN + length, :] = (
                grad_swish[u * length : (u + 1) * length, tile * LANES : (tile + 1) * LANES]
                * slope[u, tile]
            )

    def fold(value):
        return jnp.sum(value.reshape(length // 8, 8, LANES), axis=0)

    @pl.loop(0, count)
    def _(u):
        at = pl.ds(pl.multiple_of(u * length, length), length)
        out = pl.ds(pl.multiple_of(base + u * length, length), length)
        live = positions < meta[source, u]
        for tile in range(tiles):
            lanes = pl.ds(tile * LANES, LANES)
            grad_conv = gpad[u, tile, MARGIN : MARGIN + length, :]
            grad_glu = jnp.zeros((length, LANES), F32)
            for t in range(taps):
                small[tile, t] += fold(
                    pad[u, tile, pl.ds(MARGIN - first + t, length), :] * grad_conv
                )
                grad_glu += (
                    taps_ref[t : t + 1, lanes] * gpad[u, tile, pl.ds(MARGIN + first - t, length), :]
                )
            small[tile, taps] += fold(grad_conv)
            grad_glu = jnp.where(live, grad_glu, 0.0)
            gate = ab[tiles + tile, at, :]
            through = grad_glu * gate
            ge[out, lanes] = through.astype(BF16)
            ge[out, pl.ds(channels + tile * LANES, LANES)] = (
                through * ab[tile, at, :] * (1.0 - gate)
            ).astype(BF16)

    span = 768
    for start in range(0, width, span):
        cols = pl.ds(start, span)
        refs["gn"][own, cols] = lax.dot_general(
            ge[own, :], we[cols, :], NT, preferred_element_type=F32
        ).astype(BF16)


def clear_margins(*padded):
    for ref in padded:
        count, tiles, height, lanes = ref.shape
        zeros = jnp.zeros((MARGIN, lanes), F32)
        for u in range(count):
            for tile in range(tiles):
                ref[u, tile, :MARGIN, :] = zeros
                ref[u, tile, height - MARGIN :, :] = zeros


def source_scratch(count, length, channels):
    tiles = channels // LANES
    padded = pltpu.VMEM((count, tiles, length + 2 * MARGIN, LANES), F32)
    return [
        pltpu.VMEM((2 * tiles, count * length, LANES), F32),
        padded,
        padded,
        pltpu.VMEM((count, tiles, length, LANES), F32),
    ]


def weight_copies(blocks, owned, part, we, wp, small, sems):
    me = lax.axis_index("shard")
    width, wide = we.shape
    halves = width // wide
    move = pltpu.make_async_copy
    tables, first, second = [], [], []
    for b, block in enumerate(blocks):
        offset = 2 * (b % (len(blocks) // 2)) + b // (len(blocks) // 2)
        owner = me ^ offset
        tables.append(
            move(block.at[pl.ds(owned + halves * part, 16)], small.at[owner], sems.at[b, 0])
        )
        rows = pl.ds(pl.multiple_of(owner * owned, owned), owned)
        first.append(move(block.at[pl.ds(0, owned)], we.at[rows], sems.at[b, 1]))
        rows = pl.ds(pl.multiple_of(owner * part, part), part)
        for h in range(halves):
            second.append(
                move(
                    block.at[pl.ds(owned + h * part, part)],
                    wp.at[rows, pl.ds(h * wide, wide)],
                    sems.at[b, 2 + h],
                )
            )
    return dict(tables=tables, we=first, wp=second)


def fill_tables(small, owned, part, taps_ref, gain_ref):
    rows = [small[j].astype(F32) for j in range(small.shape[0])]
    taps_ref[:16] = jnp.concatenate([r[:, :part] for r in rows], axis=1)
    taps_ref[16:] = jnp.concatenate([r[:, LANES : LANES + part] for r in rows], axis=1)
    gain_ref[...] = jnp.concatenate([r[:1, 2 * LANES : 2 * LANES + owned] for r in rows], axis=1)


def weight_scratch(owners, owned, width, wide, taps):
    return [
        pltpu.VMEM((width, wide), BF16),
        pltpu.VMEM((wide // 2, width), BF16),
        pltpu.VMEM((owners, 16, wide), BF16),
        pltpu.VMEM((taps + 1, wide // 2), F32),
        pltpu.SemaphoreType.DMA((owners, 2 + width // wide)),
    ]


def near_kernel(dims, n, owned, meta, *refs):
    count, length, taps = dims
    rows = count * length
    x_hbm, g_hbm, refs = refs[:n], refs[n : 2 * n], refs[2 * n :]
    outs = refs[-24 - n : -19]
    blocks = refs[: -24 - n]
    normed_hbm, sw_hbm, ge_hbm = outs[:3]
    gn_hbm, small, gain_ref = outs[3 : 3 + n], outs[3 + n], outs[4 + n]
    x, normed, g, sw, ge, gn, ab, pad, gpad, slope = refs[-19:-9]
    we, wp, shares, taps_ref, weight_sems = refs[-9:-4]
    in_sems, out_sems, route_sems, _ = refs[-4:]
    part = owned * (we.shape[1] // 2) // we.shape[0]
    move = pltpu.make_async_copy

    def place(s):
        return pl.ds(s * rows, rows)

    incoming = {}
    for s in range(n):
        incoming["x", s] = move(x_hbm[s].at[pl.ds(0, rows)], x.at[place(s)], in_sems.at[s, 0])
        incoming["g", s] = move(
            g_hbm[s].at[pl.ds(g_hbm[s].shape[0] - rows, rows)], g.at[place(s)], in_sems.at[s, 1]
        )
    weights = weight_copies(blocks, owned, part, we, wp, shares, weight_sems)
    for copy in weights["tables"]:
        copy.start()
    incoming["x", 0].start()
    for copy in weights["we"]:
        copy.start()
    incoming["g", 0].start()
    for copy in weights["wp"]:
        copy.start()
    for s in range(1, n):
        incoming["x", s].start()
        incoming["g", s].start()
    clear_margins(pad, gpad)
    small[...] = jnp.zeros_like(small)
    views = dict(
        x=x, normed=normed, g=g, we=we, wp=wp, sw=sw, ge=ge, gn=gn, ab=ab, pad=pad, gpad=gpad,
        slope=slope, taps=taps_ref, gain=gain_ref, small=small, route=lambda s, base: [],
    )

    @pl.loop(0, n)
    def _(s):
        def ready(what):
            if what in weights:
                @pl.when(s == 0)
                def _():
                    for copy in weights[what]:
                        copy.wait()
                    if what == "tables":
                        fill_tables(shares, owned, part, taps_ref, gain_ref)
            else:
                for at in range(n):
                    @pl.when(s == at)
                    def _():
                        incoming[what, at].wait()

        base = pl.multiple_of(s * rows, rows)
        one_source(dims, views, meta, s, base, ready)
        own = pl.ds(base, rows)
        for i, (source, target) in enumerate(((normed, normed_hbm), (sw, sw_hbm), (ge, ge_hbm))):
            move(source.at[own], target.at[own], out_sems.at[s, i]).start()
        for at in range(n):
            @pl.when(s == at)
            def _():
                move(gn.at[place(at)], gn_hbm[at], out_sems.at[at, 3]).start()

    for s in range(n):
        for i, (source, target) in enumerate(((normed, normed_hbm), (sw, sw_hbm), (ge, ge_hbm))):
            move(source.at[place(s)], target.at[place(s)], out_sems.at[s, i]).wait()
        move(gn.at[place(s)], gn_hbm[s].at[pl.ds(0, rows)], out_sems.at[s, 3]).wait()


def near_call(ints, xs, gs, blocks, owned, dims):
    count, length, taps = dims
    n = len(xs)
    rows, width = count * length, xs[0].shape[1]
    wide = blocks[0].shape[1]
    channels = wide // 2
    owners = len(blocks)
    anywhere = pl.BlockSpec(memory_space=pl.ANY)
    return pl.pallas_call(
        functools.partial(near_kernel, dims, n, owned),
        out_shape=(
            jax.ShapeDtypeStruct((n * rows, width), BF16),
            jax.ShapeDtypeStruct((n * rows, channels), BF16),
            jax.ShapeDtypeStruct((n * rows, wide), BF16),
        )
        + (jax.ShapeDtypeStruct((rows, width), BF16),) * n
        + (
            jax.ShapeDtypeStruct((channels // LANES, taps + 1, 8, LANES), F32),
            jax.ShapeDtypeStruct((1, width), F32),
        ),
        in_specs=[in_smem()] + [anywhere] * (2 * n + owners),
        out_specs=(anywhere,) * (3 + n) + (in_vmem(), in_vmem()),
        scratch_shapes=[
            pltpu.VMEM((n * rows, width), BF16),
            pltpu.VMEM((n * rows, width), BF16),
            pltpu.VMEM((n * rows, width), BF16),
            pltpu.VMEM((n * rows, channels), BF16),
            pltpu.VMEM((n * rows, wide), BF16),
            pltpu.VMEM((n * rows, width), BF16),
        ]
        + source_scratch(count, length, channels)
        + weight_scratch(owners, owned, width, wide, taps)
        + [
            pltpu.SemaphoreType.DMA((n, 2)),
            pltpu.SemaphoreType.DMA((n, 4)),
            pltpu.SemaphoreType.DMA((n, count)),
            pltpu.SemaphoreType.DMA,
        ],
        compiler_params=vmem_params(VMEM_CHUNK),
        cost_estimate=LIGHT,
        name="near_sources",
    )(ints, *xs, *gs, *blocks)


def far_kernel(dims, n, owned, meta, *refs):
    count, length, taps = dims
    rows = count * length
    core = lax.axis_index("shard") % 2
    x_hbm, normed_hbm, sw_hbm, ge_hbm = refs[:4]
    g_hbm, near_small = refs[4 : 5 + n], refs[5 + n]
    blocks, outs, refs = refs[6 + n : -25 - n], refs[-25 - n : -22], refs[-22:]
    gn_hbm, keep_hbm, give_hbm, own_hbm, single_hbm = *outs[:4], outs[4:]
    x, normed, g, sw, ge, gn, ab, pad, gpad, slope = refs[:10]
    we, wp, shares, taps_ref, weight_sems = refs[10:15]
    gain_ref, small, block, in_sems, out_sems, route_sems, _ = refs[15:]
    width, wide = we.shape
    channels = wide // 2
    tiles = channels // LANES
    chips = width // owned // 2
    halves = width // wide
    part = channels // (2 * chips)
    move = pltpu.make_async_copy
    base = n * rows
    near, last = pl.ds(0, base), pl.ds(base, rows)
    tail = [pl.ds(ref.shape[0] - rows, rows) for ref in g_hbm]
    incoming = dict(
        x=[move(x_hbm.at[pl.ds(0, rows)], x.at[last], in_sems.at[0])],
        g=[move(g_hbm[n].at[tail[n]], g.at[last], in_sems.at[2])],
    )
    incoming.update(weight_copies(blocks, owned, part, we, wp, shares, weight_sems))
    later = [
        move(normed_hbm, normed.at[near], in_sems.at[4]),
        move(sw_hbm, sw.at[near], in_sems.at[5]),
        move(ge_hbm, ge.at[near], in_sems.at[6]),
    ]
    later += [
        move(g_hbm[s].at[tail[s]], g.at[pl.ds(s * rows, rows)], in_sems.at[7 + s])
        for s in range(n)
    ]
    for what in ("tables", "x", "we", "g", "wp"):
        for copy in incoming[what]:
            copy.start()
    for copy in later:
        copy.start()

    def ready(what):
        for copy in incoming[what]:
            copy.wait()
        if what == "tables":
            fill_tables(shares, owned, part, taps_ref, gain_ref)

    clear_margins(pad, gpad)
    small[...] = near_small[...]

    def pieces(s, base):
        cols = pl.ds(s * channels, channels)
        targets = [(0, own_hbm.at[:, cols]), (n, gn_hbm.at[pl.ds(rows, length), cols])]
        targets += [(1 + i, ref.at[:, cols]) for i, ref in enumerate(single_hbm)]
        return route(dims, sw, meta, s, base, targets, route_sems.at[s])

    views = dict(
        x=x, normed=normed, g=g, we=we, wp=wp, sw=sw, ge=ge, gn=gn, ab=ab, pad=pad, gpad=gpad,
        slope=slope, taps=taps_ref, gain=gain_ref, small=small, route=pieces,
    )
    one_source(dims, views, meta, n, base, ready)
    gn_out = move(gn.at[last], gn_hbm.at[pl.ds(0, rows)], out_sems.at[0])
    gn_out.start()
    routed = pieces(n, base)
    for copy in later:
        copy.wait()
    for s in range(n):
        for copy in pieces(s, s * rows):
            copy.start()
            routed.append(copy)

    sums = jnp.sum(small[...], axis=2)
    sums = jnp.concatenate([sums[tile] for tile in range(tiles)], axis=1)
    span = 2 * owned
    bottom = owned + halves * part
    for h in range(halves):
        total = lax.dot_general(
            sw[...], g[:, h * wide : (h + 1) * wide], TN, preferred_element_type=F32
        ).astype(BF16)
        for owner in range(2 * chips):
            block[owner % 2, owner // 2, owned + h * part : owned + (h + 1) * part] = total[
                owner * part : (owner + 1) * part
            ]
    fill = jnp.zeros((16, LANES - part), F32)
    blank = jnp.zeros((16, wide - 2 * LANES), F32)
    for owner in range(2 * chips):
        table = sums[:, owner * part : (owner + 1) * part]
        line = jnp.concatenate([table[:16], fill, table[16:], fill, blank], axis=1)
        block[owner % 2, owner // 2, bottom:] = line.astype(BF16)
    outward = []
    for chip in range(chips):
        total = lax.dot_general(
            normed[:, chip * span : (chip + 1) * span], ge[...], TN, preferred_element_type=F32
        ).astype(BF16)
        for which in range(2):
            block[which, chip, :owned] = total[which * owned : (which + 1) * owned]
        for i, (which, target) in enumerate(((1 - core, give_hbm), (core, keep_hbm))):
            outward.append(
                move(block.at[which, chip], target.at[chip], out_sems.at[1 + 2 * chip + i])
            )
            outward[-1].start()
    for copy in outward + routed + [gn_out]:
        copy.wait()


def far_call(ints, x, near, gs, blocks, owned, dims):
    count, length, taps = dims
    n = len(gs) - 1
    rows = count * length
    width, wide = x.shape[1], blocks[0].shape[1]
    channels = wide // 2
    tiles = channels // LANES
    owners = len(blocks)
    chips = owners // 2
    halves = width // wide
    height = owned + halves * (channels // owners) + 16
    anywhere = pl.BlockSpec(memory_space=pl.ANY)
    normed, sw, ge, small = near
    every = (n + 1) * rows
    return pl.pallas_call(
        functools.partial(far_kernel, dims, n, owned),
        out_shape=(jax.ShapeDtypeStruct((rows + length, width), BF16),)
        + (jax.ShapeDtypeStruct((chips, height, wide), BF16),) * 2
        + (jax.ShapeDtypeStruct((length, width), BF16),)
        + (jax.ShapeDtypeStruct((length, width), BF16),) * (n - 1),
        in_specs=[in_smem()] + [anywhere] * (5 + n) + [in_vmem()] + [anywhere] * owners,
        out_specs=(anywhere,) * (3 + n),
        scratch_shapes=[
            pltpu.VMEM((every, width), BF16),
            pltpu.VMEM((every, width), BF16),
            pltpu.VMEM((every, width), BF16),
            pltpu.VMEM((every, channels), BF16),
            pltpu.VMEM((every, wide), BF16),
            pltpu.VMEM((every, width), BF16),
        ]
        + source_scratch(count, length, channels)
        + weight_scratch(owners, owned, width, wide, taps)
        + [
            pltpu.VMEM((1, width), F32),
            pltpu.VMEM((tiles, taps + 1, 8, LANES), F32),
            pltpu.VMEM((2, chips, height, wide), BF16),
            pltpu.SemaphoreType.DMA((7 + n,)),
            pltpu.SemaphoreType.DMA((1 + 2 * chips,)),
            pltpu.SemaphoreType.DMA((n + 1, count)),
            pltpu.SemaphoreType.DMA,
        ],
        compiler_params=vmem_params(VMEM_CHUNK),
        cost_estimate=LIGHT,
        name="far_source",
    )(ints, x, normed, sw, ge, *gs, small, *blocks)


def vmem_params(mib):
    return pltpu.CompilerParams(vmem_limit_bytes=mib * 1024 * 1024)


def in_vmem():
    return pl.BlockSpec(memory_space=pltpu.VMEM)


def in_smem():
    return pl.BlockSpec(memory_space=pltpu.SMEM)


def owned_column(channel, index, owned, part):
    return (channel // part) * owned + index * part + channel % part


def pack_kernel(expand_hbm, project_hbm, kernel_ref, bias_ref, gain_ref, x_hbm, g_hbm, *refs):
    pack_ref, both_hbm, copies_hbm, both, expand_ref, whole, sems = refs
    rows_in = x_hbm.shape[0]
    inward = [
        pltpu.make_async_copy(x_hbm, both.at[pl.ds(0, rows_in)], sems.at[2, 0]),
        pltpu.make_async_copy(g_hbm, both.at[pl.ds(rows_in, rows_in)], sems.at[3, 0]),
    ]
    owned, width = project_hbm.shape
    wide = pack_ref.shape[1]
    channels = wide // 2
    part = owned * channels // width
    index = lax.axis_index("dp")
    rows = pl.ds(pl.multiple_of(index * part, part), part)
    chips = copies_hbm.shape[0]
    copies = [
        pltpu.make_async_copy(expand_hbm, expand_ref, sems.at[0, 0]),
        pltpu.make_async_copy(project_hbm, whole, sems.at[1, 0]),
    ]
    for copy in inward + copies:
        copy.start()
    row = lax.broadcasted_iota(jnp.int32, (width, channels), 0)
    col = lax.broadcasted_iota(jnp.int32, (1, channels), 1)
    pick = jnp.where(row == owned_column(col, index, owned, part), 1.0, 0.0).astype(BF16)
    mine = lax.broadcasted_iota(jnp.int32, (owned, LANES), 1) + index * part
    mine = jnp.where(lax.broadcasted_iota(jnp.int32, (owned, LANES), 0) == mine, 1.0, 0.0)
    mine = mine.astype(BF16)
    table = jnp.concatenate(
        [
            jnp.dot(kernel_ref[...], mine, preferred_element_type=F32),
            jnp.dot(bias_ref[...].reshape(1, owned), mine, preferred_element_type=F32),
        ],
        axis=0,
    )
    base = owned + width // wide * part
    gain = jnp.broadcast_to(gain_ref[...].reshape(1, owned).astype(F32), (16, owned))
    blank = jnp.zeros((16, wide - 2 * LANES - owned), F32)
    pack_ref[base:, :] = jnp.concatenate(
        [table[:16], table[16:], gain, blank], axis=1
    ).astype(BF16)
    for copy in inward:
        copy.wait()
    outward = [pltpu.make_async_copy(both, both_hbm, sems.at[4, 0])]
    outward[0].start()
    for copy in copies:
        copy.wait()
    for i in range(chips):
        for k in range(1, owned // part):
            outward.append(
                pltpu.make_async_copy(
                    whole.at[pl.ds(pl.multiple_of((index ^ k) * part, part), part)],
                    copies_hbm.at[i, pl.ds((k - 1) * part, part)],
                    sems.at[5 + i, k],
                )
            )
            outward[-1].start()
    block = whole[rows, :]
    for h in range(2):
        pack_ref[:owned, h * channels : (h + 1) * channels] = jnp.dot(
            expand_ref[:, h * width : (h + 1) * width], pick, preferred_element_type=F32
        ).astype(BF16)
    for h in range(width // wide):
        pack_ref[owned + h * part : owned + (h + 1) * part, :] = block[:, h * wide : (h + 1) * wide]
    for copy in outward:
        copy.wait()


def pack_call(expand_weight, project_weight, kernel, bias, gain, x, g, part, wide):
    owned, width = project_weight.shape
    height = owned + width // wide * part + 16
    chips = width // owned // 2
    rows = x.shape[0]
    anywhere = pl.BlockSpec(memory_space=pl.ANY)
    return pl.pallas_call(
        pack_kernel,
        out_shape=(
            jax.ShapeDtypeStruct((height, wide), BF16),
            jax.ShapeDtypeStruct((2 * rows, width), BF16),
            jax.ShapeDtypeStruct((chips, owned - part, width), BF16),
        ),
        in_specs=[anywhere] * 2 + [in_vmem()] * 3 + [anywhere] * 2,
        out_specs=(in_vmem(), anywhere, anywhere),
        scratch_shapes=[
            pltpu.VMEM((2 * rows, width), BF16),
            pltpu.VMEM(expand_weight.shape, BF16),
            pltpu.VMEM((owned, width), BF16),
            pltpu.SemaphoreType.DMA((5 + chips, owned // part)),
        ],
        compiler_params=vmem_params(VMEM_PACK),
        cost_estimate=LIGHT,
        name="pack",
    )(expand_weight, project_weight, kernel.T, bias, gain, x, g)


def encode_kernel(dims, meta, *refs):
    n, length, owned = dims
    frames = refs[:n]
    pieces, below, blocks = refs[n : 2 * n - 1], refs[2 * n - 1], refs[2 * n : 2 * n + 2]
    packs, (out_ref, cat, weight, residual, sems) = refs[2 * n + 2 : -5], refs[-5:]
    shard = lax.axis_index("shard")
    channels = cat.shape[1] // n
    part = owned // n
    me = lax.axis_index("dp")

    def rows(at, size):
        return pl.ds(pl.multiple_of(at * size, size), size)

    moves = []
    for which, block in enumerate(blocks):
        for chip in range(block.shape[0]):
            owner = 2 * chip + ((shard % 2) ^ which)
            for k in range(1, n):
                start = pl.multiple_of((me ^ k) * channels + owner * part, part)
                source = block.at[chip, pl.ds((k - 1) * part, part)]
                moves.append((source, weight.at[pl.ds(start, part)]))
    wide = packs[0].shape[1]
    for b, block in enumerate(packs):
        owner = shard ^ (2 * (b % (len(packs) // 2)) + b // (len(packs) // 2))
        start = pl.multiple_of(me * channels + owner * part, part)
        for h in range(weight.shape[1] // wide):
            source = block.at[pl.ds(owned + h * part, part)]
            moves.append((source, weight.at[pl.ds(start, part), pl.ds(h * wide, wide)]))
    for k in range(n):
        moves.append(
            (
                frames[k].at[rows(meta[me ^ k, n + me], length)],
                residual.at[rows(me ^ k, length)],
            )
        )
    for m in range(n):
        lanes = pl.ds(pl.multiple_of((me ^ m) * channels, channels), channels)
        for k in range(n):
            cols = pl.ds(k * channels, channels)
            if m < n - 1:
                source = pieces[m].at[:, cols]
            else:
                source = below.at[pl.ds(n * length, length), cols]
            moves.append((source, cat.at[rows(me ^ m ^ k, length), lanes]))
    copies = [
        pltpu.make_async_copy(source, target, sems.at[i])
        for i, (source, target) in enumerate(moves)
    ]
    for copy in copies:
        copy.start()
    for copy in copies:
        copy.wait()
    span = 512
    for start in range(0, cat.shape[1], span):
        cols = slice(start, start + span)
        term = jnp.dot(cat[...], weight[:, cols], preferred_element_type=F32)
        out_ref[:, cols] = (residual[:, cols].astype(F32) + term).astype(BF16)


def encode_call(ints, pieces, below, frames, blocks, packs, length):
    n = len(frames)
    width = blocks[0].shape[2]
    owned = width // len(packs)
    halves = width // packs[0].shape[1]
    anywhere = pl.BlockSpec(memory_space=pl.ANY)
    return pl.pallas_call(
        functools.partial(encode_kernel, (n, length, owned)),
        out_shape=jax.ShapeDtypeStruct((n * length, width), BF16),
        in_specs=[in_smem()] + [anywhere] * (2 * n + len(blocks) + len(packs)),
        out_specs=in_vmem(),
        scratch_shapes=[
            pltpu.VMEM((n * length, width), BF16),
            pltpu.VMEM((width, width), BF16),
            pltpu.VMEM((n * length, width), BF16),
            pltpu.SemaphoreType.DMA((len(packs) * (n - 1 + halves) + n + n * n,)),
        ],
        compiler_params=vmem_params(VMEM_ENCODE),
        cost_estimate=LIGHT,
        name="encode",
    )(ints, *frames, *pieces, below, *blocks, *packs)


def frame_grad_kernel(n, x_ref, g_ref, gain_ref, *refs):
    out_ref = refs[n]
    x = x_ref[...].astype(F32)
    centred = x - jnp.mean(x, axis=1, keepdims=True)
    inverse = lax.rsqrt(jnp.mean(centred * centred, axis=1, keepdims=True) + EPS)
    standard = centred * inverse
    grad = sum(ref[...].astype(F32) for ref in refs[:n]) * gain_ref[...]
    grad_in = inverse * (
        grad
        - jnp.mean(grad, axis=1, keepdims=True)
        - standard * jnp.mean(grad * standard, axis=1, keepdims=True)
    )
    out_ref[...] = (g_ref[...].astype(F32) + grad_in).astype(BF16)


def frame_grad_call(x, g, gain, returned):
    count, length, width = x.shape
    rows = count * length
    step = 64
    block = pl.BlockSpec((step, width), lambda s: (s, 0))
    out = pl.pallas_call(
        functools.partial(frame_grad_kernel, len(returned)),
        out_shape=jax.ShapeDtypeStruct((rows, width), BF16),
        grid=(rows // step,),
        in_specs=[block, block, pl.BlockSpec((1, width), lambda s: (0, 0))]
        + [block] * len(returned),
        out_specs=block,
        compiler_params=vmem_params(VMEM_FRAME),
        cost_estimate=LIGHT,
        name="frame_grad",
    )(x.reshape(rows, width), g.reshape(rows, width), gain, *returned)
    return out.reshape(count, length, width)


def unpack_kernel(dims, *refs):
    n, owned, part, half = dims
    blocks, (weight_ref, before, gain_ref) = refs[:n], refs[n : n + 3]
    expand_ref, project_ref, gain_out, cat, grads, project, sems = refs[-7:]
    channels = blocks[0].shape[1]
    width = cat.shape[1]
    wide = 2 * channels
    halves = width // wide
    me = lax.axis_index("dp")
    for k in range(n):
        cat[:, pl.ds(pl.multiple_of((me ^ k) * channels, channels), channels)] = blocks[k][:owned]
        rows = pl.ds(pl.multiple_of((me ^ k) * part, part), part)
        for h in range(halves):
            project[h, rows, :] = blocks[k][owned + h * part : owned + (h + 1) * part].astype(F32)
    copies = [
        pltpu.make_async_copy(
            project.at[h],
            project_ref.at[:, pl.ds(h * wide + half * channels, channels)],
            sems.at[0, h],
        )
        for h in range(halves)
    ]
    for copy in copies:
        copy.start()
    along = before[...]
    span = 512
    for i, start in enumerate(range(0, width, span)):
        row = lax.broadcasted_iota(jnp.int32, (width, span), 0)
        col = lax.broadcasted_iota(jnp.int32, (1, span), 1) + start
        place = col % owned // part * channels + col // owned * part + col % part
        spread = jnp.where(row == place, 1.0, 0.0).astype(BF16)
        grad = jnp.dot(cat[...], spread, preferred_element_type=F32)
        grads[i] = grad
        copy = pltpu.make_async_copy(
            grads.at[i],
            expand_ref.at[:, pl.ds(half * width + start, span)],
            sems.at[1, i],
        )
        copy.start()
        copies.append(copy)
        along += jnp.sum(
            grad * weight_ref[:, start : start + span].astype(F32), axis=1, keepdims=True
        )
    if half == 0:
        gain_out[...] = along
    else:
        row = jnp.transpose(jnp.broadcast_to(along, (owned, LANES)))[:1]
        gain_out[...] = row / gain_ref[...].astype(F32)
    for copy in copies:
        copy.wait()


def unpack_call(half, blocks, weight, before, gain, outputs, owned, part, width):
    n = len(blocks)
    channels = blocks[0].shape[1]
    halves = width // (2 * channels)
    anywhere = pl.BlockSpec(memory_space=pl.ANY)
    return pl.pallas_call(
        functools.partial(unpack_kernel, (n, owned, part, half)),
        out_shape=(
            jax.ShapeDtypeStruct((owned, 2 * width), F32),
            jax.ShapeDtypeStruct((owned, width), F32),
            jax.ShapeDtypeStruct((1, owned) if half else (owned, 1), F32),
        ),
        grid=(1,),
        in_specs=[in_vmem()] * n
        + [pl.BlockSpec((owned, width), lambda s: (0, half)), in_vmem(), in_vmem()]
        + [anywhere] * len(outputs),
        out_specs=(anywhere, anywhere, in_vmem()),
        scratch_shapes=[
            pltpu.VMEM((owned, width), BF16),
            pltpu.VMEM((width // 512, owned, 512), F32),
            pltpu.VMEM((halves, owned, channels), F32),
            pltpu.SemaphoreType.DMA((2, max(halves, width // 512))),
        ],
        input_output_aliases={n + 3 + i: i for i in range(len(outputs))},
        compiler_params=vmem_params(VMEM_UNPACK),
        cost_estimate=LIGHT,
        name="unpack",
    )(*blocks, weight, before, gain, *outputs)


def tie(value, *after):
    return lax.optimization_barrier((value,) + after)[0]


def gather_owners(x):
    blocks = [x] + [swap(x, "shard", 8, 2 * m) for m in (1, 2, 3)]
    return blocks + [swap(block, "shard", 8, 1) for block in blocks]


def add_cores_kernel(keep_hbm, got_hbm, *refs):
    n = len(refs) - 3
    outs, (keep, got, sems) = refs[:n], refs[n:]
    chip = lax.axis_index("shard") // 2
    move = pltpu.make_async_copy
    order = list(range(1, n)) + [0]
    inward = [
        (
            move(keep_hbm.at[chip ^ m], keep.at[m], sems.at[m, 0]),
            move(got_hbm.at[chip ^ m], got.at[m], sems.at[m, 1]),
        )
        for m in range(n)
    ]
    outward = [move(keep.at[m], outs[m], sems.at[m, 2]) for m in range(n)]
    for m in order:
        for copy in inward[m]:
            copy.start()
    for m in order:
        for copy in inward[m]:
            copy.wait()
        keep[m] = (keep[m].astype(F32) + got[m].astype(F32)).astype(BF16)
        outward[m].start()
    for copy in outward:
        copy.wait()


def add_cores(keep, got):
    n = keep.shape[0]
    anywhere = pl.BlockSpec(memory_space=pl.ANY)
    return pl.pallas_call(
        add_cores_kernel,
        out_shape=(jax.ShapeDtypeStruct(keep.shape[1:], BF16),) * n,
        in_specs=[anywhere] * 2,
        out_specs=(anywhere,) * n,
        scratch_shapes=[
            pltpu.VMEM(keep.shape, BF16),
            pltpu.VMEM(keep.shape, BF16),
            pltpu.SemaphoreType.DMA((n, 3)),
        ],
        compiler_params=vmem_params(VMEM_HOP),
        cost_estimate=LIGHT,
        name="add_cores",
    )(keep, got)


def add_chips_kernel(n, *refs):
    total = sum(ref[...].astype(F32) for ref in refs[:n]).astype(BF16)
    channels = refs[n].shape[1]
    for half, ref in enumerate(refs[n:]):
        ref[...] = total[:, half * channels : (half + 1) * channels]


def add_chips(come):
    rows, wide = come[0].shape
    return pl.pallas_call(
        functools.partial(add_chips_kernel, len(come)),
        out_shape=(jax.ShapeDtypeStruct((rows, wide // 2), BF16),) * 2,
        in_specs=[in_vmem()] * len(come),
        out_specs=(in_vmem(),) * 2,
        compiler_params=vmem_params(VMEM_HOP),
        cost_estimate=LIGHT,
        name="add_chips",
    )(*come)


def fast_body(
    frames,
    cotangent,
    lengths,
    send_order,
    norm_gain,
    conv_bias,
    kernel,
    expand_weight,
    project_weight,
):
    n_dp, n_shard = lax.axis_size("dp"), lax.axis_size("shard")
    count, length, width = frames.shape
    owned, taps = kernel.shape
    part = owned // n_dp
    wide = 2 * n_shard * part
    rows = count * length
    dims = (count, length, taps)
    x_own = frames.reshape(rows, width)
    g_own = cotangent.reshape(rows, width)
    pack, both, project = pack_call(
        expand_weight, project_weight, kernel, conv_bias, norm_gain, x_own, g_own, part, wide
    )
    ints = jnp.concatenate([lengths, send_order])
    ints = lax.all_to_all(jnp.broadcast_to(ints, (n_dp, 2 * count)), "dp", 0, 0, tiled=True)
    pack, both, ints = lax.optimization_barrier((pack, both, ints))
    both_x = swap(both, "dp", 4, 1)
    both_y = swap(both, "dp", 4, 2)
    packs = [pack] + [swap(pack, "shard", 8, 2 * m) for m in (1, 2, 3)]
    *packs, both_x, both_y = lax.optimization_barrier((*packs, both_x, both_y))
    packs += [swap(block, "shard", 8, 1) for block in packs]
    x_all = [x_own, both_x, both_y, swap(both_x[:rows], "dp", 4, 2)]
    g_all = [g_own, both_x, both_y, swap(both_y[rows:], "dp", 4, 1)]
    line = [[2 * c + i for c in range(n_shard // 2)] for i in range(2)]
    project = tie(project, *packs[1:4])
    project = lax.all_to_all(project, "shard", 0, 0, axis_index_groups=line, tiled=True)

    near = near_call(ints, x_all[:3], g_all[:3], packs, owned, dims)
    returned = [near[3]] + [swap(near[3 + k], "dp", n_dp, k) for k in (1, 2)]
    gain = near[7]
    far = far_call(ints, x_all[3], near[:3] + near[6:7], g_all, packs, owned, dims)

    keep, give = lax.optimization_barrier((*far[1:3], project, *returned[1:3]))[:2]
    sums = add_cores(keep, swap(give, "shard", 8, 1))
    come = [sums[0]] + [swap(sums[m], "shard", 8, 2 * m) for m in (1, 2, 3)]
    below, *single = lax.optimization_barrier((far[0], *far[4:], sums[1]))[:-1]
    single = [swap(piece, "dp", n_dp, 1 + i) for i, piece in enumerate(single)]
    returned.append(swap(below, "dp", n_dp, 3))
    project = [project, swap(tie(project, sums[1]), "shard", 8, 1)]
    pieces = [tie(far[3], come[1])] + single
    encoded = encode_call(ints, pieces, returned[3], x_all, project, packs, length)
    frame_grad = frame_grad_call(frames, tie(cotangent, come[1]), gain, returned)
    come[0] = tie(come[0], encoded, frame_grad)

    come[0] = tie(come[0], encoded, frame_grad)
    gathered = [[half] + [swap(half, "dp", 4, k) for k in (1, 2, 3)] for half in add_chips(come)]
    base = owned + width // wide * part
    table = jnp.stack([a[base:] for a in gathered[0]])
    table = jnp.take(table, lax.axis_index("dp") ^ jnp.arange(n_dp), axis=0).astype(F32)
    table = jnp.concatenate([table[:, :, :part], table[:, :, LANES : LANES + part]], axis=1)
    table = table.transpose(0, 2, 1).reshape(owned, taps + 1)
    outputs, along = (), jnp.zeros((owned, 1), F32)
    for half in range(2):
        *outputs, along = unpack_call(
            half, gathered[half], expand_weight, along, norm_gain[None], outputs, owned, part, width
        )
    expand_grad, project_grad = outputs
    return (
        encoded.reshape(frames.shape),
        frame_grad,
        along.reshape(owned),
        table[:, taps],
        table[:, :taps],
        expand_grad,
        project_grad,
    )


def depthwise(signal, taps_table):
    taps = taps_table.shape[0]
    half = (taps - 1) // 2
    length = signal.shape[1]
    padded = jnp.pad(signal, ((0, 0), (half, half), (0, 0)))
    result = jnp.zeros_like(signal)
    for offset in range(taps):
        result = result + padded[:, offset : offset + length, :] * taps_table[offset]
    return result


def kernel_terms(signal, upstream, taps):
    half = (taps - 1) // 2
    length = signal.shape[1]
    padded = jnp.pad(signal, ((0, 0), (half, half), (0, 0)))
    rows = []
    for offset in range(taps):
        rows.append(jnp.sum(padded[:, offset : offset + length, :] * upstream, axis=(0, 1)))
    return jnp.stack(rows, axis=0)


def chunk_compute(x, g, live, gain, taps, bias, expand_slice, project_slice):
    count, length, width = x.shape
    rows = count * length
    channels = taps.shape[1]
    inputs = x.reshape(rows, width).astype(F32)
    live_rows = live.reshape(rows, 1)
    centred = inputs - jnp.mean(inputs, axis=1, keepdims=True)
    variance = jnp.mean(centred * centred, axis=1, keepdims=True)
    standard = centred * lax.rsqrt(variance + EPS)
    normed = (standard * gain).astype(BF16)
    expanded = jnp.dot(normed, expand_slice, preferred_element_type=F32)
    value = expanded[:, :channels]
    gate = jax.nn.sigmoid(expanded[:, channels:])
    glu = (value * gate * live_rows).astype(BF16).astype(F32).reshape(count, length, channels)
    conv = depthwise(glu, taps).reshape(rows, channels) + bias
    conv_sig = jax.nn.sigmoid(conv)
    swished = (conv * conv_sig).astype(BF16)
    masked = (g.reshape(rows, width).astype(F32) * live_rows).astype(BF16)
    grad_swish = lax.dot_general(
        masked, project_slice, (((1,), (1,)), ((), ())), preferred_element_type=F32
    )
    grad_conv = grad_swish * conv_sig * (1.0 + conv * (1.0 - conv_sig))
    bias_part = jnp.sum(grad_conv, axis=0)
    volume = grad_conv.reshape(count, length, channels)
    kernel_part = kernel_terms(glu, volume, taps.shape[0])
    grad_glu = depthwise(volume, taps[::-1]).reshape(rows, channels) * live_rows
    grad_expanded = jnp.concatenate(
        [grad_glu * gate, grad_glu * value * gate * (1.0 - gate)], axis=1
    ).astype(BF16)
    grad_normed = lax.dot_general(
        grad_expanded, expand_slice, (((1,), (1,)), ((), ())), preferred_element_type=F32
    )
    gain_part = jnp.sum(grad_normed * standard, axis=0)
    return normed, masked, swished, grad_expanded, grad_normed.astype(BF16), (
        gain_part,
        bias_part,
        kernel_part,
    )


def swap(x, axis, size, k):
    return lax.ppermute(x, axis, [(p, p ^ k) for p in range(size)])


def gather_dp(x, n_dp):
    if n_dp == 4:
        half = x.shape[0] // 2
        along_x = swap(x, "dp", 4, 1)
        along_y = swap(x, "dp", 4, 2)
        far = jnp.concatenate(
            [swap(along_x[:half], "dp", 4, 2), swap(along_y[half:], "dp", 4, 1)], axis=0
        )
        return [x, along_x, along_y, far]
    return [x] + [swap(x, "dp", n_dp, k) for k in range(1, n_dp)]


def gather_shard(x, n_shard):
    if n_shard == 8:
        me = lax.axis_index("shard")
        chip, core = me // 2, me % 2
        blocks = [x] + [
            lax.ppermute(x, "shard", [(p, (p + 2 * k) % 8) for p in range(8)]) for k in (1, 2, 3)
        ]
        mine = jnp.stack(blocks)
        mine = jnp.take(mine, (chip - jnp.arange(4)) % 4, axis=0)
        other = swap(mine, "shard", 8, 1)
        pair = jnp.where(core == 0, jnp.stack([mine, other], 1), jnp.stack([other, mine], 1))
        return pair.reshape((8,) + x.shape)
    return lax.all_gather(x, "shard", axis=0)


def reduce_shard(x, n_shard):
    x = x.astype(BF16)
    if n_shard == 8:
        me = lax.axis_index("shard")
        chip, core = me // 2, me % 2
        cube = x.reshape((4, 2) + x.shape[1:])
        keep = jnp.take(cube, core, axis=1)
        give = jnp.take(cube, 1 - core, axis=1)
        both = (keep.astype(F32) + swap(give, "shard", 8, 1).astype(F32)).astype(BF16)
        total = jnp.take(both, chip, axis=0).astype(F32)
        for k in (1, 2, 3):
            piece = jnp.take(both, (chip + k) % 4, axis=0)
            total = total + lax.ppermute(
                piece, "shard", [(p, (p + 2 * k) % 8) for p in range(8)]
            ).astype(F32)
        return total
    return lax.psum_scatter(x, "shard", scatter_dimension=0, tiled=False).astype(F32)


def generic_body(
    frames,
    cotangent,
    lengths,
    send_order,
    norm_gain,
    conv_bias,
    kernel,
    expand_weight,
    project_weight,
):
    n_dp, n_shard = lax.axis_size("dp"), lax.axis_size("shard")
    count, length, width = frames.shape
    per_peer = count // n_dp
    owned, taps = kernel.shape
    part = owned // n_dp
    channels = n_shard * part
    me = lax.axis_index("dp")

    x_own = jnp.take(frames, send_order, axis=0)
    g_own = jnp.take(cotangent, send_order, axis=0)
    len_own = jnp.take(lengths, send_order, axis=0)

    expand_cols = lax.dynamic_index_in_dim(
        expand_weight.reshape(owned, 2, n_shard, n_dp, part), me, axis=3, keepdims=False
    ).reshape(owned, 2 * channels)
    project_rows = lax.dynamic_slice_in_dim(project_weight, me * part, part, axis=0)
    small = jnp.concatenate(
        [
            lax.dynamic_slice_in_dim(kernel, me * part, part, axis=0).reshape(-1),
            lax.dynamic_slice_in_dim(conv_bias, me * part, part, axis=0),
            norm_gain,
        ]
    )
    wide = 2 * channels
    small_rows = 16
    small = jnp.pad(small, (0, small_rows * wide - small.shape[0])).reshape(small_rows, wide)
    n_halves = width // wide
    pack = jnp.concatenate(
        [expand_cols] + [project_rows[:, h * wide : (h + 1) * wide] for h in range(n_halves)] + [small], axis=0
    )
    packs = gather_shard(pack, n_shard)
    expand_slice = packs[:, :owned].reshape(width, wide)
    project_slice = jnp.concatenate(
        [
            packs[:, owned + h * part : owned + (h + 1) * part].reshape(channels, wide)
            for h in range(n_halves)
        ],
        axis=1,
    )
    small_all = packs[:, owned + n_halves * part :].reshape(n_shard, -1).astype(F32)
    taps_table = small_all[:, : part * taps].reshape(channels, taps).T
    bias = small_all[:, part * taps : part * (taps + 1)].reshape(channels)
    gain = small_all[:, part * (taps + 1) : part * (taps + 1) + owned].reshape(width)
    project_full = gather_shard(project_weight, n_shard).reshape(n_shard, n_dp, part, width)

    x_all = gather_dp(x_own, n_dp)
    g_all = gather_dp(g_own, n_dp)
    len_all = [len_own] + [swap(len_own, "dp", n_dp, k) for k in range(1, n_dp)]

    normeds, maskeds, swisheds, grad_expandeds, returned = [], [], [], [], []
    sums = None
    positions = lax.broadcasted_iota(jnp.int32, (count, length), 1)
    for k in range(n_dp):
        live = (positions < len_all[k][:, None]).astype(F32)
        normed, masked, swished, grad_expanded, grad_normed, parts = chunk_compute(
            x_all[k], g_all[k], live, gain, taps_table, bias, expand_slice, project_slice
        )
        normeds.append(normed)
        maskeds.append(masked)
        swisheds.append(swished.reshape(n_dp, per_peer, length, channels))
        grad_expandeds.append(grad_expanded)
        returned.append(grad_normed if k == 0 else swap(grad_normed, "dp", n_dp, k))
        sums = parts if sums is None else tuple(a + b for a, b in zip(sums, parts))

    stack = jnp.stack(swisheds)
    total = None
    for m in range(n_dp):
        piece = lax.dynamic_index_in_dim(stack, me ^ m, axis=1, keepdims=False)
        if m:
            piece = swap(piece, "dp", n_dp, m)
        piece = jnp.stack([piece[k ^ m] for k in range(n_dp)])
        rows = lax.dynamic_index_in_dim(project_full, me ^ m, axis=1, keepdims=False)
        term = jnp.dot(
            piece.reshape(count * length, channels),
            rows.reshape(channels, width),
            preferred_element_type=F32,
        )
        total = term if total is None else total + term
    mine = jnp.stack(
        [
            lax.dynamic_slice_in_dim(x_all[k], me * per_peer, per_peer, axis=0)
            for k in range(n_dp)
        ]
    )
    len_mine = jnp.stack(
        [
            lax.dynamic_slice_in_dim(len_all[k], me * per_peer, per_peer, axis=0)
            for k in range(n_dp)
        ]
    )
    live_mine = (positions < len_mine.reshape(count, 1)).astype(F32)
    encoded = (
        mine.reshape(count, length, width).astype(F32)
        + total.reshape(count, length, width) * live_mine[:, :, None]
    ).astype(BF16)
    encoded = jnp.take(
        encoded.reshape(n_dp, per_peer, length, width), me ^ jnp.arange(n_dp), axis=0
    ).reshape(count, length, width)

    grad_normed = sum(piece.astype(F32) for piece in returned)
    inputs = x_own.reshape(count * length, width).astype(F32)
    centred = inputs - jnp.mean(inputs, axis=1, keepdims=True)
    variance = jnp.mean(centred * centred, axis=1, keepdims=True)
    inverse = lax.rsqrt(variance + EPS)
    standard = centred * inverse
    grad_standard = grad_normed * gain
    grad_inputs = inverse * (
        grad_standard
        - jnp.mean(grad_standard, axis=1, keepdims=True)
        - standard * jnp.mean(grad_standard * standard, axis=1, keepdims=True)
    )
    frame_sorted = (g_own.reshape(count * length, width).astype(F32) + grad_inputs).astype(BF16)
    back = jnp.argmax(
        send_order[None, :] == jnp.arange(count, dtype=jnp.int32)[:, None], axis=1
    )
    frame_grad = jnp.take(frame_sorted.reshape(count, length, width), back, axis=0)

    expand_part = sum(
        lax.dot_general(a, b, (((0,), (0,)), ((), ())), preferred_element_type=F32)
        for a, b in zip(normeds, grad_expandeds)
    )
    project_part = sum(
        lax.dot_general(
            a.reshape(-1, channels), b, (((0,), (0,)), ((), ())), preferred_element_type=F32
        )
        for a, b in zip(swisheds, maskeds)
    )
    gain_part, bias_part, kernel_part = sums
    small_part = jnp.concatenate(
        [
            kernel_part.T.reshape(n_shard, part * taps),
            bias_part.reshape(n_shard, part),
            gain_part.reshape(n_shard, owned),
        ],
        axis=1,
    )
    small_part = jnp.pad(small_part, ((0, 0), (0, small_rows * wide - small_part.shape[1])))
    project_part = project_part.reshape(n_shard, part, width)
    grad_pack = jnp.concatenate(
        [expand_part.reshape(n_shard, owned, wide)]
        + [project_part[:, :, h * wide : (h + 1) * wide] for h in range(n_halves)]
        + [small_part.reshape(n_shard, small_rows, wide)],
        axis=1,
    )
    reduced = reduce_shard(grad_pack, n_shard).astype(BF16)
    gathered = jnp.stack(gather_dp(reduced, n_dp))
    gathered = jnp.take(gathered, me ^ jnp.arange(n_dp), axis=0).astype(F32)
    expand_grad = (
        gathered[:, :owned]
        .reshape(n_dp, owned, 2, n_shard, part)
        .transpose(1, 2, 3, 0, 4)
        .reshape(owned, 2 * width)
    )
    project_grad = jnp.concatenate(
        [
            gathered[:, owned + h * part : owned + (h + 1) * part].reshape(owned, wide)
            for h in range(n_halves)
        ],
        axis=1,
    )
    small_grad = gathered[:, owned + n_halves * part :].reshape(n_dp, -1)
    kernel_grad = small_grad[:, : part * taps].reshape(owned, taps)
    bias_grad = small_grad[:, part * taps : part * (taps + 1)].reshape(owned)
    gain_grad = jnp.sum(small_grad[:, part * (taps + 1) : part * (taps + 1) + owned], axis=0)
    return encoded, frame_grad, gain_grad, bias_grad, kernel_grad, expand_grad, project_grad


def body(*arrays):
    fast = lax.axis_size("dp") == 4 and lax.axis_size("shard") == 8
    return (fast_body if fast else generic_body)(*arrays)


def solution(mesh):
    return jax.shard_map(
        body,
        mesh=mesh,
        in_specs=(
            P(("dp", "shard"), None, None),
            P(("dp", "shard"), None, None),
            P(("dp", "shard")),
            P(("dp", "shard")),
            P("shard"),
            P("shard"),
            P("shard", None),
            P("shard", None),
            P("shard", None),
        ),
        out_specs=(
            P(("dp", "shard"), None, None),
            P(("dp", "shard"), None, None),
            P("shard"),
            P("shard"),
            P("shard", None),
            P("shard", None),
            P("shard", None),
        ),
        check_vma=False,
    )
```
